32 devices in a mesh: grp: 2 (over core), blk: 16 (over z, y, x).
Axes of the slice: x: 2, y: 2, z: 4, core: 2. Of those that a mesh axis runs over, the one named last changes fastest.
Arguments:
- short_tokens: bfloat16 [192, 64, 768], P(('grp', 'blk')), may hold values from -6 to 6
- long_tokens: bfloat16 [64, 256, 768], P(('grp', 'blk')), may hold values from -6 to 6
- short_lengths: int32 [192], P(('grp', 'blk')), may hold values from 16 to 64
- long_lengths: int32 [64], P(('grp', 'blk')), may hold values from 64 to 256
- short_cotangent: bfloat16 [192, 64, 768], P(('grp', 'blk')), may hold values from -6 to 6
- long_cotangent: bfloat16 [64, 256, 768], P(('grp', 'blk')), may hold values from -6 to 6
- queries: bfloat16 [128, 768], P(('grp', 'blk')), may hold values from -12 to 12
- positives: int32 [128], P(('grp', 'blk')), may hold values from 0 to 255, as said below
- hard_negatives: int32 [128], P(('grp', 'blk')), may hold values from 0 to 255, as said below
- w_query: bfloat16 [768, 768], replicated, may hold values from -0.21875 to 0.21875
- b_query: bfloat16 [768], replicated, may hold values from -3 to 3
- w_key: bfloat16 [768, 768], replicated, may hold values from -0.21875 to 0.21875
- w_value: bfloat16 [768, 768], replicated, may hold values from -0.21875 to 0.21875
- b_value: bfloat16 [768], replicated, may hold values from -3 to 3
- w_out: bfloat16 [768, 768], replicated, may hold values from -1.25 to 1.25
- b_out: bfloat16 [768], replicated, may hold values from -3 to 3
- gain_one: bfloat16 [768], replicated, may hold values from 0.5 to 1.5
- shift_one: bfloat16 [768], replicated, may hold values from -3 to 3
- w_inner: bfloat16 [768, 3072], replicated, may hold values from -0.21875 to 0.21875
- b_inner: bfloat16 [3072], replicated, may hold values from -3 to 3
- w_outer: bfloat16 [3072, 768], replicated, may hold values from -0.109375 to 0.109375
- b_outer: bfloat16 [768], replicated, may hold values from -3 to 3
- gain_two: bfloat16 [768], replicated, may hold values from 0.5 to 1.5
- shift_two: bfloat16 [768], replicated, may hold values from -3 to 3
Outputs:
- short_output: bfloat16 [192, 64, 768], P(('grp', 'blk'))
- long_output: bfloat16 [64, 256, 768], P(('grp', 'blk'))
- short_grad: float32 [192, 64, 768], P(('grp', 'blk'))
- long_grad: float32 [64, 256, 768], P(('grp', 'blk'))
- query_loss: float32 [128], P(('grp', 'blk'))
- grad_w_query: float32 [768, 768], P('blk')
- grad_b_query: float32 [768], P('blk')
- grad_w_key: float32 [768, 768], P('blk')
- grad_w_value: float32 [768, 768], P('blk')
- grad_b_value: float32 [768], P('blk')
- grad_w_out: float32 [768, 768], P('blk')
- grad_b_out: float32 [768], P('blk')
- grad_gain_one: float32 [768], P('blk')
- grad_shift_one: float32 [768], P('blk')
- grad_w_inner: float32 [768, 3072], P('blk')
- grad_b_inner: float32 [3072], P('blk')
- grad_w_outer: float32 [3072, 768], P('blk')
- grad_b_outer: float32 [768], P('blk')
- grad_gain_two: float32 [768], P('blk')
- grad_shift_two: float32 [768], P('blk')
The draws below stay inside these ranges and needn't reach their ends.
Inputs may be any that keep to these rules, and one draw needn't show every extreme that they name: positives and hard_negatives together name every passage number exactly once. positives and hard_negatives together name every passage number exactly once.
All inputs are finite; a program needn't handle non-finite values.
Results may differ from the reference program's by a relative error of at most 0.015.
Values may be sent and summed in bfloat16 or wider, within the bound.
A program may use at most 256 MiB of HBM per device.

```python
import math
import jax
import jax.numpy as jnp
from jax import lax

D = 768
HEADS = 12
HEAD = 64
FF = 3072
SHORT_LEN = 64
LONG_LEN = 256
SHORT_DEV = 6
LONG_DEV = 2
BLOCKS = 32
SHORT = 192
LONG = 64
PASSAGES = 256
QUERIES = 128


def passage_order(key):
    return jax.random.permutation(key, PASSAGES).astype(jnp.int32)


def draw_positives(key, part):
    order = passage_order(key)
    return order[:QUERIES]


def draw_hard_negatives(key, part):
    order = passage_order(key)
    return order[QUERIES:]


def plant(values, own_key, least, largest):
    index_at = [jax.random.randint(jax.random.fold_in(own_key, axis), (), 0, length) for axis, length in enumerate(values.shape)]
    widest = values.shape.index(max(values.shape))
    next_to = index_at[:widest] + [(index_at[widest] + 1) % values.shape[widest]] + index_at[widest + 1:]
    return values.at[tuple(index_at)].set(least).at[tuple(next_to)].set(largest)


def block_levels(own_key, dims, pieces, smallest, high):
    def one(axis_at, blocks):
        steps = jax.random.uniform(jax.random.fold_in(jax.random.fold_in(own_key, 6), axis_at), (blocks,), jnp.float32, smallest / len(pieces), high / len(pieces))
        return jnp.repeat(jnp.exp(steps), dims[axis_at] // blocks).reshape((-1,) + (1,) * (len(dims) - axis_at - 1))

    loudness = one(*pieces[0])
    for cut in pieces[1:]:
        loudness = loudness * one(*cut)
    return loudness


def noise(rng, dims, scale, reach, split=(), dtype=jnp.bfloat16):
    result = scale * jax.random.normal(rng, dims, jnp.float32)
    if split:
        result = result * block_levels(rng, dims, split, -0.22, 0.18)
    return jnp.clip(result, -reach, reach).astype(dtype)


def setup_inputs(seed: int = 0) -> dict:
    key_of = jax.random.split(jax.random.key(seed), 25)
    short_tokens = noise(key_of[0], (SHORT, SHORT_LEN, D), 1.0, 6.0, ((0, 32),))
    long_tokens = noise(key_of[1], (LONG, LONG_LEN, D), 1.0, 6.0, ((0, 32),))
    short_lengths = plant(jax.random.randint(key_of[2], (SHORT,), SHORT_LEN // 4, SHORT_LEN + 1), jax.random.fold_in(key_of[2], 1), SHORT_LEN // 4, SHORT_LEN).astype(jnp.int32)
    long_lengths = plant(jax.random.randint(key_of[3], (LONG,), LONG_LEN // 4, LONG_LEN + 1), jax.random.fold_in(key_of[3], 1), LONG_LEN // 4, LONG_LEN).astype(jnp.int32)
    short_cotangent = noise(key_of[4], (SHORT, SHORT_LEN, D), 1.0, 6.0, ((0, 32),))
    long_cotangent = noise(key_of[5], (LONG, LONG_LEN, D), 1.0, 6.0, ((0, 32),))
    queries = noise(key_of[6], (QUERIES, D), 2.0, 12.0, ((0, 32),))
    positives = draw_positives(jax.random.fold_in(key_of[24], 71), 0)
    hard_negatives = draw_hard_negatives(jax.random.fold_in(key_of[24], 71), 0)
    w_query = noise(key_of[9], (D, D), D ** -0.5, 0.21875)
    b_query = noise(key_of[10], (D,), 0.5, 3.0)
    w_key = noise(key_of[11], (D, D), D ** -0.5, 0.21875)
    w_value = noise(key_of[12], (D, D), D ** -0.5, 0.21875)
    b_value = noise(key_of[13], (D,), 0.5, 3.0)
    w_out = noise(key_of[14], (D, D), (D // 32) ** -0.5, 1.25)
    b_out = noise(key_of[15], (D,), 0.5, 3.0)
    gain_one = jnp.clip(1.0 + 0.1 * jax.random.normal(key_of[16], (D,), jnp.float32), 0.5, 1.5).astype(jnp.bfloat16)
    shift_one = noise(key_of[17], (D,), 0.5, 3.0)
    w_inner = noise(key_of[18], (D, FF), D ** -0.5, 0.21875)
    b_inner = noise(key_of[19], (FF,), 0.5, 3.0)
    w_outer = noise(key_of[20], (FF, D), FF ** -0.5, 0.109375)
    b_outer = noise(key_of[21], (D,), 0.5, 3.0)
    gain_two = jnp.clip(1.0 + 0.1 * jax.random.normal(key_of[22], (D,), jnp.float32), 0.5, 1.5).astype(jnp.bfloat16)
    shift_two = noise(key_of[23], (D,), 0.5, 3.0)
    return {"short_tokens": short_tokens, "long_tokens": long_tokens, "short_lengths": short_lengths, "long_lengths": long_lengths, "short_cotangent": short_cotangent, "long_cotangent": long_cotangent, "queries": queries, "positives": positives, "hard_negatives": hard_negatives, "w_query": w_query, "b_query": b_query, "w_key": w_key, "w_value": w_value, "b_value": b_value, "w_out": w_out, "b_out": b_out, "gain_one": gain_one, "shift_one": shift_one, "w_inner": w_inner, "b_inner": b_inner, "w_outer": w_outer, "b_outer": b_outer, "gain_two": gain_two, "shift_two": shift_two}


norm_epsilon = 1e-05
contrast_weight = 8.0
masked_value = -1000000000.0
highest = lax.Precision.HIGHEST

@jax.custom_vjp
def low(v):
    return lax.optimization_barrier(v.astype(jnp.bfloat16)).astype(jnp.float32)

@jax.custom_vjp
def low_back(v):
    return v

def low_keep(v):
    return (low(v), None)

def low_pass(kept, grad):
    return (grad,)

def back_keep(v):
    return (v, None)

def back_low(kept, grad):
    return (low(grad),)
low.defvjp(low_keep, low_pass)
low_back.defvjp(back_keep, back_low)

def layer_norm(value, gain, shift):
    center = value - lax.optimization_barrier(jnp.mean(value, axis=-1, keepdims=True))
    spread = lax.optimization_barrier(jnp.mean(center * center, axis=-1, keepdims=True))
    return center * lax.rsqrt(spread + norm_epsilon) * gain + shift

def product(left, right):
    return jnp.dot(left, right, precision=highest, preferred_element_type=jnp.float32)

def encode(tokens, lengths, params):
    w_query, b_query, w_key, w_value, b_value, w_out, b_out, gain_one, shift_one, w_inner, b_inner, w_outer, b_outer, gain_two, shift_two = params
    count, seq, width = tokens.shape
    rows = tokens.reshape(count * seq, width)
    query = low(low_back(product(rows, w_query)) + b_query).reshape(count, seq, HEADS, HEAD)
    keys = low(low_back(product(rows, w_key))).reshape(count, seq, HEADS, HEAD)
    values = low(low_back(product(rows, w_value)) + b_value).reshape(count, seq, HEADS, HEAD)
    scores = low_back(jnp.einsum('nqhd,nkhd->nhqk', query, keys, precision=highest) * HEAD ** (-0.5))
    valid = jnp.arange(seq)[None, :] < lengths[:, None]
    scores = jnp.where(valid[:, None, None, :], scores, masked_value)
    top = lax.optimization_barrier(jnp.max(scores, axis=-1, keepdims=True))
    expo = jnp.exp(scores - top)
    probs = expo / lax.optimization_barrier(jnp.sum(expo, axis=-1, keepdims=True))
    mixed = jnp.einsum('nhqk,nkhd->nqhd', low(probs), values, precision=highest)
    context = low(low_back(mixed)).reshape(count * seq, width)
    attended = low_back(product(context, w_out)) + b_out
    first = layer_norm(rows + attended, gain_one, shift_one)
    inner = low(jax.nn.gelu(low_back(product(low(first), w_inner)) + b_inner, approximate=False))
    second = low_back(product(inner, w_outer)) + b_outer
    return layer_norm(first + second, gain_two, shift_two).reshape(count, seq, width)

def run_bucket(tokens, lengths, params):
    count, seq, width = tokens.shape
    group = math.gcd(count, max(1, 4096 // seq))
    blocks = tokens.reshape(count // group, group, seq, width)
    spans = lengths.reshape(count // group, group)
    checked = jax.checkpoint(encode)
    results = lax.map(lambda item: checked(item[0], item[1], params), (blocks, spans))
    return results.reshape(count, seq, width)

def reference(short_tokens, long_tokens, short_lengths, long_lengths, short_cotangent, long_cotangent, queries, positives, hard_negatives, w_query, b_query, w_key, w_value, b_value, w_out, b_out, gain_one, shift_one, w_inner, b_inner, w_outer, b_outer, gain_two, shift_two):
    params = tuple((item.astype(jnp.float32) for item in (w_query, b_query, w_key, w_value, b_value, w_out, b_out, gain_one, shift_one, w_inner, b_inner, w_outer, b_outer, gain_two, shift_two)))
    short_valid = (jnp.arange(SHORT_LEN)[None, :] < short_lengths[:, None]).astype(jnp.float32)
    long_valid = (jnp.arange(LONG_LEN)[None, :] < long_lengths[:, None]).astype(jnp.float32)
    short_weight = short_cotangent.astype(jnp.float32) * short_valid[:, :, None]
    long_weight = long_cotangent.astype(jnp.float32) * long_valid[:, :, None]
    query_rows = queries.astype(jnp.float32)

    def objective(short_rows, long_rows, weights):
        short_out = run_bucket(short_rows, short_lengths, weights)
        long_out = run_bucket(long_rows, long_lengths, weights)
        linear = jnp.sum(short_out * short_weight) + jnp.sum(long_out * long_weight)
        cls = jnp.concatenate([short_out[:, 0, :].reshape(BLOCKS, SHORT_DEV, D), long_out[:, 0, :].reshape(BLOCKS, LONG_DEV, D)], axis=1).reshape(PASSAGES, D)
        match = product(query_rows, low(cls).T) * D ** (-0.5)
        top = lax.optimization_barrier(jnp.max(match, axis=1, keepdims=True))
        logsum = top[:, 0] + jnp.log(lax.optimization_barrier(jnp.sum(jnp.exp(match - top), axis=1)))
        positive = jnp.take_along_axis(match, positives[:, None], axis=1)[:, 0]
        negative = jnp.take_along_axis(match, hard_negatives[:, None], axis=1)[:, 0]
        losses = logsum - positive + jax.nn.softplus(negative - positive)
        return (linear + contrast_weight * jnp.sum(losses), (short_out, long_out, losses))
    total, pull, extra = jax.vjp(objective, short_tokens.astype(jnp.float32), long_tokens.astype(jnp.float32), params, has_aux=True)
    short_grad, long_grad, grads = pull(jnp.ones((), jnp.float32))
    short_out, long_out, losses = extra
    grad_w_query, grad_b_query, grad_w_key, grad_w_value, grad_b_value, grad_w_out, grad_b_out, grad_gain_one, grad_shift_one, grad_w_inner, grad_b_inner, grad_w_outer, grad_b_outer, grad_gain_two, grad_shift_two = grads
    return (short_out.astype(jnp.bfloat16), long_out.astype(jnp.bfloat16), short_grad, long_grad, losses, grad_w_query, grad_b_query, grad_w_key, grad_w_value, grad_b_value, grad_w_out, grad_b_out, grad_gain_one, grad_shift_one, grad_w_inner, grad_b_inner, grad_w_outer, grad_b_outer, grad_gain_two, grad_shift_two)
```

```python
import functools

import jax
import jax.numpy as jnp
from jax import lax
from jax.experimental import pallas as pl
from jax.experimental.pallas import tpu as pltpu
from jax.sharding import PartitionSpec as P

HEADS = 12
HEAD = 64


norm_epsilon = 1e-05
contrast_weight = 8.0
masked_value = -1000000000.0


def layer_norm(value, gain, shift):
    center = value - jnp.mean(value, axis=-1, keepdims=True)
    spread = jnp.mean(center * center, axis=-1, keepdims=True)
    return center * lax.rsqrt(spread + norm_epsilon) * gain + shift


def exact_gelu(value):
    return jax.nn.gelu(value, approximate=False)


def split_heads(value, count, seq):
    return value.reshape(count, seq, HEADS, HEAD)


def attention_scores(query, keys, valid):
    scores = jnp.einsum(
        "nqhd,nkhd->nhqk", query, keys, preferred_element_type=jnp.float32
    ) * HEAD ** (-0.5)
    return jnp.where(valid[:, None, None, :], scores, masked_value)


def forward_bucket(tokens, lengths, params):
    (
        w_query,
        b_query,
        w_key,
        w_value,
        b_value,
        w_out,
        b_out,
        gain_one,
        shift_one,
        w_inner,
        b_inner,
        w_outer,
        b_outer,
        gain_two,
        shift_two,
    ) = params
    count, seq, width = tokens.shape
    rows = tokens.reshape(count * seq, width)
    query = (jnp.dot(rows, w_query, preferred_element_type=jnp.float32) + b_query).astype(
        jnp.bfloat16
    )
    keys = jnp.dot(rows, w_key, preferred_element_type=jnp.float32).astype(jnp.bfloat16)
    values = (jnp.dot(rows, w_value, preferred_element_type=jnp.float32) + b_value).astype(
        jnp.bfloat16
    )
    valid = lax.broadcasted_iota(jnp.int32, (count, seq), 1) < lengths[:, None]
    scores = attention_scores(split_heads(query, count, seq), split_heads(keys, count, seq), valid)
    top = jnp.max(scores, axis=-1, keepdims=True)
    expo = jnp.exp(scores - top)
    total = jnp.sum(expo, axis=-1, keepdims=True)
    logsum = top + jnp.log(total)
    probs = (expo / total).astype(jnp.bfloat16)
    context = (
        jnp.einsum(
            "nhqk,nkhd->nqhd",
            probs,
            split_heads(values, count, seq),
            preferred_element_type=jnp.float32,
        )
        .astype(jnp.bfloat16)
        .reshape(count * seq, width)
    )
    mixed_one = rows + jnp.dot(context, w_out, preferred_element_type=jnp.float32) + b_out
    first = layer_norm(mixed_one, gain_one, shift_one)
    first_low = first.astype(jnp.bfloat16)
    pre = jnp.dot(first_low, w_inner, preferred_element_type=jnp.float32) + b_inner
    inner = exact_gelu(pre).astype(jnp.bfloat16)
    mixed_two = first + jnp.dot(inner, w_outer, preferred_element_type=jnp.float32) + b_outer
    output = layer_norm(mixed_two, gain_two, shift_two)
    kept = (
        rows,
        query,
        keys,
        values,
        valid,
        logsum,
        context,
        mixed_one,
        first_low,
        pre,
        inner,
        mixed_two,
    )
    return (output.reshape(count, seq, width), kept)


def backward_bucket(d_output, kept, params):
    (
        w_query,
        b_query,
        w_key,
        w_value,
        b_value,
        w_out,
        b_out,
        gain_one,
        shift_one,
        w_inner,
        b_inner,
        w_outer,
        b_outer,
        gain_two,
        shift_two,
    ) = params
    (
        rows,
        query,
        keys,
        values,
        valid,
        logsum,
        context,
        mixed_one,
        first_low,
        pre,
        inner,
        mixed_two,
    ) = kept
    count, seq = valid.shape
    width = rows.shape[1]
    f32 = jnp.float32
    unused, pull_two = jax.vjp(layer_norm, mixed_two, gain_two, shift_two)
    d_mixed_two, grad_gain_two, grad_shift_two = pull_two(d_output)
    d_second = d_mixed_two.astype(jnp.bfloat16)
    grad_w_outer = jnp.einsum("rf,rd->fd", inner, d_second, preferred_element_type=f32)
    grad_b_outer = jnp.sum(d_mixed_two, axis=0)
    d_inner = jnp.einsum("rd,fd->rf", d_second, w_outer, preferred_element_type=f32)
    unused, pull_gelu = jax.vjp(exact_gelu, pre)
    (d_pre,) = pull_gelu(d_inner)
    d_pre_low = d_pre.astype(jnp.bfloat16)
    grad_w_inner = jnp.einsum("rd,rf->df", first_low, d_pre_low, preferred_element_type=f32)
    grad_b_inner = jnp.sum(d_pre, axis=0)
    d_first = d_mixed_two + jnp.einsum("rf,df->rd", d_pre_low, w_inner, preferred_element_type=f32)
    unused, pull_one = jax.vjp(layer_norm, mixed_one, gain_one, shift_one)
    d_mixed_one, grad_gain_one, grad_shift_one = pull_one(d_first)
    d_attended = d_mixed_one.astype(jnp.bfloat16)
    grad_w_out = jnp.einsum("rd,re->de", context, d_attended, preferred_element_type=f32)
    grad_b_out = jnp.sum(d_mixed_one, axis=0)
    d_context = jnp.einsum("re,de->rd", d_attended, w_out, preferred_element_type=f32).astype(
        jnp.bfloat16
    )
    query_heads = split_heads(query, count, seq)
    key_heads = split_heads(keys, count, seq)
    value_heads = split_heads(values, count, seq)
    context_heads = split_heads(d_context, count, seq)
    probs = jnp.exp(attention_scores(query_heads, key_heads, valid) - logsum)
    d_probs = jnp.einsum("nqhd,nkhd->nhqk", context_heads, value_heads, preferred_element_type=f32)
    d_values = jnp.einsum(
        "nhqk,nqhd->nkhd", probs.astype(jnp.bfloat16), context_heads, preferred_element_type=f32
    ).reshape(count * seq, width)
    d_scores = (probs * (d_probs - jnp.sum(probs * d_probs, axis=-1, keepdims=True))).astype(
        jnp.bfloat16
    )
    d_query = jnp.einsum(
        "nhqk,nkhd->nqhd", d_scores, key_heads, preferred_element_type=f32
    ).reshape(count * seq, width) * HEAD ** (-0.5)
    d_keys = jnp.einsum(
        "nhqk,nqhd->nkhd", d_scores, query_heads, preferred_element_type=f32
    ).reshape(count * seq, width) * HEAD ** (-0.5)
    grad_b_query = jnp.sum(d_query, axis=0)
    grad_b_value = jnp.sum(d_values, axis=0)
    query_low = d_query.astype(jnp.bfloat16)
    keys_low = d_keys.astype(jnp.bfloat16)
    values_low = d_values.astype(jnp.bfloat16)
    grad_w_query = jnp.einsum("rd,re->de", rows, query_low, preferred_element_type=f32)
    grad_w_key = jnp.einsum("rd,re->de", rows, keys_low, preferred_element_type=f32)
    grad_w_value = jnp.einsum("rd,re->de", rows, values_low, preferred_element_type=f32)
    d_rows = d_mixed_one + jnp.einsum("re,de->rd", query_low, w_query, preferred_element_type=f32)
    d_rows = d_rows + jnp.einsum("re,de->rd", keys_low, w_key, preferred_element_type=f32)
    d_rows = d_rows + jnp.einsum("re,de->rd", values_low, w_value, preferred_element_type=f32)
    grads = (
        grad_w_query,
        grad_b_query,
        grad_w_key,
        grad_w_value,
        grad_b_value,
        grad_w_out,
        grad_b_out,
        grad_gain_one,
        grad_shift_one,
        grad_w_inner,
        grad_b_inner,
        grad_w_outer,
        grad_b_outer,
        grad_gain_two,
        grad_shift_two,
    )
    return (d_rows.reshape(count, seq, width), grads)


MESH = pl.DeviceIdType.MESH
UNITS = 12


def reduce_kernel(
    wq, wk, wv, wo, wi, wu, vec,
    oq, ok, ov, oo, oi, ou, ovec,
    mine, fromcore, r1, r2, r3, fin, fincore,
    vmine, vcore, v1, v2, v3,
    lsem, cs, cr, s1, q1, s2, q2, s3, q3, s4, q4, vs, vr,
):
    core = lax.axis_index("grp")
    chip = lax.axis_index("blk")
    x = chip % 2
    y = (chip // 2) % 2
    z = chip // 4

    def at(zz, yy, xx):
        return zz * 4 + yy * 2 + xx

    other_core = (1 - core, chip)
    other_x = (core, at(z, y, 1 - x))
    other_y = (core, at(z, 1 - y, x))
    other_z = [(core, at((z + d) % 4, y, x)) for d in (1, 2, 3)]
    peers = [other_core, other_x, other_y] + other_z
    barrier = pltpu.get_barrier_semaphore()
    for peer in peers:
        pl.semaphore_signal(barrier, inc=1, device_id=peer, device_id_type=MESH)
    pl.semaphore_wait(barrier, len(peers))

    def remote(src, dst, send, recv, peer):
        return pltpu.make_async_remote_copy(
            src_ref=src, dst_ref=dst, send_sem=send, recv_sem=recv, device_id=peer, device_id_type=MESH
        )

    def source(u, half):
        cols = pl.ds(pl.multiple_of(half * 384, 128), 384)
        if u < 4:
            ref = wu
            return ref.at[:, :, :, pl.ds(48 * u, 48), cols]
        if u < 8:
            lo = pl.multiple_of((u - 4) * 768 + half * 384, 128)
            return wi.at[:, :, :, :, pl.ds(lo, 384)]
        return (wo, wv, wk, wq)[u - 8].at[:, :, :, :, cols]

    core_copies = []
    local_copies = []
    for u in range(UNITS):
        copy = remote(source(u, 1 - core), fromcore.at[u], cs.at[u], cr.at[u], other_core)
        copy.start()
        core_copies.append(copy)
        local = pltpu.make_async_copy(source(u, core), mine.at[u], lsem.at[u])
        local.start()
        local_copies.append(local)
    vc = remote(vec, vcore, vs.at[0], vr.at[0], other_core)
    vc.start()
    pending = []

    def stage_one(u):
        local_copies[u].wait()
        core_copies[u].wait_recv()
        for zz in range(4):
            mine[u, zz] = (mine[u, zz].astype(jnp.float32) + fromcore[u, zz].astype(jnp.float32)).astype(jnp.bfloat16)
        if u % 2 == 0:
            copy = remote(mine.at[u, :, :, 1 - x], r1.at[u], s1.at[u], q1.at[u], other_x)
        else:
            copy = remote(mine.at[u, :, 1 - y], r1.at[u], s1.at[u], q1.at[u], other_y)
        copy.start()
        return copy

    def stage_two(u, got):
        got.wait_recv()
        if u % 2 == 0:
            for zz in range(4):
                for yy in range(2):
                    mine[u, zz, yy, x] = (
                        mine[u, zz, yy, x].astype(jnp.float32) + r1[u, zz, yy].astype(jnp.float32)
                    ).astype(jnp.bfloat16)
            copy = remote(mine.at[u, :, 1 - y, x], r2.at[u], s2.at[u], q2.at[u], other_y)
        else:
            for zz in range(4):
                mine[u, zz, y] = (mine[u, zz, y].astype(jnp.float32) + r1[u, zz].astype(jnp.float32)).astype(
                    jnp.bfloat16
                )
            copy = remote(mine.at[u, :, y, 1 - x], r2.at[u], s2.at[u], q2.at[u], other_x)
        copy.start()
        return copy

    def stage_three(u, got):
        got.wait_recv()
        for zz in range(4):
            mine[u, zz, y, x] = (
                mine[u, zz, y, x].astype(jnp.float32) + r2[u, zz].astype(jnp.float32)
            ).astype(jnp.bfloat16)
        copies = []
        for d in range(3):
            copy = remote(
                mine.at[u, (z + d + 1) % 4, y, x], r3.at[u, d], s3.at[u, d], q3.at[u, d], other_z[d]
            )
            copy.start()
            copies.append(copy)
        return copies

    def stage_four(u, got):
        total = mine[u, z, y, x].astype(jnp.float32)
        for d in range(3):
            got[d].wait_recv()
            total = total + r3[u, d].astype(jnp.float32)
        fin[u] = total
        copy = remote(fin.at[u], fincore.at[u], s4.at[u], q4.at[u], other_core)
        copy.start()
        return copy

    def place(u, half, value):
        cols = pl.ds(pl.multiple_of(half * 384, 128), 384)
        if u < 4:
            ou[pl.ds(48 * u, 48), cols] = value
        elif u < 8:
            oi[:, pl.ds(pl.multiple_of((u - 4) * 768 + half * 384, 128), 384)] = value
        else:
            (oo, ov, ok, oq)[u - 8][:, cols] = value

    def stage_five(u, got):
        place(u, core, fin[u])
        got.wait_recv()
        place(u, 1 - core, fincore[u])

    c1, c2, c3, c4 = {}, {}, {}, {}
    for t in range(UNITS + 7):
        if t < UNITS:
            c1[t] = stage_one(t)
        if 0 <= t - 2 < UNITS:
            c2[t - 2] = stage_two(t - 2, c1[t - 2])
        if 0 <= t - 4 < UNITS:
            c3[t - 4] = stage_three(t - 4, c2[t - 4])
        if 0 <= t - 5 < UNITS:
            c4[t - 5] = stage_four(t - 5, c3[t - 5])
        if 0 <= t - 6 < UNITS:
            stage_five(t - 6, c4[t - 6])
        if t == 1:
            vc.wait_recv()
            vmine[...] = vec[...] + vcore[...]
            vx = remote(vmine.at[:, :, 1 - x], v1, vs.at[1], vr.at[1], other_x)
            vx.start()
        if t == 4:
            vx.wait_recv()
            for zz in range(4):
                for yy in range(2):
                    vmine[zz, yy, x] = vmine[zz, yy, x] + v1[zz, yy]
            vy = remote(vmine.at[:, 1 - y, x], v2, vs.at[2], vr.at[2], other_y)
            vy.start()
        if t == 7:
            vy.wait_recv()
            for zz in range(4):
                vmine[zz, y, x] = vmine[zz, y, x] + v2[zz]
            vz = []
            for d in range(3):
                copy = remote(vmine.at[(z + d + 1) % 4, y, x], v3.at[d], vs.at[3 + d], vr.at[3 + d], other_z[d])
                copy.start()
                vz.append(copy)
        if t == 10:
            total = vmine[z, y, x]
            for d in range(3):
                vz[d].wait_recv()
                total = total + v3[d]
            ovec[...] = total
    for u in range(UNITS):
        core_copies[u].wait_send()
        c1[u].wait_send()
        c2[u].wait_send()
        for copy in c3[u]:
            copy.wait_send()
        c4[u].wait_send()
    for copy in [vc, vx, vy] + vz:
        copy.wait_send()


def reduce_grads(wq, wk, wv, wo, wi, wu, vec):
    bf = jnp.bfloat16
    f32 = jnp.float32
    dma = pltpu.SemaphoreType.DMA
    shaped = [item.reshape(4, 2, 2, item.shape[0] // 16, item.shape[1]).astype(bf) for item in (wq, wk, wv, wo, wi, wu)]
    outs = [jax.ShapeDtypeStruct((item.shape[3], item.shape[4]), f32) for item in shaped]
    outs.append(jax.ShapeDtypeStruct((16, 128), f32))
    any_ = pl.BlockSpec(memory_space=pl.ANY)
    vmem = pl.BlockSpec(memory_space=pltpu.VMEM)
    n = UNITS
    return pl.pallas_call(
        reduce_kernel,
        out_shape=tuple(outs),
        in_specs=[any_] * 6 + [vmem],
        out_specs=tuple([vmem] * 7),
        scratch_shapes=[
            pltpu.VMEM((n, 4, 2, 2, 48, 384), bf),
            pltpu.VMEM((n, 4, 2, 2, 48, 384), bf),
            pltpu.VMEM((n, 4, 2, 48, 384), bf),
            pltpu.VMEM((n, 4, 48, 384), bf),
            pltpu.VMEM((n, 3, 48, 384), bf),
            pltpu.VMEM((n, 48, 384), f32),
            pltpu.VMEM((n, 48, 384), f32),
            pltpu.VMEM((4, 2, 2, 16, 128), f32),
            pltpu.VMEM((4, 2, 2, 16, 128), f32),
            pltpu.VMEM((4, 2, 16, 128), f32),
            pltpu.VMEM((4, 16, 128), f32),
            pltpu.VMEM((3, 16, 128), f32),
            dma((n,)), dma((n,)), dma((n,)), dma((n,)), dma((n,)), dma((n,)), dma((n,)),
            dma((n, 3)), dma((n, 3)), dma((n,)), dma((n,)), dma((6,)), dma((6,)),
        ],
        compiler_params=pltpu.CompilerParams(
            collective_id=1, has_side_effects=True, vmem_limit_bytes=56 * 1024 * 1024
        ),
        name="reduce_grads",
    )(*shaped, vec)


def contrast_kernel(pay, loss, d_cls, gathered, ss, rs):
    core = lax.axis_index("grp")
    chip = lax.axis_index("blk")
    x = chip % 2
    y = (chip // 2) % 2
    z = chip // 4
    f32 = jnp.float32

    def at(zz, yy, xx):
        return zz * 4 + yy * 2 + xx

    other_core = (1 - core, chip)
    other_x = (core, at(z, y, 1 - x))
    other_y = (core, at(z, 1 - y, x))
    other_z = [(core, at((z + d) % 4, y, x)) for d in (1, 2, 3)]
    peers = [other_core, other_x, other_y] + other_z
    barrier = pltpu.get_barrier_semaphore()
    for peer in peers:
        pl.semaphore_signal(barrier, inc=1, device_id=peer, device_id_type=MESH)
    pl.semaphore_wait(barrier, len(peers))

    def remote(piece, k, peer):
        copy = pltpu.make_async_remote_copy(
            src_ref=piece, dst_ref=piece, send_sem=ss.at[k], recv_sem=rs.at[k], device_id=peer, device_id_type=MESH
        )
        copy.start()
        return copy

    gathered[core, z, y, x] = pay[...]
    first = remote(gathered.at[core, z, y, x], 0, other_core)
    first.wait()
    second = remote(gathered.at[:, z, y, x], 1, other_x)
    second.wait()
    third = remote(gathered.at[:, z, y], 2, other_y)
    third.wait()
    last = [remote(gathered.at[:, z], 3 + d, other_z[d]) for d in range(3)]
    for copy in last:
        copy.wait()
    rows = 512
    width = 768
    scale = width ** (-0.5)
    table = gathered[...].reshape(rows, 896)
    embed = table[:, :width]
    extras = table[:, width:]
    pick = (
        lax.broadcasted_iota(jnp.int32, (16, 128), 0) == lax.broadcasted_iota(jnp.int32, (16, 128), 1)
    ).astype(jnp.bfloat16)
    nt = (((1,), (1,)), ((), ()))
    ids = lax.dot_general(pick, extras, nt, preferred_element_type=f32)
    positive = ids[0:1] * 16.0 + ids[1:2]
    negative = ids[2:3] * 16.0 + ids[3:4]
    match = lax.dot_general(embed, embed, nt, preferred_element_type=f32) * scale
    row = lax.broadcasted_iota(jnp.int32, (rows, 1), 0)
    is_passage = (row % 16) < 8
    number = jnp.where(is_passage, (row // 16) * 8 + row % 16, -1).astype(f32)
    masked = jnp.where(is_passage, match, -1e30)
    top = jnp.max(masked, axis=0, keepdims=True)
    lse = jnp.log(jnp.sum(jnp.exp(masked - top), axis=0, keepdims=True)) + top
    pos_score = jnp.sum(jnp.where(number == positive, match, 0.0), axis=0, keepdims=True)
    neg_score = jnp.sum(jnp.where(number == negative, match, 0.0), axis=0, keepdims=True)
    gap = neg_score - pos_score
    tail = jnp.exp(-jnp.abs(gap))
    softplus = jnp.maximum(gap, 0.0) + jnp.log1p(tail)
    loss[...] = jnp.broadcast_to(lse - pos_score + softplus, loss.shape)
    sig = jnp.where(gap >= 0, 1.0, tail) / (1.0 + tail)
    own = lax.dot_general(pay[:, :width], embed, nt, preferred_element_type=f32) * scale
    own_row = lax.broadcasted_iota(jnp.int32, (16, 1), 0)
    own_number = jnp.where(own_row < 8, (core * 16 + chip) * 8 + own_row, -2).astype(f32)
    lane = lax.broadcasted_iota(jnp.int32, (1, rows), 1) % 16
    used = (own_row < 8) & (lane >= 8) & (lane < 12)
    coef = jnp.exp(jnp.where(used, own - lse, -1e30))
    coef = coef - jnp.where(own_number == positive, 1.0 + sig, 0.0) + jnp.where(own_number == negative, sig, 0.0)
    coef = jnp.where(used, contrast_weight * coef, 0.0)
    total = jnp.zeros((16, width), f32)
    for _ in range(3):
        part = coef.astype(jnp.bfloat16)
        total = total + jnp.dot(part, embed, preferred_element_type=f32)
        coef = coef - part.astype(f32)
    d_cls[...] = total * scale


def contrast(cls_low, queries, positives, hard_negatives):
    bf = jnp.bfloat16
    ids = jnp.stack(
        [positives // 16, positives % 16, hard_negatives // 16, hard_negatives % 16], axis=1
    ).astype(bf)
    payload = jnp.concatenate(
        [
            jnp.pad(cls_low, ((0, 0), (0, 128))),
            jnp.concatenate([queries, jnp.pad(ids, ((0, 0), (0, 124)))], axis=1),
            jnp.zeros((4, 896), bf),
        ],
        axis=0,
    )
    vmem = pl.BlockSpec(memory_space=pltpu.VMEM)
    dma = pltpu.SemaphoreType.DMA
    return pl.pallas_call(
        contrast_kernel,
        out_shape=(
            jax.ShapeDtypeStruct((8, 512), jnp.float32),
            jax.ShapeDtypeStruct((16, 768), jnp.float32),
        ),
        in_specs=[vmem],
        out_specs=(vmem, vmem),
        scratch_shapes=[pltpu.VMEM((2, 4, 2, 2, 16, 896), bf), dma((6,)), dma((6,))],
        compiler_params=pltpu.CompilerParams(collective_id=2, has_side_effects=True),
        name="contrast",
    )(payload)


def contrast_whole(cls_low, queries, positives, hard_negatives, scale):
    f32 = jnp.float32
    passage_count = cls_low.shape[0]
    query_count = queries.shape[0]
    me = lax.axis_index(("grp", "blk"))
    own_ids = me * passage_count + lax.broadcasted_iota(jnp.int32, (passage_count,), 0)
    start_top = jnp.full((query_count,), -1e30, f32)
    piece = lax.all_gather(cls_low, ("grp", "blk"), axis=0, tiled=True)
    top = start_top
    scores = jnp.einsum("qd,pd->qp", queries, piece, preferred_element_type=f32) * scale
    ids = lax.broadcasted_iota(jnp.int32, (1, piece.shape[0]), 1)
    new_top = jnp.maximum(top, jnp.max(scores, axis=1))
    total = jnp.sum(jnp.exp(scores - new_top[:, None]), axis=1)
    pos_score = jnp.sum(jnp.where(ids == positives[:, None], scores, 0.0), axis=1)
    neg_score = jnp.sum(jnp.where(ids == hard_negatives[:, None], scores, 0.0), axis=1)
    top, total, pos_score, neg_score = (new_top, total, pos_score, neg_score)
    logsum = top + jnp.log(total)
    losses = logsum - pos_score + jax.nn.softplus(neg_score - pos_score)
    sigma = jax.nn.sigmoid(neg_score - pos_score)
    coef_pos = contrast_weight * (1.0 + sigma)
    coef_neg = contrast_weight * sigma
    query_piece = lax.all_gather(queries.astype(f32), ("grp", "blk"), axis=0, tiled=True)
    lse_piece = lax.all_gather(logsum, ("grp", "blk"), axis=0, tiled=True)
    pos_coef = lax.all_gather(coef_pos, ("grp", "blk"), axis=0, tiled=True)
    neg_coef = lax.all_gather(coef_neg, ("grp", "blk"), axis=0, tiled=True)
    pos_piece = lax.all_gather(positives, ("grp", "blk"), axis=0, tiled=True)
    neg_piece = lax.all_gather(hard_negatives, ("grp", "blk"), axis=0, tiled=True)
    scores = (
        jnp.einsum(
            "pd,qd->pq", cls_low, query_piece.astype(jnp.bfloat16), preferred_element_type=f32
        )
        * scale
    )
    weight = contrast_weight * jnp.exp(scores - lse_piece[None, :])
    weight = weight - jnp.where(own_ids[:, None] == pos_piece[None, :], pos_coef[None, :], 0.0)
    weight = weight + jnp.where(own_ids[:, None] == neg_piece[None, :], neg_coef[None, :], 0.0)
    d_cls = (
        jnp.dot(weight, query_piece, precision=lax.Precision.HIGHEST, preferred_element_type=f32)
        * scale
    )
    return losses, d_cls


def reduce_whole(totals):
    reduced = (
        lax.psum_scatter(totals[0], "blk", scatter_dimension=0, tiled=True),
        lax.psum_scatter(totals[1], "blk", scatter_dimension=0, tiled=True),
        lax.psum_scatter(totals[2], "blk", scatter_dimension=0, tiled=True),
        lax.psum_scatter(totals[3], "blk", scatter_dimension=0, tiled=True),
        lax.psum_scatter(totals[4], "blk", scatter_dimension=0, tiled=True),
        lax.psum_scatter(totals[5], "blk", scatter_dimension=0, tiled=True),
        lax.psum_scatter(totals[6], "blk", scatter_dimension=0, tiled=True),
        lax.psum_scatter(totals[7], "blk", scatter_dimension=0, tiled=True),
        lax.psum_scatter(totals[8], "blk", scatter_dimension=0, tiled=True),
        lax.psum_scatter(totals[9], "blk", scatter_dimension=0, tiled=True),
        lax.psum_scatter(totals[10], "blk", scatter_dimension=0, tiled=True),
        lax.psum_scatter(totals[11], "blk", scatter_dimension=0, tiled=True),
        lax.psum_scatter(totals[12], "blk", scatter_dimension=0, tiled=True),
        lax.psum_scatter(totals[13], "blk", scatter_dimension=0, tiled=True),
        lax.psum_scatter(totals[14], "blk", scatter_dimension=0, tiled=True),
    )
    reduced = (
        lax.psum(reduced[0].astype(jnp.bfloat16), "grp").astype(jnp.float32),
        lax.psum(reduced[1].astype(jnp.bfloat16), "grp").astype(jnp.float32),
        lax.psum(reduced[2].astype(jnp.bfloat16), "grp").astype(jnp.float32),
        lax.psum(reduced[3].astype(jnp.bfloat16), "grp").astype(jnp.float32),
        lax.psum(reduced[4].astype(jnp.bfloat16), "grp").astype(jnp.float32),
        lax.psum(reduced[5].astype(jnp.bfloat16), "grp").astype(jnp.float32),
        lax.psum(reduced[6].astype(jnp.bfloat16), "grp").astype(jnp.float32),
        lax.psum(reduced[7].astype(jnp.bfloat16), "grp").astype(jnp.float32),
        lax.psum(reduced[8].astype(jnp.bfloat16), "grp").astype(jnp.float32),
        lax.psum(reduced[9].astype(jnp.bfloat16), "grp").astype(jnp.float32),
        lax.psum(reduced[10].astype(jnp.bfloat16), "grp").astype(jnp.float32),
        lax.psum(reduced[11].astype(jnp.bfloat16), "grp").astype(jnp.float32),
        lax.psum(reduced[12].astype(jnp.bfloat16), "grp").astype(jnp.float32),
        lax.psum(reduced[13].astype(jnp.bfloat16), "grp").astype(jnp.float32),
        lax.psum(reduced[14].astype(jnp.bfloat16), "grp").astype(jnp.float32),
    )
    return reduced


VECTORS = (1, 4, 6, 7, 8, 12, 13, 14)


def reduce_all(totals):
    me = lax.axis_index("blk")
    pieces = [totals[i].reshape(16, 1, 48) for i in VECTORS]
    pieces = jnp.pad(jnp.concatenate(pieces, axis=1), ((0, 0), (0, 0), (0, 80)))
    inner_rows = totals[10].reshape(16, 1, 192)
    pieces = pieces.reshape(4, 2, 2, 8, 128)
    wide = jnp.pad(inner_rows.reshape(16, 2, 96), ((0, 0), (0, 6), (0, 32))).reshape(4, 2, 2, 8, 128)
    vec = jnp.concatenate([pieces, wide], axis=3)
    grads = reduce_grads(totals[0], totals[2], totals[3], totals[5], totals[9], totals[11], vec)
    vec = grads[6]
    result = [None] * 15
    for place, i in enumerate((0, 2, 3, 5, 9, 11)):
        result[i] = grads[place]
    for place, i in enumerate(VECTORS):
        result[i] = vec[place, :48]
    result[10] = vec[8:10, :96].reshape(192)
    return tuple(result)


def body(
    fast,
    short_tokens,
    long_tokens,
    short_lengths,
    long_lengths,
    short_cotangent,
    long_cotangent,
    queries,
    positives,
    hard_negatives,
    w_query,
    b_query,
    w_key,
    w_value,
    b_value,
    w_out,
    b_out,
    gain_one,
    shift_one,
    w_inner,
    b_inner,
    w_outer,
    b_outer,
    gain_two,
    shift_two,
):
    f32 = jnp.float32
    params = (
        w_query,
        b_query.astype(f32),
        w_key,
        w_value,
        b_value.astype(f32),
        w_out,
        b_out.astype(f32),
        gain_one.astype(f32),
        shift_one.astype(f32),
        w_inner,
        b_inner.astype(f32),
        w_outer,
        b_outer.astype(f32),
        gain_two.astype(f32),
        shift_two.astype(f32),
    )
    short_out, short_kept = forward_bucket(short_tokens, short_lengths, params)
    long_out, long_kept = forward_bucket(long_tokens, long_lengths, params)
    short_count = short_tokens.shape[0]
    width = short_tokens.shape[2]
    scale = width ** (-0.5)
    cls_low = jnp.concatenate([short_out[:, 0, :], long_out[:, 0, :]], axis=0).astype(jnp.bfloat16)
    passage_count = cls_low.shape[0]
    query_count = queries.shape[0]
    me = lax.axis_index(("grp", "blk"))
    if fast:
        loss_rows, d_own = contrast(cls_low, queries, positives, hard_negatives)
        losses = lax.dynamic_slice(loss_rows[0], (me * 16 + 8,), (query_count,))
        d_cls = d_own[:passage_count]
    else:
        losses, d_cls = contrast_whole(cls_low, queries, positives, hard_negatives, scale)
    short_d = short_cotangent.astype(f32) * short_kept[4][:, :, None]
    short_d = short_d.at[:, 0, :].add(d_cls[:short_count])
    long_d = long_cotangent.astype(f32) * long_kept[4][:, :, None]
    long_d = long_d.at[:, 0, :].add(d_cls[short_count:])
    short_grad, short_terms = backward_bucket(short_d.reshape(-1, width), short_kept, params)
    long_grad, long_terms = backward_bucket(long_d.reshape(-1, width), long_kept, params)
    totals = tuple((first + second for first, second in zip(short_terms, long_terms)))
    reduced = reduce_all(totals) if fast else reduce_whole(totals)
    return (
        short_out.astype(jnp.bfloat16),
        long_out.astype(jnp.bfloat16),
        short_grad,
        long_grad,
        losses,
        reduced[0],
        reduced[1],
        reduced[2],
        reduced[3],
        reduced[4],
        reduced[5],
        reduced[6],
        reduced[7],
        reduced[8],
        reduced[9],
        reduced[10],
        reduced[11],
        reduced[12],
        reduced[13],
        reduced[14],
    )


def solution(mesh):
    fast = mesh.shape["grp"] == 2 and mesh.shape["blk"] == 16
    in_specs = (
        P(("grp", "blk"), None, None),
        P(("grp", "blk"), None, None),
        P(("grp", "blk")),
        P(("grp", "blk")),
        P(("grp", "blk"), None, None),
        P(("grp", "blk"), None, None),
        P(("grp", "blk"), None),
        P(("grp", "blk")),
        P(("grp", "blk")),
        P(),
        P(),
        P(),
        P(),
        P(),
        P(),
        P(),
        P(),
        P(),
        P(),
        P(),
        P(),
        P(),
        P(),
        P(),
    )
    out_specs = (
        P(("grp", "blk"), None, None),
        P(("grp", "blk"), None, None),
        P(("grp", "blk"), None, None),
        P(("grp", "blk"), None, None),
        P(("grp", "blk")),
        P("blk", None),
        P("blk"),
        P("blk", None),
        P("blk", None),
        P("blk"),
        P("blk", None),
        P("blk"),
        P("blk"),
        P("blk"),
        P("blk", None),
        P("blk"),
        P("blk", None),
        P("blk"),
        P("blk"),
        P("blk"),
    )
    return jax.shard_map(functools.partial(body, fast), mesh=mesh, in_specs=in_specs, out_specs=out_specs, check_vma=False)
```

```python
import jax
import jax.numpy as jnp
from jax import lax
from jax.experimental import pallas as pl
from jax.experimental.pallas import tpu as pltpu
from jax.sharding import PartitionSpec as P

HEADS = 12
HEAD = 64


norm_epsilon = 1e-05
contrast_weight = 8.0
masked_value = -1000000000.0
bf = jnp.bfloat16
f32 = jnp.float32
NT = (((1,), (1,)), ((), ()))
TN = (((0,), (0,)), ((), ()))
NN = (((1,), (0,)), ((), ()))
MESH = pl.DeviceIdType.MESH


def layer_norm(value, gain, shift):
    center = value - jnp.mean(value, axis=-1, keepdims=True)
    spread = jnp.mean(center * center, axis=-1, keepdims=True)
    return center * lax.rsqrt(spread + norm_epsilon) * gain + shift


def exact_gelu(value):
    return jax.nn.gelu(value, approximate=False)


def split_heads(value, count, seq):
    return value.reshape(count, seq, HEADS, HEAD)


def attention_scores(query, keys, valid):
    scores = jnp.einsum(
        "nqhd,nkhd->nhqk", query, keys, preferred_element_type=jnp.float32
    ) * HEAD ** (-0.5)
    return jnp.where(valid[:, None, None, :], scores, masked_value)


def forward_bucket(tokens, lengths, params):
    (
        w_query,
        b_query,
        w_key,
        w_value,
        b_value,
        w_out,
        b_out,
        gain_one,
        shift_one,
        w_inner,
        b_inner,
        w_outer,
        b_outer,
        gain_two,
        shift_two,
    ) = params
    count, seq, width = tokens.shape
    rows = tokens.reshape(count * seq, width)
    query = (jnp.dot(rows, w_query, preferred_element_type=jnp.float32) + b_query).astype(
        jnp.bfloat16
    )
    keys = jnp.dot(rows, w_key, preferred_element_type=jnp.float32).astype(jnp.bfloat16)
    values = (jnp.dot(rows, w_value, preferred_element_type=jnp.float32) + b_value).astype(
        jnp.bfloat16
    )
    valid = lax.broadcasted_iota(jnp.int32, (count, seq), 1) < lengths[:, None]
    scores = attention_scores(split_heads(query, count, seq), split_heads(keys, count, seq), valid)
    top = jnp.max(scores, axis=-1, keepdims=True)
    expo = jnp.exp(scores - top)
    total = jnp.sum(expo, axis=-1, keepdims=True)
    logsum = top + jnp.log(total)
    probs = (expo / total).astype(jnp.bfloat16)
    context = (
        jnp.einsum(
            "nhqk,nkhd->nqhd",
            probs,
            split_heads(values, count, seq),
            preferred_element_type=jnp.float32,
        )
        .astype(jnp.bfloat16)
        .reshape(count * seq, width)
    )
    mixed_one = rows + jnp.dot(context, w_out, preferred_element_type=jnp.float32) + b_out
    first = layer_norm(mixed_one, gain_one, shift_one)
    first_low = first.astype(jnp.bfloat16)
    pre = jnp.dot(first_low, w_inner, preferred_element_type=jnp.float32) + b_inner
    inner = exact_gelu(pre).astype(jnp.bfloat16)
    mixed_two = first + jnp.dot(inner, w_outer, preferred_element_type=jnp.float32) + b_outer
    output = layer_norm(mixed_two, gain_two, shift_two)
    kept = (
        rows,
        query,
        keys,
        values,
        valid,
        logsum,
        context,
        mixed_one,
        first_low,
        pre,
        inner,
        mixed_two,
    )
    return (output.reshape(count, seq, width), kept)


def backward_bucket(d_output, kept, params):
    (
        w_query,
        b_query,
        w_key,
        w_value,
        b_value,
        w_out,
        b_out,
        gain_one,
        shift_one,
        w_inner,
        b_inner,
        w_outer,
        b_outer,
        gain_two,
        shift_two,
    ) = params
    (
        rows,
        query,
        keys,
        values,
        valid,
        logsum,
        context,
        mixed_one,
        first_low,
        pre,
        inner,
        mixed_two,
    ) = kept
    count, seq = valid.shape
    width = rows.shape[1]
    f32 = jnp.float32
    unused, pull_two = jax.vjp(layer_norm, mixed_two, gain_two, shift_two)
    d_mixed_two, grad_gain_two, grad_shift_two = pull_two(d_output)
    d_second = d_mixed_two.astype(jnp.bfloat16)
    grad_w_outer = jnp.einsum("rf,rd->fd", inner, d_second, preferred_element_type=f32)
    grad_b_outer = jnp.sum(d_mixed_two, axis=0)
    d_inner = jnp.einsum("rd,fd->rf", d_second, w_outer, preferred_element_type=f32)
    unused, pull_gelu = jax.vjp(exact_gelu, pre)
    (d_pre,) = pull_gelu(d_inner)
    d_pre_low = d_pre.astype(jnp.bfloat16)
    grad_w_inner = jnp.einsum("rd,rf->df", first_low, d_pre_low, preferred_element_type=f32)
    grad_b_inner = jnp.sum(d_pre, axis=0)
    d_first = d_mixed_two + jnp.einsum("rf,df->rd", d_pre_low, w_inner, preferred_element_type=f32)
    unused, pull_one = jax.vjp(layer_norm, mixed_one, gain_one, shift_one)
    d_mixed_one, grad_gain_one, grad_shift_one = pull_one(d_first)
    d_attended = d_mixed_one.astype(jnp.bfloat16)
    grad_w_out = jnp.einsum("rd,re->de", context, d_attended, preferred_element_type=f32)
    grad_b_out = jnp.sum(d_mixed_one, axis=0)
    d_context = jnp.einsum("re,de->rd", d_attended, w_out, preferred_element_type=f32).astype(
        jnp.bfloat16
    )
    query_heads = split_heads(query, count, seq)
    key_heads = split_heads(keys, count, seq)
    value_heads = split_heads(values, count, seq)
    context_heads = split_heads(d_context, count, seq)
    probs = jnp.exp(attention_scores(query_heads, key_heads, valid) - logsum)
    d_probs = jnp.einsum("nqhd,nkhd->nhqk", context_heads, value_heads, preferred_element_type=f32)
    d_values = jnp.einsum(
        "nhqk,nqhd->nkhd", probs.astype(jnp.bfloat16), context_heads, preferred_element_type=f32
    ).reshape(count * seq, width)
    d_scores = (probs * (d_probs - jnp.sum(probs * d_probs, axis=-1, keepdims=True))).astype(
        jnp.bfloat16
    )
    d_query = jnp.einsum(
        "nhqk,nkhd->nqhd", d_scores, key_heads, preferred_element_type=f32
    ).reshape(count * seq, width) * HEAD ** (-0.5)
    d_keys = jnp.einsum(
        "nhqk,nqhd->nkhd", d_scores, query_heads, preferred_element_type=f32
    ).reshape(count * seq, width) * HEAD ** (-0.5)
    grad_b_query = jnp.sum(d_query, axis=0)
    grad_b_value = jnp.sum(d_values, axis=0)
    query_low = d_query.astype(jnp.bfloat16)
    keys_low = d_keys.astype(jnp.bfloat16)
    values_low = d_values.astype(jnp.bfloat16)
    grad_w_query = jnp.einsum("rd,re->de", rows, query_low, preferred_element_type=f32)
    grad_w_key = jnp.einsum("rd,re->de", rows, keys_low, preferred_element_type=f32)
    grad_w_value = jnp.einsum("rd,re->de", rows, values_low, preferred_element_type=f32)
    d_rows = d_mixed_one + jnp.einsum("re,de->rd", query_low, w_query, preferred_element_type=f32)
    d_rows = d_rows + jnp.einsum("re,de->rd", keys_low, w_key, preferred_element_type=f32)
    d_rows = d_rows + jnp.einsum("re,de->rd", values_low, w_value, preferred_element_type=f32)
    grads = (
        grad_w_query,
        grad_b_query,
        grad_w_key,
        grad_w_value,
        grad_b_value,
        grad_w_out,
        grad_b_out,
        grad_gain_one,
        grad_shift_one,
        grad_w_inner,
        grad_b_inner,
        grad_w_outer,
        grad_b_outer,
        grad_gain_two,
        grad_shift_two,
    )
    return (d_rows.reshape(count, seq, width), grads)


def contrast_whole(cls_low, queries, positives, hard_negatives, scale):
    f32 = jnp.float32
    passage_count = cls_low.shape[0]
    query_count = queries.shape[0]
    me = lax.axis_index(("grp", "blk"))
    own_ids = me * passage_count + lax.broadcasted_iota(jnp.int32, (passage_count,), 0)
    start_top = jnp.full((query_count,), -1e30, f32)
    piece = lax.all_gather(cls_low, ("grp", "blk"), axis=0, tiled=True)
    top = start_top
    scores = jnp.einsum("qd,pd->qp", queries, piece, preferred_element_type=f32) * scale
    ids = lax.broadcasted_iota(jnp.int32, (1, piece.shape[0]), 1)
    new_top = jnp.maximum(top, jnp.max(scores, axis=1))
    total = jnp.sum(jnp.exp(scores - new_top[:, None]), axis=1)
    pos_score = jnp.sum(jnp.where(ids == positives[:, None], scores, 0.0), axis=1)
    neg_score = jnp.sum(jnp.where(ids == hard_negatives[:, None], scores, 0.0), axis=1)
    top, total, pos_score, neg_score = (new_top, total, pos_score, neg_score)
    logsum = top + jnp.log(total)
    losses = logsum - pos_score + jax.nn.softplus(neg_score - pos_score)
    sigma = jax.nn.sigmoid(neg_score - pos_score)
    coef_pos = contrast_weight * (1.0 + sigma)
    coef_neg = contrast_weight * sigma
    query_piece = lax.all_gather(queries.astype(f32), ("grp", "blk"), axis=0, tiled=True)
    lse_piece = lax.all_gather(logsum, ("grp", "blk"), axis=0, tiled=True)
    pos_coef = lax.all_gather(coef_pos, ("grp", "blk"), axis=0, tiled=True)
    neg_coef = lax.all_gather(coef_neg, ("grp", "blk"), axis=0, tiled=True)
    pos_piece = lax.all_gather(positives, ("grp", "blk"), axis=0, tiled=True)
    neg_piece = lax.all_gather(hard_negatives, ("grp", "blk"), axis=0, tiled=True)
    scores = (
        jnp.einsum(
            "pd,qd->pq", cls_low, query_piece.astype(jnp.bfloat16), preferred_element_type=f32
        )
        * scale
    )
    weight = contrast_weight * jnp.exp(scores - lse_piece[None, :])
    weight = weight - jnp.where(own_ids[:, None] == pos_piece[None, :], pos_coef[None, :], 0.0)
    weight = weight + jnp.where(own_ids[:, None] == neg_piece[None, :], neg_coef[None, :], 0.0)
    d_cls = (
        jnp.dot(weight, query_piece, precision=lax.Precision.HIGHEST, preferred_element_type=f32)
        * scale
    )
    return losses, d_cls


def reduce_whole(totals):
    reduced = (
        lax.psum_scatter(totals[0], "blk", scatter_dimension=0, tiled=True),
        lax.psum_scatter(totals[1], "blk", scatter_dimension=0, tiled=True),
        lax.psum_scatter(totals[2], "blk", scatter_dimension=0, tiled=True),
        lax.psum_scatter(totals[3], "blk", scatter_dimension=0, tiled=True),
        lax.psum_scatter(totals[4], "blk", scatter_dimension=0, tiled=True),
        lax.psum_scatter(totals[5], "blk", scatter_dimension=0, tiled=True),
        lax.psum_scatter(totals[6], "blk", scatter_dimension=0, tiled=True),
        lax.psum_scatter(totals[7], "blk", scatter_dimension=0, tiled=True),
        lax.psum_scatter(totals[8], "blk", scatter_dimension=0, tiled=True),
        lax.psum_scatter(totals[9], "blk", scatter_dimension=0, tiled=True),
        lax.psum_scatter(totals[10], "blk", scatter_dimension=0, tiled=True),
        lax.psum_scatter(totals[11], "blk", scatter_dimension=0, tiled=True),
        lax.psum_scatter(totals[12], "blk", scatter_dimension=0, tiled=True),
        lax.psum_scatter(totals[13], "blk", scatter_dimension=0, tiled=True),
        lax.psum_scatter(totals[14], "blk", scatter_dimension=0, tiled=True),
    )
    reduced = (
        lax.psum(reduced[0].astype(jnp.bfloat16), "grp").astype(jnp.float32),
        lax.psum(reduced[1].astype(jnp.bfloat16), "grp").astype(jnp.float32),
        lax.psum(reduced[2].astype(jnp.bfloat16), "grp").astype(jnp.float32),
        lax.psum(reduced[3].astype(jnp.bfloat16), "grp").astype(jnp.float32),
        lax.psum(reduced[4].astype(jnp.bfloat16), "grp").astype(jnp.float32),
        lax.psum(reduced[5].astype(jnp.bfloat16), "grp").astype(jnp.float32),
        lax.psum(reduced[6].astype(jnp.bfloat16), "grp").astype(jnp.float32),
        lax.psum(reduced[7].astype(jnp.bfloat16), "grp").astype(jnp.float32),
        lax.psum(reduced[8].astype(jnp.bfloat16), "grp").astype(jnp.float32),
        lax.psum(reduced[9].astype(jnp.bfloat16), "grp").astype(jnp.float32),
        lax.psum(reduced[10].astype(jnp.bfloat16), "grp").astype(jnp.float32),
        lax.psum(reduced[11].astype(jnp.bfloat16), "grp").astype(jnp.float32),
        lax.psum(reduced[12].astype(jnp.bfloat16), "grp").astype(jnp.float32),
        lax.psum(reduced[13].astype(jnp.bfloat16), "grp").astype(jnp.float32),
        lax.psum(reduced[14].astype(jnp.bfloat16), "grp").astype(jnp.float32),
    )
    return reduced


def body(
    short_tokens,
    long_tokens,
    short_lengths,
    long_lengths,
    short_cotangent,
    long_cotangent,
    queries,
    positives,
    hard_negatives,
    w_query,
    b_query,
    w_key,
    w_value,
    b_value,
    w_out,
    b_out,
    gain_one,
    shift_one,
    w_inner,
    b_inner,
    w_outer,
    b_outer,
    gain_two,
    shift_two,
):
    f32 = jnp.float32
    params = (
        w_query,
        b_query.astype(f32),
        w_key,
        w_value,
        b_value.astype(f32),
        w_out,
        b_out.astype(f32),
        gain_one.astype(f32),
        shift_one.astype(f32),
        w_inner,
        b_inner.astype(f32),
        w_outer,
        b_outer.astype(f32),
        gain_two.astype(f32),
        shift_two.astype(f32),
    )
    short_out, short_kept = forward_bucket(short_tokens, short_lengths, params)
    long_out, long_kept = forward_bucket(long_tokens, long_lengths, params)
    short_count = short_tokens.shape[0]
    width = short_tokens.shape[2]
    scale = width ** (-0.5)
    cls_low = jnp.concatenate([short_out[:, 0, :], long_out[:, 0, :]], axis=0).astype(jnp.bfloat16)
    passage_count = cls_low.shape[0]
    query_count = queries.shape[0]
    me = lax.axis_index(("grp", "blk"))
    losses, d_cls = contrast_whole(cls_low, queries, positives, hard_negatives, scale)
    short_d = short_cotangent.astype(f32) * short_kept[4][:, :, None]
    short_d = short_d.at[:, 0, :].add(d_cls[:short_count])
    long_d = long_cotangent.astype(f32) * long_kept[4][:, :, None]
    long_d = long_d.at[:, 0, :].add(d_cls[short_count:])
    short_grad, short_terms = backward_bucket(short_d.reshape(-1, width), short_kept, params)
    long_grad, long_terms = backward_bucket(long_d.reshape(-1, width), long_kept, params)
    totals = tuple((first + second for first, second in zip(short_terms, long_terms)))
    reduced = reduce_whole(totals)
    return (
        short_out.astype(jnp.bfloat16),
        long_out.astype(jnp.bfloat16),
        short_grad,
        long_grad,
        losses,
        reduced[0],
        reduced[1],
        reduced[2],
        reduced[3],
        reduced[4],
        reduced[5],
        reduced[6],
        reduced[7],
        reduced[8],
        reduced[9],
        reduced[10],
        reduced[11],
        reduced[12],
        reduced[13],
        reduced[14],
    )


def dot(a, b, dims=NN):
    return lax.dot_general(a, b, dims, preferred_element_type=f32)


def pair_masks():
    lane = lax.broadcasted_iota(jnp.int32, (1, 128), 1)
    low = (lane < HEAD).astype(bf)
    return low, 1 - low


def gelu_parts(pre):
    z = jnp.abs(pre)
    bell = jnp.exp(pre * pre * -0.5)
    t = 1.0 / (1.0 + 0.23164190 * z)
    poly = t * (0.127414796 + t * (-0.142248368 + t * (0.7107068705 + t * (-0.7265760135 + t * 0.5307027145))))
    small = poly * bell
    phi = jnp.where(pre >= 0, 1.0 - small, small)
    return pre * phi, phi + pre * (bell * 0.3989422804014327)


def norm_parts(value):
    center = value - jnp.mean(value, axis=-1, keepdims=True)
    spread = jnp.mean(center * center, axis=-1, keepdims=True)
    rstd = lax.rsqrt(spread + norm_epsilon)
    return center * rstd, rstd


def forward_kernel(
    lens_s, lens_l, pos, neg, xs_h, xl_h, wq_h, wk_h, wv_h, wo_h, wi_h, wu_h,
    queries, b_query, b_value, b_out, gain_one, shift_one, b_outer, gain_two, shift_two, b_inner,
    outs_h, outl_h, qkvx_h, prob_h, ctx_h, xhat1_h, low1_h, inner_h, slope_h, xhat2_h, rstd_o, cls_o, vecs,
    qkvx, wqkv, wo, wi, wu, prob, ctx, first, xhat1, low1, inner, slope, xhat2, outv, lsem, osem,
):
    def load(src, dst, k):
        copy = pltpu.make_async_copy(src, dst, lsem.at[k])
        copy.start()
        return copy

    loads = [
        load(xs_h, qkvx.at[0:384, 2304:3072], 0),
        load(xl_h, qkvx.at[384:896, 2304:3072], 1),
        load(wq_h, wqkv.at[0], 2),
        load(wk_h, wqkv.at[1], 3),
        load(wv_h, wqkv.at[2], 4),
        load(wo_h, wo, 5),
        load(wi_h, wi, 6),
        load(wu_h, wu, 7),
    ]
    stores = []

    def store(src, dst):
        copy = pltpu.make_async_copy(src, dst, osem.at[len(stores)])
        copy.start()
        stores.append(copy)

    def vec(i):
        return vecs[i:i + 1, :]

    vecs[...] = jnp.zeros_like(vecs)
    for i, item in enumerate((b_query, None, b_value, b_out, gain_one, shift_one, b_outer, gain_two, shift_two)):
        if item is not None:
            vecs[i:i + 1, :] = item[...].astype(f32).reshape(1, 768)
    for i in range(4):
        vecs[9 + i:10 + i, :] = b_inner[768 * i:768 * i + 768].astype(f32).reshape(1, 768)

    loads[0].wait()
    loads[1].wait()
    for m in range(3):
        loads[2 + m].wait()

        @pl.loop(0, 3)
        def _(j):
            cols = pl.ds(pl.multiple_of(j * 256, 256), 256)
            res = dot(qkvx[:, 2304:3072], wqkv[m, :, cols])
            if m != 1:
                res = res + vecs[m:m + 1, cols]
            if m == 0:
                res = res.astype(bf).astype(f32) * HEAD ** (-0.5)
            qkvx[:, pl.ds(pl.multiple_of(m * 768 + j * 256, 256), 256)] = res.astype(bf)

    store(qkvx, qkvx_h)
    low, high = pair_masks()

    def attend(r0, n, p, valid, dest):
        rows = pl.ds(r0, n)
        q = qkvx[rows, pl.ds(pl.multiple_of(p * 128, 128), 128)]
        k = qkvx[rows, pl.ds(pl.multiple_of(768 + p * 128, 128), 128)]
        v = qkvx[rows, pl.ds(pl.multiple_of(1536 + p * 128, 128), 128)]
        acc = None
        for h, mask in enumerate((low, high)):
            s = jnp.where(valid, dot(q, k * mask, NT), masked_value)
            e = jnp.exp(s - jnp.max(s, axis=1, keepdims=True))
            weight = (e * (1.0 / jnp.sum(e, axis=1, keepdims=True))).astype(bf)
            dest(h, weight)
            part = dot(weight, v * mask)
            acc = part if acc is None else acc + part
        ctx[rows, pl.ds(pl.multiple_of(p * 128, 128), 128)] = acc.astype(bf)

    ki = lax.broadcasted_iota(jnp.int32, (1, 256), 1)
    for n in range(2):
        valid = ki < lens_l[n]

        @pl.loop(0, 6)
        def _(p):
            def keep(h, weight):
                prob[256 * n:256 * n + 256, pl.ds(pl.multiple_of(p * 512 + h * 256, 256), 256)] = weight

            attend(384 + 256 * n, 256, p, valid, keep)

    kj = lax.broadcasted_iota(jnp.int32, (128, 128), 1)
    qj = lax.broadcasted_iota(jnp.int32, (128, 128), 0)
    for g in range(3):
        valid = ((qj < 64) & (kj < lens_s[2 * g])) | ((qj >= 64) & (kj >= 64) & (kj - 64 < lens_s[2 * g + 1]))
        valid = valid & ((qj >= 64) | (kj < 64))

        @pl.loop(0, 6)
        def _(p):
            i = g * 6 + p
            start = pl.multiple_of(512 + 128 * (i // 12), 128)

            def keep(h, weight):
                prob[pl.ds(start, 128), pl.ds(pl.multiple_of((i % 12) * 256 + h * 128, 128), 128)] = weight

            attend(128 * g, 128, p, valid, keep)

    store(prob, prob_h)
    store(ctx, ctx_h)
    loads[5].wait()

    @pl.loop(0, 4)
    def _(i):
        rows = pl.ds(pl.multiple_of(i * 224, 32), 224)
        mixed = qkvx[rows, 2304:3072].astype(f32) + dot(ctx[rows, :], wo[...]) + vec(3)
        xhat, rstd = norm_parts(mixed)
        xhat1[rows, :] = xhat.astype(bf)
        rstd_o[rows, 0:128] = jnp.broadcast_to(rstd, (224, 128))
        value = xhat * vec(4) + vec(5)
        first[rows, :] = value
        low1[rows, :] = value.astype(bf)

    store(xhat1, xhat1_h)
    store(low1, low1_h)
    loads[6].wait()

    @pl.loop(0, 12)
    def _(j):
        cols = pl.ds(pl.multiple_of(j * 256, 256), 256)
        bias = vecs[pl.ds(9 + j // 3, 1), pl.ds(pl.multiple_of((j % 3) * 256, 256), 256)]
        pre = dot(low1[...], wi[:, cols]) + bias
        act, grad = gelu_parts(pre)
        inner[:, cols] = act.astype(bf)
        slope[:, cols] = grad.astype(bf)

    store(inner, inner_h)
    store(slope, slope_h)
    loads[7].wait()

    @pl.loop(0, 4)
    def _(i):
        rows = pl.ds(pl.multiple_of(i * 224, 32), 224)
        mixed = first[rows, :] + dot(inner[rows, :], wu[...]) + vec(6)
        xhat, rstd = norm_parts(mixed)
        xhat2[rows, :] = xhat.astype(bf)
        rstd_o[rows, 128:256] = jnp.broadcast_to(rstd, (224, 128))
        outv[rows, :] = (xhat * vec(7) + vec(8)).astype(bf)

    def mark(r0, n, count):
        used = lax.broadcasted_iota(jnp.int32, (n, 128), 0) < count
        rstd_o[r0:r0 + n, 256:384] = jnp.where(used, 1.0, 0.0)

    for i in range(6):
        mark(64 * i, 64, lens_s[i])
    for i in range(2):
        mark(384 + 256 * i, 256, lens_l[i])
    store(xhat2, xhat2_h)
    store(outv.at[0:384], outs_h)
    store(outv.at[384:896], outl_h)
    pieces = [outv[64 * i:64 * i + 1, :] for i in range(6)] + [outv[384 + 256 * i:384 + 256 * i + 1, :] for i in range(2)]
    table = [item.astype(f32) for item in pieces] + [queries[...].astype(f32), jnp.zeros((4, 768), f32)]
    cls_o[:, 0:768] = jnp.concatenate(table, axis=0).astype(bf)
    row = lax.broadcasted_iota(jnp.int32, (16, 128), 0)
    lane = lax.broadcasted_iota(jnp.int32, (16, 128), 1)
    marks = jnp.zeros((16, 128), f32)
    for i in range(4):
        digits = (pos[i] // 16, pos[i] % 16, neg[i] // 16, neg[i] % 16)
        for k in range(4):
            marks = marks + jnp.where((row == 8 + i) & (lane == k), digits[k].astype(f32), 0.0)
    cls_o[:, 768:896] = marks.astype(bf)
    for copy in stores:
        copy.wait()


def forward(short_tokens, long_tokens, short_lengths, long_lengths, positives, hard_negatives, weights, small):
    any_ = pl.BlockSpec(memory_space=pl.ANY)
    vmem = pl.BlockSpec(memory_space=pltpu.VMEM)
    smem = pl.BlockSpec(memory_space=pltpu.SMEM)
    sds = jax.ShapeDtypeStruct
    outs = (
        sds((384, 768), bf), sds((512, 768), bf), sds((896, 3072), bf), sds((768, 3072), bf),
        sds((896, 768), bf), sds((896, 768), bf), sds((896, 768), bf),
        sds((896, 3072), bf), sds((896, 3072), bf), sds((896, 768), bf), sds((896, 384), f32), sds((16, 896), bf),
        sds((16, 768), f32),
    )
    return pl.pallas_call(
        forward_kernel,
        out_shape=outs,
        in_specs=[smem] * 4 + [any_] * 8 + [vmem] * 10,
        out_specs=tuple([any_] * 10 + [vmem] * 3),
        scratch_shapes=[
            pltpu.VMEM((896, 3072), bf),
            pltpu.VMEM((3, 768, 768), bf),
            pltpu.VMEM((768, 768), bf),
            pltpu.VMEM((768, 3072), bf),
            pltpu.VMEM((3072, 768), bf),
            pltpu.VMEM((768, 3072), bf),
            pltpu.VMEM((896, 768), bf),
            pltpu.VMEM((896, 768), f32),
            pltpu.VMEM((896, 768), bf),
            pltpu.VMEM((896, 768), bf),
            pltpu.VMEM((896, 3072), bf),
            pltpu.VMEM((896, 3072), bf),
            pltpu.VMEM((896, 768), bf),
            pltpu.VMEM((896, 768), bf),
            pltpu.SemaphoreType.DMA((8,)),
            pltpu.SemaphoreType.DMA((16,)),
        ],
        compiler_params=pltpu.CompilerParams(vmem_limit_bytes=60 * 1024 * 1024),
        name="forward",
    )(
        short_lengths, long_lengths, positives, hard_negatives, short_tokens.reshape(384, 768),
        long_tokens.reshape(512, 768), *weights, *small,
    )


def place():
    core = lax.axis_index("grp")
    chip = lax.axis_index("blk")
    return core, chip, chip // 4, (chip // 2) % 2, chip % 2


def backward_kernel(
    pay, vecs, rstd, cots_h, cotl_h, qkvx_h, prob_h, ctx_h, xhat1_h, low1_h, inner_h, slope_h, xhat2_h,
    wq_h, wk_h, wv_h, wo_h, wi_h, wu_h,
    drows_h, fin_h, sums_o, loss,
    gathered, bufa, bufb, w1, w2, cot, xhat2, low1, xhat1, ctx, d, d2low, fin, sums, vr,
    both_o, from_o, r1_o, r2_o, r3_o, both_i, from_i, r1_i, r2_i, r3_i,
    lsem, osem, gs, gr, cs, cr, s1, q1, s2, q2, s3, q3, s4, q4, vs, vq,
):
    core, chip, z, y, x = place()

    def at(zz, yy, xx):
        return zz * 4 + yy * 2 + xx

    other_core = (1 - core, chip)
    other_x = (core, at(z, y, 1 - x))
    other_y = (core, at(z, 1 - y, x))
    other_z = [(core, at((z + k) % 4, y, x)) for k in (1, 2, 3)]
    peers = [other_core, other_x, other_y] + other_z
    barrier = pltpu.get_barrier_semaphore()
    for peer in peers:
        pl.semaphore_signal(barrier, inc=1, device_id=peer, device_id_type=MESH)

    loads = {}

    def load(name, *pairs):
        copies = []
        for src, dst in pairs:
            copy = pltpu.make_async_copy(src, dst, lsem.at[sum(len(c) for c in loads.values()) + len(copies)])
            copy.start()
            copies.append(copy)
        loads[name] = copies

    def ready(name):
        for copy in loads[name]:
            copy.wait()

    load("cot", (cots_h, cot.at[0:384]), (cotl_h, cot.at[384:896]))
    load("xhat2", (xhat2_h, xhat2))
    load("inner", (inner_h, bufa))
    load("wu", (wu_h, w1))
    load("slope", (slope_h, bufb))
    load("low1", (low1_h, low1))
    load("wi", (wi_h, w2))
    load("xhat1", (xhat1_h, xhat1))
    load("ctx", (ctx_h, ctx))

    def remote(src, dst, send, recv, peer):
        copy = pltpu.make_async_remote_copy(
            src_ref=src, dst_ref=dst, send_sem=send, recv_sem=recv, device_id=peer, device_id_type=MESH
        )
        copy.start()
        sent.append(copy)
        return copy

    sent = []
    gathered[core, z, y, x] = pay[...]
    sums[...] = jnp.zeros_like(sums)
    pl.semaphore_wait(barrier, len(peers))

    def add_sum(i, value):
        sums[i:i + 1, :] += jnp.sum(value, axis=0, keepdims=True)

    def norm_two(i):
        rows = pl.ds(224 * i, 224)
        e = cot[rows, :].astype(f32) * rstd[rows, 256:257]
        xh = xhat2[rows, :].astype(f32)
        eg = e * vecs[7:8, :]
        add_sum(6, e * xh)
        add_sum(7, e)
        value = (eg - jnp.mean(eg, axis=1, keepdims=True) - xh * jnp.mean(eg * xh, axis=1, keepdims=True)) * rstd[
            rows, 128:129
        ]
        add_sum(5, value)
        d[rows, :] = value
        d2low[rows, :] = value.astype(bf)

    def spread(piece, k, peer):
        return remote(piece, piece, gs.at[k], gr.at[k], peer)

    hop = spread(gathered.at[core, z, y, x], 0, other_core)
    ready("cot")
    ready("xhat2")
    norm_two(0)
    hop.wait_recv()
    hop = spread(gathered.at[:, z, y, x], 1, other_x)
    norm_two(1)
    hop.wait_recv()
    hop = spread(gathered.at[:, z, y], 2, other_y)
    norm_two(2)
    hop.wait_recv()
    hops = [spread(gathered.at[:, z], 3 + k, other_z[k]) for k in range(3)]
    norm_two(3)
    for hop in hops:
        hop.wait_recv()
    d_cls = contrast_math(core * 16 + chip, pay, gathered, loss)

    starts = [64 * i for i in range(6)] + [384 + 256 * i for i in range(2)]
    e = d_cls[0:8, :]
    xh = jnp.concatenate([xhat2[r:r + 1, :].astype(f32) for r in starts], axis=0)
    scale_rows = jnp.concatenate([rstd[r:r + 1, 128:129] for r in starts], axis=0)
    eg = e * vecs[7:8, :]
    add_sum(6, e * xh)
    add_sum(7, e)
    extra = (eg - jnp.mean(eg, axis=1, keepdims=True) - xh * jnp.mean(eg * xh, axis=1, keepdims=True)) * scale_rows
    add_sum(5, extra)
    for i, r in enumerate(starts):
        top = lax.broadcasted_iota(jnp.int32, (16, 1), 0) == 0
        value = d[r:r + 16, :] + jnp.where(top, extra[i:i + 1, :], 0.0)
        d[r:r + 16, :] = value
        d2low[r:r + 16, :] = value.astype(bf)

    def plus(a, b):
        return (a.astype(f32) + b.astype(f32)).astype(bf)

    got = {}

    def halves(u):
        if u < 4:
            return both_o.at[u], from_o.at[u], r1_o.at[u], r2_o.at[u]
        return both_i.at[u - 4], from_i.at[u - 4], r1_i.at[u - 4], r2_i.at[u - 4]

    def cross(u):
        mine, came, _, _ = halves(u)
        got["c", u] = remote(mine.at[1 - core], came, cs.at[u], cr.at[u], other_core)

    def first_hop(u):
        mine, came, one, _ = halves(u)
        got["c", u].wait_recv()
        if u < 4:
            for a in range(2):
                mine[core, a] = plus(mine[core, a], came[a])
            src = mine.at[core, :, 1 - x] if u % 2 == 0 else mine.at[core, 1 - y]
        else:
            for a in range(4):
                mine[core, a] = plus(mine[core, a], came[a])
            src = mine.at[core, :, :, 1 - x] if u % 2 == 0 else mine.at[core, :, 1 - y]
        got["1", u] = remote(src, one, s1.at[u], q1.at[u], other_x if u % 2 == 0 else other_y)

    def second_hop(u):
        mine, _, one, two = halves(u)
        got["1", u].wait_recv()
        even = u % 2 == 0
        if u < 4:
            for a in range(2):
                if even:
                    mine[core, a, x] = plus(mine[core, a, x], one[a])
                else:
                    mine[core, y, a] = plus(mine[core, y, a], one[a])
            src = mine.at[core, 1 - y, x] if even else mine.at[core, y, 1 - x]
        else:
            for a in range(4):
                for b in range(2):
                    if even:
                        mine[core, a, b, x] = plus(mine[core, a, b, x], one[a, b])
                    else:
                        mine[core, a, y, b] = plus(mine[core, a, y, b], one[a, b])
            src = mine.at[core, :, 1 - y, x] if even else mine.at[core, :, y, 1 - x]
        got["2", u] = remote(src, two, s2.at[u], q2.at[u], other_y if even else other_x)

    def third_hop(u):
        if u < 4:
            for v in range(4):
                got["2", v].wait_recv()
                both_o[v, core, y, x] = plus(both_o[v, core, y, x], r2_o[v])
            for k in range(3):
                got["3", u, k] = remote(
                    both_o.at[(z + k + 1) % 4, core, y, x], r3_o.at[k], s3.at[0, k], q3.at[0, k], other_z[k]
                )
            return
        got["2", u].wait_recv()
        mine, _, _, two = halves(u)
        for a in range(4):
            mine[core, a, y, x] = plus(mine[core, a, y, x], two[a])
        for k in range(3):
            got["3", u, k] = remote(
                mine.at[core, (z + k + 1) % 4, y, x], r3_i.at[u - 4, k], s3.at[u - 3, k], q3.at[u - 3, k], other_z[k]
            )

    cols = pl.ds(pl.multiple_of(core * 384, 128), 384)

    def last_hop(u):
        if u < 4:
            total = both_o[z, core, y, x].astype(f32)
            for k in range(3):
                got["3", u, k].wait_recv()
                total = total + r3_o[k].astype(f32)
            for a in range(4):
                fin[a, :, cols] = total[48 * a:48 * a + 48]
                got["4", a] = remote(fin.at[a, :, cols], fin.at[a, :, cols], s4.at[a], q4.at[a], other_core)
            return
        mine = both_i.at[u - 4]
        total = mine[core, z, y, x].astype(f32)
        for k in range(3):
            got["3", u, k].wait_recv()
            total = total + r3_i[u - 4, k].astype(f32)
        fin[u, :, cols] = total
        got["4", u] = remote(fin.at[u, :, cols], fin.at[u, :, cols], s4.at[u], q4.at[u], other_core)

    def make_outer(u):
        for a in range(2):
            cut = bufa[:, 768 * u + 384 * a:768 * u + 384 * a + 384]
            res = dot(cut, d2low[...], TN).astype(bf)
            for h in range(2):
                for b in range(2):
                    both_o[u, h, a, b] = res[192 * b:192 * b + 192, 384 * h:384 * h + 384]
        cross(u)

    def make_unit(u, left, right):
        for a in range(2):
            res = dot(left[:, 384 * a:384 * a + 384], right, TN).astype(bf)
            for h in range(2):
                for b in range(8):
                    both_i[u - 4, h, 2 * a + b // 4, (b // 2) % 2, b % 2] = res[
                        48 * b:48 * b + 48, 384 * h:384 * h + 384
                    ]
        cross(u)

    ready("inner")
    for u in range(4):
        make_outer(u)
        if u >= 1:
            first_hop(u - 1)
    load("qkvx", (qkvx_h, bufa))
    ready("wu")
    ready("slope")

    def make_pre(g):
        @pl.loop(0, 3)
        def _(j):
            lanes = pl.ds(pl.multiple_of(768 * g + j * 256, 256), 256)
            back = dot(d2low[...], w1[lanes, :], NT) * bufb[:, lanes].astype(f32)
            bufb[:, lanes] = back.astype(bf)
            sums[8 + g:9 + g, pl.ds(pl.multiple_of(j * 256, 256), 256)] = jnp.sum(back, axis=0, keepdims=True)

    make_pre(0)
    first_hop(3)
    make_pre(1)
    second_hop(0)
    make_pre(2)
    second_hop(1)
    make_pre(3)
    load("w1", (wq_h, w1.at[0:768]), (wk_h, w1.at[768:1536]), (wv_h, w1.at[1536:2304]), (wo_h, w1.at[2304:3072]))
    ready("low1")
    for u in range(4):
        make_unit(4 + u, low1, bufb[:, 768 * u:768 * u + 768])
        if u >= 1:
            first_hop(3 + u)
        if u == 0:
            second_hop(2)
        if u == 1:
            second_hop(3)
    ready("wi")
    ready("xhat1")

    def norm_one(i):
        rows = pl.ds(224 * i, 224)
        e = d[rows, :] + dot(bufb[rows, :], w2[...], NT)
        xh = xhat1[rows, :].astype(f32)
        eg = e * vecs[4:5, :]
        add_sum(3, e * xh)
        add_sum(4, e)
        value = (eg - jnp.mean(eg, axis=1, keepdims=True) - xh * jnp.mean(eg * xh, axis=1, keepdims=True)) * rstd[
            rows, 0:1
        ]
        add_sum(2, value)
        d[rows, :] = value
        cot[rows, :] = value.astype(bf)

    norm_one(0)
    first_hop(7)
    norm_one(1)
    third_hop(0)
    norm_one(2)
    second_hop(4)
    norm_one(3)
    load("prob", (prob_h, w2))
    ready("ctx")
    make_unit(8, ctx, cot[...])
    second_hop(5)
    ready("w1")

    @pl.loop(0, 3)
    def _(j):
        lanes = pl.ds(pl.multiple_of(j * 256, 256), 256)
        xhat2[:, lanes] = dot(cot[...], w1[pl.ds(pl.multiple_of(2304 + j * 256, 256), 256), :], NT).astype(bf)

    first_hop(8)
    ready("prob")
    ready("qkvx")
    low, high = pair_masks()

    def attend(r0, n, p, prob):
        rows = pl.ds(r0, n)
        lanes = pl.ds(pl.multiple_of(p * 128, 128), 128)
        q = bufa[rows, lanes]
        k = bufa[rows, pl.ds(pl.multiple_of(768 + p * 128, 128), 128)]
        v = bufa[rows, pl.ds(pl.multiple_of(1536 + p * 128, 128), 128)]
        do = xhat2[rows, lanes]
        dq = dk = dv = None
        for h, mask in enumerate((low, high)):
            ph = prob[:, h * n:(h + 1) * n]
            pf = ph.astype(f32)
            dp = dot(do, v * mask, NT)
            ds = (pf * (dp - jnp.sum(pf * dp, axis=1, keepdims=True))).astype(bf)
            a = dot(ph, do * mask, TN)
            b = dot(ds, k * mask)
            c = dot(ds, q * mask, TN)
            dq = b if h == 0 else dq + b
            dk = c if h == 0 else dk + c
            dv = a if h == 0 else dv + a
        dq = dq * HEAD ** (-0.5)
        bufb[rows, lanes] = dq.astype(bf)
        bufb[rows, pl.ds(pl.multiple_of(768 + p * 128, 128), 128)] = dk.astype(bf)
        bufb[rows, pl.ds(pl.multiple_of(1536 + p * 128, 128), 128)] = dv.astype(bf)
        sums[0:1, lanes] += jnp.sum(dq, axis=0, keepdims=True)
        sums[1:2, lanes] += jnp.sum(dv, axis=0, keepdims=True)

    def attend_long(n):
        @pl.loop(0, 6)
        def _(p):
            attend(384 + 256 * n, 256, p, w2[256 * n:256 * n + 256, pl.ds(pl.multiple_of(p * 512, 512), 512)])

    def attend_short(g):
        @pl.loop(0, 6)
        def _(p):
            i = g * 6 + p
            start = pl.multiple_of(512 + 128 * (i // 12), 128)
            attend(
                128 * g, 128, p, w2[pl.ds(start, 128), pl.ds(pl.multiple_of((i % 12) * 256, 256), 256)]
            )

    attend_long(0)
    second_hop(6)
    attend_long(1)
    second_hop(7)
    attend_short(0)
    last_hop(0)
    attend_short(1)
    third_hop(4)
    attend_short(2)
    third_hop(5)
    rows_x = bufa.at[:, 2304:3072]
    make_unit(9, rows_x, bufb[:, 1536:2304])
    second_hop(8)
    make_unit(10, rows_x, bufb[:, 768:1536])
    first_hop(9)
    make_unit(11, rows_x, bufb[:, 0:768])
    first_hop(10)
    last_hop(4)
    last_hop(5)
    third_hop(6)
    vec_hops = {}
    vec_hops[0] = remote(sums, vr.at[0], vs.at[0], vq.at[0], other_core)

    def drow(i):
        rows = pl.ds(224 * i, 224)
        total = d[rows, :]
        for m in range(3):
            total = total + dot(bufb[rows, 768 * m:768 * m + 768], w1[768 * m:768 * m + 768, :], NT)
        d[rows, :] = total

    drow(0)
    first_hop(11)
    third_hop(7)
    drow(1)
    vec_hops[0].wait()
    sums[...] += vr[0]
    vec_hops[1] = remote(sums, vr.at[1], vs.at[1], vq.at[1], other_x)
    last_hop(6)
    second_hop(9)
    drow(2)
    third_hop(8)
    last_hop(7)
    drow(3)
    out = pltpu.make_async_copy(d, drows_h, osem.at[0])
    out.start()
    second_hop(10)
    vec_hops[1].wait()
    sums[...] += vr[1]
    vec_hops[2] = remote(sums, vr.at[2], vs.at[2], vq.at[2], other_y)
    second_hop(11)
    third_hop(9)
    last_hop(8)
    third_hop(10)
    third_hop(11)
    vec_hops[2].wait()
    sums[...] += vr[2]
    vz = [remote(sums, vr.at[3 + k], vs.at[3 + k], vq.at[3 + k], other_z[k]) for k in range(3)]
    last_hop(9)
    last_hop(10)
    last_hop(11)
    for hop in vz:
        hop.wait_recv()
    sums_o[...] = sums[...] + vr[3] + vr[4] + vr[5]
    for u in range(12):
        got["4", u].wait_recv()
    final = pltpu.make_async_copy(fin, fin_h, osem.at[1])
    final.start()
    for copy in sent:
        if not any(copy is item for item in (vec_hops[0], vec_hops[1], vec_hops[2])):
            copy.wait_send()
    out.wait()
    final.wait()


def contrast_math(me, pay, gathered, loss):
    rows = 512
    width = 768
    scale = width ** (-0.5)
    table = gathered[...].reshape(rows, 896)
    embed = table[:, :width]
    extras = table[:, width:]
    pick = (
        lax.broadcasted_iota(jnp.int32, (16, 128), 0) == lax.broadcasted_iota(jnp.int32, (16, 128), 1)
    ).astype(bf)
    ids = dot(pick, extras, NT)
    positive = ids[0:1] * 16.0 + ids[1:2]
    negative = ids[2:3] * 16.0 + ids[3:4]
    match = dot(embed, embed, NT) * scale
    row = lax.broadcasted_iota(jnp.int32, (rows, 1), 0)
    is_passage = (row % 16) < 8
    number = jnp.where(is_passage, (row // 16) * 8 + row % 16, -1).astype(f32)
    masked = jnp.where(is_passage, match, -1e30)
    top = jnp.max(masked, axis=0, keepdims=True)
    lse = jnp.log(jnp.sum(jnp.exp(masked - top), axis=0, keepdims=True)) + top
    pos_score = jnp.sum(jnp.where(number == positive, match, 0.0), axis=0, keepdims=True)
    neg_score = jnp.sum(jnp.where(number == negative, match, 0.0), axis=0, keepdims=True)
    gap = neg_score - pos_score
    tail = jnp.exp(-jnp.abs(gap))
    softplus = jnp.maximum(gap, 0.0) + jnp.log1p(tail)
    loss[...] = jnp.broadcast_to(lse - pos_score + softplus, loss.shape)
    sig = jnp.where(gap >= 0, 1.0, tail) / (1.0 + tail)
    own = dot(pay[:, :width], embed, NT) * scale
    own_row = lax.broadcasted_iota(jnp.int32, (16, 1), 0)
    own_number = jnp.where(own_row < 8, me * 8 + own_row, -2).astype(f32)
    lane = lax.broadcasted_iota(jnp.int32, (1, rows), 1) % 16
    used = (own_row < 8) & (lane >= 8) & (lane < 12)
    coef = jnp.exp(jnp.where(used, own - lse, -1e30))
    coef = coef - jnp.where(own_number == positive, 1.0 + sig, 0.0) + jnp.where(own_number == negative, sig, 0.0)
    coef = jnp.where(used, contrast_weight * coef, 0.0)
    total = jnp.zeros((16, width), f32)
    for _ in range(3):
        part = coef.astype(bf)
        total = total + dot(part, embed)
        coef = coef - part.astype(f32)
    return total * scale


def backward(pay, vecs, rstd, *arrays):
    any_ = pl.BlockSpec(memory_space=pl.ANY)
    vmem = pl.BlockSpec(memory_space=pltpu.VMEM)
    sds = jax.ShapeDtypeStruct
    dma = pltpu.SemaphoreType.DMA
    mem = pltpu.VMEM
    return pl.pallas_call(
        backward_kernel,
        out_shape=(sds((896, 768), f32), sds((12, 48, 768), f32), sds((16, 768), f32), sds((8, 512), f32)),
        in_specs=[vmem] * 3 + [any_] * 16,
        out_specs=(any_, any_, vmem, vmem),
        scratch_shapes=[
            mem((2, 4, 2, 2, 16, 896), bf),
            mem((896, 3072), bf), mem((896, 3072), bf), mem((3072, 768), bf), mem((768, 3072), bf),
            mem((896, 768), bf), mem((896, 768), bf), mem((896, 768), bf), mem((896, 768), bf), mem((896, 768), bf),
            mem((896, 768), f32), mem((896, 768), bf), mem((12, 48, 768), f32), mem((16, 768), f32),
            mem((6, 16, 768), f32),
            mem((4, 2, 2, 2, 192, 384), bf), mem((4, 2, 2, 192, 384), bf), mem((4, 2, 192, 384), bf),
            mem((4, 192, 384), bf), mem((3, 192, 384), bf),
            mem((8, 2, 4, 2, 2, 48, 384), bf), mem((8, 4, 2, 2, 48, 384), bf), mem((8, 4, 2, 48, 384), bf),
            mem((8, 4, 48, 384), bf), mem((8, 3, 48, 384), bf),
            dma((20,)), dma((2,)), dma((6,)), dma((6,)),
            dma((12,)), dma((12,)), dma((12,)), dma((12,)), dma((12,)), dma((12,)),
            dma((9, 3)), dma((9, 3)), dma((12,)), dma((12,)), dma((6,)), dma((6,)),
        ],
        compiler_params=pltpu.CompilerParams(
            collective_id=1, has_side_effects=True, vmem_limit_bytes=64 * 1024 * 1024 - 65536
        ),
        name="backward",
    )(pay, vecs, rstd, *arrays)


def finish_kernel(
    drows, fin, sums, loss,
    o_short, o_long, o_loss, o_wq, o_bq, o_wk, o_wv, o_bv, o_wo, o_bo, o_g1, o_s1, o_wi, o_bi, o_wu, o_bu, o_g2, o_s2,
    sem,
):
    core, chip, z, y, x = place()
    copies = []

    def move(src, dst):
        copy = pltpu.make_async_copy(src, dst, sem.at[len(copies)])
        copy.start()
        copies.append(copy)

    move(drows.at[0:384], o_short)
    move(drows.at[384:896], o_long)
    for u in range(4):
        move(fin.at[u], o_wu.at[48 * u:48 * u + 48])
        move(fin.at[4 + u], o_wi.at[:, 768 * u:768 * u + 768])
    for u, dst in enumerate((o_wo, o_wv, o_wk, o_wq)):
        move(fin.at[8 + u], dst)
    small = pltpu.roll(sums[0:8, :], (768 - 48 * chip) % 768, 1)
    for i, dst in enumerate((o_bq, o_bv, o_bo, o_g1, o_s1, o_bu, o_g2, o_s2)):
        dst[...] = small[i, 0:48]
    wide = pltpu.roll(sums[pl.ds(8 + z, 1), :], (768 - 192 * (chip % 4)) % 768, 1)
    o_bi[...] = wide[0, 0:192]
    mine = pltpu.roll(loss[...], (512 - 16 * (core * 16 + chip) - 8) % 512, 1)
    o_loss[...] = mine[0, 0:4]
    for copy in copies:
        copy.wait()


def finish(drows, fin, sums, loss):
    any_ = pl.BlockSpec(memory_space=pl.ANY)
    vmem = pl.BlockSpec(memory_space=pltpu.VMEM)
    sds = jax.ShapeDtypeStruct
    square = (sds((48, 768), f32), any_)
    line = (sds((48,), f32), vmem)
    outs = [
        (sds((384, 768), f32), any_), (sds((512, 768), f32), any_), (sds((4,), f32), vmem),
        square, line, square, square, line, square, line, line, line,
        (sds((48, 3072), f32), any_), (sds((192,), f32), vmem), (sds((192, 768), f32), any_), line, line, line,
    ]
    return pl.pallas_call(
        finish_kernel,
        out_shape=tuple(item[0] for item in outs),
        in_specs=[vmem] * 4,
        out_specs=tuple(item[1] for item in outs),
        scratch_shapes=[pltpu.SemaphoreType.DMA((14,))],
        compiler_params=pltpu.CompilerParams(vmem_limit_bytes=16 * 1024 * 1024),
        name="finish",
    )(drows, fin, sums, loss)


def fast_body(
    short_tokens, long_tokens, short_lengths, long_lengths, short_cotangent, long_cotangent, queries, positives,
    hard_negatives, w_query, b_query, w_key, w_value, b_value, w_out, b_out, gain_one, shift_one, w_inner, b_inner,
    w_outer, b_outer, gain_two, shift_two,
):
    weights = (w_query, w_key, w_value, w_out, w_inner, w_outer)
    small = (queries, b_query, b_value, b_out, gain_one, shift_one, b_outer, gain_two, shift_two, b_inner)
    (
        out_short, out_long, qkvx, prob, ctx, xhat1, low1, inner, slope, xhat2, rstd, payload, vecs,
    ) = forward(
        short_tokens, long_tokens, short_lengths, long_lengths, positives, hard_negatives, weights, small
    )
    drows, fin, sums, loss = backward(
        payload, vecs, rstd, short_cotangent.reshape(384, 768), long_cotangent.reshape(512, 768), qkvx, prob, ctx,
        xhat1, low1, inner, slope, xhat2, *weights,
    )
    (
        d_short, d_long, losses, g_wq, g_bq, g_wk, g_wv, g_bv, g_wo, g_bo, g_g1, g_s1, g_wi, g_bi, g_wu, g_bu, g_g2,
        g_s2,
    ) = finish(drows, fin, sums, loss)
    return (
        out_short.reshape(short_tokens.shape), out_long.reshape(long_tokens.shape),
        d_short.reshape(short_tokens.shape), d_long.reshape(long_tokens.shape),
        losses, g_wq, g_bq, g_wk, g_wv, g_bv, g_wo, g_bo, g_g1, g_s1, g_wi, g_bi, g_wu, g_bu, g_g2, g_s2,
    )


def solution(mesh):
    fast = mesh.shape["grp"] == 2 and mesh.shape["blk"] == 16
    in_specs = (
        P(("grp", "blk"), None, None),
        P(("grp", "blk"), None, None),
        P(("grp", "blk")),
        P(("grp", "blk")),
        P(("grp", "blk"), None, None),
        P(("grp", "blk"), None, None),
        P(("grp", "blk"), None),
        P(("grp", "blk")),
        P(("grp", "blk")),
        P(),
        P(),
        P(),
        P(),
        P(),
        P(),
        P(),
        P(),
        P(),
        P(),
        P(),
        P(),
        P(),
        P(),
        P(),
    )
    out_specs = (
        P(("grp", "blk"), None, None),
        P(("grp", "blk"), None, None),
        P(("grp", "blk"), None, None),
        P(("grp", "blk"), None, None),
        P(("grp", "blk")),
        P("blk", None),
        P("blk"),
        P("blk", None),
        P("blk", None),
        P("blk"),
        P("blk", None),
        P("blk"),
        P("blk"),
        P("blk"),
        P("blk", None),
        P("blk"),
        P("blk", None),
        P("blk"),
        P("blk"),
        P("blk"),
    )
    return jax.shard_map(fast_body if fast else body, mesh=mesh, in_specs=in_specs, out_specs=out_specs, check_vma=False)
```

```python
import jax
import jax.numpy as jnp
from jax import lax
from jax.experimental import pallas as pl
from jax.experimental.pallas import tpu as pltpu
from jax.sharding import PartitionSpec as P

HEADS = 12
HEAD = 64


norm_epsilon = 1e-05
contrast_weight = 8.0
masked_value = -1000000000.0
bf = jnp.bfloat16
f32 = jnp.float32
NT = (((1,), (1,)), ((), ()))
TN = (((0,), (0,)), ((), ()))
NN = (((1,), (0,)), ((), ()))
MESH = pl.DeviceIdType.MESH


def layer_norm(value, gain, shift):
    center = value - jnp.mean(value, axis=-1, keepdims=True)
    spread = jnp.mean(center * center, axis=-1, keepdims=True)
    return center * lax.rsqrt(spread + norm_epsilon) * gain + shift


def exact_gelu(value):
    return jax.nn.gelu(value, approximate=False)


def split_heads(value, count, seq):
    return value.reshape(count, seq, HEADS, HEAD)


def attention_scores(query, keys, valid):
    scores = jnp.einsum(
        "nqhd,nkhd->nhqk", query, keys, preferred_element_type=jnp.float32
    ) * HEAD ** (-0.5)
    return jnp.where(valid[:, None, None, :], scores, masked_value)


def forward_bucket(tokens, lengths, params):
    (
        w_query,
        b_query,
        w_key,
        w_value,
        b_value,
        w_out,
        b_out,
        gain_one,
        shift_one,
        w_inner,
        b_inner,
        w_outer,
        b_outer,
        gain_two,
        shift_two,
    ) = params
    count, seq, width = tokens.shape
    rows = tokens.reshape(count * seq, width)
    query = (jnp.dot(rows, w_query, preferred_element_type=jnp.float32) + b_query).astype(
        jnp.bfloat16
    )
    keys = jnp.dot(rows, w_key, preferred_element_type=jnp.float32).astype(jnp.bfloat16)
    values = (jnp.dot(rows, w_value, preferred_element_type=jnp.float32) + b_value).astype(
        jnp.bfloat16
    )
    valid = lax.broadcasted_iota(jnp.int32, (count, seq), 1) < lengths[:, None]
    scores = attention_scores(split_heads(query, count, seq), split_heads(keys, count, seq), valid)
    top = jnp.max(scores, axis=-1, keepdims=True)
    expo = jnp.exp(scores - top)
    total = jnp.sum(expo, axis=-1, keepdims=True)
    logsum = top + jnp.log(total)
    probs = (expo / total).astype(jnp.bfloat16)
    context = (
        jnp.einsum(
            "nhqk,nkhd->nqhd",
            probs,
            split_heads(values, count, seq),
            preferred_element_type=jnp.float32,
        )
        .astype(jnp.bfloat16)
        .reshape(count * seq, width)
    )
    mixed_one = rows + jnp.dot(context, w_out, preferred_element_type=jnp.float32) + b_out
    first = layer_norm(mixed_one, gain_one, shift_one)
    first_low = first.astype(jnp.bfloat16)
    pre = jnp.dot(first_low, w_inner, preferred_element_type=jnp.float32) + b_inner
    inner = exact_gelu(pre).astype(jnp.bfloat16)
    mixed_two = first + jnp.dot(inner, w_outer, preferred_element_type=jnp.float32) + b_outer
    output = layer_norm(mixed_two, gain_two, shift_two)
    kept = (
        rows,
        query,
        keys,
        values,
        valid,
        logsum,
        context,
        mixed_one,
        first_low,
        pre,
        inner,
        mixed_two,
    )
    return (output.reshape(count, seq, width), kept)


def backward_bucket(d_output, kept, params):
    (
        w_query,
        b_query,
        w_key,
        w_value,
        b_value,
        w_out,
        b_out,
        gain_one,
        shift_one,
        w_inner,
        b_inner,
        w_outer,
        b_outer,
        gain_two,
        shift_two,
    ) = params
    (
        rows,
        query,
        keys,
        values,
        valid,
        logsum,
        context,
        mixed_one,
        first_low,
        pre,
        inner,
        mixed_two,
    ) = kept
    count, seq = valid.shape
    width = rows.shape[1]
    f32 = jnp.float32
    unused, pull_two = jax.vjp(layer_norm, mixed_two, gain_two, shift_two)
    d_mixed_two, grad_gain_two, grad_shift_two = pull_two(d_output)
    d_second = d_mixed_two.astype(jnp.bfloat16)
    grad_w_outer = jnp.einsum("rf,rd->fd", inner, d_second, preferred_element_type=f32)
    grad_b_outer = jnp.sum(d_mixed_two, axis=0)
    d_inner = jnp.einsum("rd,fd->rf", d_second, w_outer, preferred_element_type=f32)
    unused, pull_gelu = jax.vjp(exact_gelu, pre)
    (d_pre,) = pull_gelu(d_inner)
    d_pre_low = d_pre.astype(jnp.bfloat16)
    grad_w_inner = jnp.einsum("rd,rf->df", first_low, d_pre_low, preferred_element_type=f32)
    grad_b_inner = jnp.sum(d_pre, axis=0)
    d_first = d_mixed_two + jnp.einsum("rf,df->rd", d_pre_low, w_inner, preferred_element_type=f32)
    unused, pull_one = jax.vjp(layer_norm, mixed_one, gain_one, shift_one)
    d_mixed_one, grad_gain_one, grad_shift_one = pull_one(d_first)
    d_attended = d_mixed_one.astype(jnp.bfloat16)
    grad_w_out = jnp.einsum("rd,re->de", context, d_attended, preferred_element_type=f32)
    grad_b_out = jnp.sum(d_mixed_one, axis=0)
    d_context = jnp.einsum("re,de->rd", d_attended, w_out, preferred_element_type=f32).astype(
        jnp.bfloat16
    )
    query_heads = split_heads(query, count, seq)
    key_heads = split_heads(keys, count, seq)
    value_heads = split_heads(values, count, seq)
    context_heads = split_heads(d_context, count, seq)
    probs = jnp.exp(attention_scores(query_heads, key_heads, valid) - logsum)
    d_probs = jnp.einsum("nqhd,nkhd->nhqk", context_heads, value_heads, preferred_element_type=f32)
    d_values = jnp.einsum(
        "nhqk,nqhd->nkhd", probs.astype(jnp.bfloat16), context_heads, preferred_element_type=f32
    ).reshape(count * seq, width)
    d_scores = (probs * (d_probs - jnp.sum(probs * d_probs, axis=-1, keepdims=True))).astype(
        jnp.bfloat16
    )
    d_query = jnp.einsum(
        "nhqk,nkhd->nqhd", d_scores, key_heads, preferred_element_type=f32
    ).reshape(count * seq, width) * HEAD ** (-0.5)
    d_keys = jnp.einsum(
        "nhqk,nqhd->nkhd", d_scores, query_heads, preferred_element_type=f32
    ).reshape(count * seq, width) * HEAD ** (-0.5)
    grad_b_query = jnp.sum(d_query, axis=0)
    grad_b_value = jnp.sum(d_values, axis=0)
    query_low = d_query.astype(jnp.bfloat16)
    keys_low = d_keys.astype(jnp.bfloat16)
    values_low = d_values.astype(jnp.bfloat16)
    grad_w_query = jnp.einsum("rd,re->de", rows, query_low, preferred_element_type=f32)
    grad_w_key = jnp.einsum("rd,re->de", rows, keys_low, preferred_element_type=f32)
    grad_w_value = jnp.einsum("rd,re->de", rows, values_low, preferred_element_type=f32)
    d_rows = d_mixed_one + jnp.einsum("re,de->rd", query_low, w_query, preferred_element_type=f32)
    d_rows = d_rows + jnp.einsum("re,de->rd", keys_low, w_key, preferred_element_type=f32)
    d_rows = d_rows + jnp.einsum("re,de->rd", values_low, w_value, preferred_element_type=f32)
    grads = (
        grad_w_query,
        grad_b_query,
        grad_w_key,
        grad_w_value,
        grad_b_value,
        grad_w_out,
        grad_b_out,
        grad_gain_one,
        grad_shift_one,
        grad_w_inner,
        grad_b_inner,
        grad_w_outer,
        grad_b_outer,
        grad_gain_two,
        grad_shift_two,
    )
    return (d_rows.reshape(count, seq, width), grads)


def contrast_whole(cls_low, queries, positives, hard_negatives, scale):
    f32 = jnp.float32
    passage_count = cls_low.shape[0]
    query_count = queries.shape[0]
    me = lax.axis_index(("grp", "blk"))
    own_ids = me * passage_count + lax.broadcasted_iota(jnp.int32, (passage_count,), 0)
    start_top = jnp.full((query_count,), -1e30, f32)
    piece = lax.all_gather(cls_low, ("grp", "blk"), axis=0, tiled=True)
    top = start_top
    scores = jnp.einsum("qd,pd->qp", queries, piece, preferred_element_type=f32) * scale
    ids = lax.broadcasted_iota(jnp.int32, (1, piece.shape[0]), 1)
    new_top = jnp.maximum(top, jnp.max(scores, axis=1))
    total = jnp.sum(jnp.exp(scores - new_top[:, None]), axis=1)
    pos_score = jnp.sum(jnp.where(ids == positives[:, None], scores, 0.0), axis=1)
    neg_score = jnp.sum(jnp.where(ids == hard_negatives[:, None], scores, 0.0), axis=1)
    top, total, pos_score, neg_score = (new_top, total, pos_score, neg_score)
    logsum = top + jnp.log(total)
    losses = logsum - pos_score + jax.nn.softplus(neg_score - pos_score)
    sigma = jax.nn.sigmoid(neg_score - pos_score)
    coef_pos = contrast_weight * (1.0 + sigma)
    coef_neg = contrast_weight * sigma
    query_piece = lax.all_gather(queries.astype(f32), ("grp", "blk"), axis=0, tiled=True)
    lse_piece = lax.all_gather(logsum, ("grp", "blk"), axis=0, tiled=True)
    pos_coef = lax.all_gather(coef_pos, ("grp", "blk"), axis=0, tiled=True)
    neg_coef = lax.all_gather(coef_neg, ("grp", "blk"), axis=0, tiled=True)
    pos_piece = lax.all_gather(positives, ("grp", "blk"), axis=0, tiled=True)
    neg_piece = lax.all_gather(hard_negatives, ("grp", "blk"), axis=0, tiled=True)
    scores = (
        jnp.einsum(
            "pd,qd->pq", cls_low, query_piece.astype(jnp.bfloat16), preferred_element_type=f32
        )
        * scale
    )
    weight = contrast_weight * jnp.exp(scores - lse_piece[None, :])
    weight = weight - jnp.where(own_ids[:, None] == pos_piece[None, :], pos_coef[None, :], 0.0)
    weight = weight + jnp.where(own_ids[:, None] == neg_piece[None, :], neg_coef[None, :], 0.0)
    d_cls = (
        jnp.dot(weight, query_piece, precision=lax.Precision.HIGHEST, preferred_element_type=f32)
        * scale
    )
    return losses, d_cls


def reduce_whole(totals):
    reduced = (
        lax.psum_scatter(totals[0], "blk", scatter_dimension=0, tiled=True),
        lax.psum_scatter(totals[1], "blk", scatter_dimension=0, tiled=True),
        lax.psum_scatter(totals[2], "blk", scatter_dimension=0, tiled=True),
        lax.psum_scatter(totals[3], "blk", scatter_dimension=0, tiled=True),
        lax.psum_scatter(totals[4], "blk", scatter_dimension=0, tiled=True),
        lax.psum_scatter(totals[5], "blk", scatter_dimension=0, tiled=True),
        lax.psum_scatter(totals[6], "blk", scatter_dimension=0, tiled=True),
        lax.psum_scatter(totals[7], "blk", scatter_dimension=0, tiled=True),
        lax.psum_scatter(totals[8], "blk", scatter_dimension=0, tiled=True),
        lax.psum_scatter(totals[9], "blk", scatter_dimension=0, tiled=True),
        lax.psum_scatter(totals[10], "blk", scatter_dimension=0, tiled=True),
        lax.psum_scatter(totals[11], "blk", scatter_dimension=0, tiled=True),
        lax.psum_scatter(totals[12], "blk", scatter_dimension=0, tiled=True),
        lax.psum_scatter(totals[13], "blk", scatter_dimension=0, tiled=True),
        lax.psum_scatter(totals[14], "blk", scatter_dimension=0, tiled=True),
    )
    reduced = (
        lax.psum(reduced[0].astype(jnp.bfloat16), "grp").astype(jnp.float32),
        lax.psum(reduced[1].astype(jnp.bfloat16), "grp").astype(jnp.float32),
        lax.psum(reduced[2].astype(jnp.bfloat16), "grp").astype(jnp.float32),
        lax.psum(reduced[3].astype(jnp.bfloat16), "grp").astype(jnp.float32),
        lax.psum(reduced[4].astype(jnp.bfloat16), "grp").astype(jnp.float32),
        lax.psum(reduced[5].astype(jnp.bfloat16), "grp").astype(jnp.float32),
        lax.psum(reduced[6].astype(jnp.bfloat16), "grp").astype(jnp.float32),
        lax.psum(reduced[7].astype(jnp.bfloat16), "grp").astype(jnp.float32),
        lax.psum(reduced[8].astype(jnp.bfloat16), "grp").astype(jnp.float32),
        lax.psum(reduced[9].astype(jnp.bfloat16), "grp").astype(jnp.float32),
        lax.psum(reduced[10].astype(jnp.bfloat16), "grp").astype(jnp.float32),
        lax.psum(reduced[11].astype(jnp.bfloat16), "grp").astype(jnp.float32),
        lax.psum(reduced[12].astype(jnp.bfloat16), "grp").astype(jnp.float32),
        lax.psum(reduced[13].astype(jnp.bfloat16), "grp").astype(jnp.float32),
        lax.psum(reduced[14].astype(jnp.bfloat16), "grp").astype(jnp.float32),
    )
    return reduced


def body(
    short_tokens,
    long_tokens,
    short_lengths,
    long_lengths,
    short_cotangent,
    long_cotangent,
    queries,
    positives,
    hard_negatives,
    w_query,
    b_query,
    w_key,
    w_value,
    b_value,
    w_out,
    b_out,
    gain_one,
    shift_one,
    w_inner,
    b_inner,
    w_outer,
    b_outer,
    gain_two,
    shift_two,
):
    f32 = jnp.float32
    params = (
        w_query,
        b_query.astype(f32),
        w_key,
        w_value,
        b_value.astype(f32),
        w_out,
        b_out.astype(f32),
        gain_one.astype(f32),
        shift_one.astype(f32),
        w_inner,
        b_inner.astype(f32),
        w_outer,
        b_outer.astype(f32),
        gain_two.astype(f32),
        shift_two.astype(f32),
    )
    short_out, short_kept = forward_bucket(short_tokens, short_lengths, params)
    long_out, long_kept = forward_bucket(long_tokens, long_lengths, params)
    short_count = short_tokens.shape[0]
    width = short_tokens.shape[2]
    scale = width ** (-0.5)
    cls_low = jnp.concatenate([short_out[:, 0, :], long_out[:, 0, :]], axis=0).astype(jnp.bfloat16)
    passage_count = cls_low.shape[0]
    query_count = queries.shape[0]
    me = lax.axis_index(("grp", "blk"))
    losses, d_cls = contrast_whole(cls_low, queries, positives, hard_negatives, scale)
    short_d = short_cotangent.astype(f32) * short_kept[4][:, :, None]
    short_d = short_d.at[:, 0, :].add(d_cls[:short_count])
    long_d = long_cotangent.astype(f32) * long_kept[4][:, :, None]
    long_d = long_d.at[:, 0, :].add(d_cls[short_count:])
    short_grad, short_terms = backward_bucket(short_d.reshape(-1, width), short_kept, params)
    long_grad, long_terms = backward_bucket(long_d.reshape(-1, width), long_kept, params)
    totals = tuple((first + second for first, second in zip(short_terms, long_terms)))
    reduced = reduce_whole(totals)
    return (
        short_out.astype(jnp.bfloat16),
        long_out.astype(jnp.bfloat16),
        short_grad,
        long_grad,
        losses,
        reduced[0],
        reduced[1],
        reduced[2],
        reduced[3],
        reduced[4],
        reduced[5],
        reduced[6],
        reduced[7],
        reduced[8],
        reduced[9],
        reduced[10],
        reduced[11],
        reduced[12],
        reduced[13],
        reduced[14],
    )


def dot(a, b, dims=NN):
    return lax.dot_general(a, b, dims, preferred_element_type=f32)


def pair_masks():
    lane = lax.broadcasted_iota(jnp.int32, (1, 128), 1)
    low = (lane < HEAD).astype(bf)
    return low, 1 - low


def gelu_parts(pre):
    bell = jnp.exp(pre * pre * -0.5)
    phi = 0.5 * (1.0 + lax.erf(pre * 0.7071067811865476))
    return pre * phi, phi + pre * (bell * 0.3989422804014327)


def norm_parts(value):
    center = value - jnp.mean(value, axis=-1, keepdims=True)
    spread = jnp.mean(center * center, axis=-1, keepdims=True)
    rstd = lax.rsqrt(spread + norm_epsilon)
    return center * rstd, rstd


def forward_kernel(
    lens_s, lens_l, pos, neg, xs_h, xl_h, cots_h, cotl_h, wq_h, wk_h, wv_h, wo_h, wi_h, wu_h,
    queries, b_query, b_value, b_out, gain_one, shift_one, b_outer, gain_two, shift_two, b_inner,
    outs_h, outl_h, qkvx_h, prob_h, ctx_h, xhat1_h, low1_h, inner_h, slope_h, d_h, rstd_o, vecs, sums, loss,
    qkvx, wqkv, wo, wi, wu, prob, ctx, first, xhat1, low1, inner, slope, d, outv, cot, keep8, quest, table, lsem, osem, gs, gr,
):
    core, chip, z, y, x = place()

    def at(zz, yy, xx):
        return zz * 4 + yy * 2 + xx

    other_core = (1 - core, chip)
    other_x = (core, at(z, y, 1 - x))
    other_y = (core, at(z, 1 - y, x))
    other_z = [(core, at((z + k) % 4, y, x)) for k in (1, 2, 3)]
    peers = [other_core, other_x, other_y] + other_z
    barrier = pltpu.get_barrier_semaphore()
    for peer in peers:
        pl.semaphore_signal(barrier, inc=1, device_id=peer, device_id_type=MESH)
    sent = []

    def hop(array, stage, first):
        if stage == 0:
            pieces = [(array.at[core, z, y, x], peer) for peer in other_z]
        elif stage == 1:
            pieces = [(array.at[core, :, y, x], other_x)]
        elif stage == 2:
            pieces = [(array.at[core, :, y], other_y)]
        else:
            pieces = [(array.at[core], other_core)]
        copies = []
        for k, (piece, peer) in enumerate(pieces):
            slot = first + (k if stage == 0 else stage + 2)
            copy = pltpu.make_async_remote_copy(
                src_ref=piece, dst_ref=piece, send_sem=gs.at[slot], recv_sem=gr.at[slot], device_id=peer,
                device_id_type=MESH,
            )
            copy.start()
            copies.append(copy)
        sent.extend(copies)
        return copies

    def arrive(copies):
        for copy in copies:
            copy.wait_recv()

    def load(src, dst, k):
        copy = pltpu.make_async_copy(src, dst, lsem.at[k])
        copy.start()
        return copy

    loads = [
        load(xs_h, qkvx.at[0:384, 2304:3072], 0),
        load(xl_h, qkvx.at[384:896, 2304:3072], 1),
        load(wq_h, wqkv.at[0], 2),
        load(wk_h, wqkv.at[1], 3),
        load(wv_h, wqkv.at[2], 4),
    ]
    stores = []

    def store(src, dst):
        copy = pltpu.make_async_copy(src, dst, osem.at[len(stores)])
        copy.start()
        stores.append(copy)

    def vec(i):
        return vecs[i:i + 1, :]

    vecs[...] = jnp.zeros_like(vecs)
    for i, item in enumerate((b_query, None, b_value, b_out, gain_one, shift_one, b_outer, gain_two, shift_two)):
        if item is not None:
            vecs[i:i + 1, :] = item[...].astype(f32).reshape(1, 768)
    for i in range(4):
        vecs[9 + i:10 + i, :] = b_inner[768 * i:768 * i + 768].astype(f32).reshape(1, 768)

    lane = lax.broadcasted_iota(jnp.int32, (1, 128), 1)

    def mark(r0, n, count):
        used = lax.broadcasted_iota(jnp.int32, (n, 128), 0) < count
        rstd_o[r0:r0 + n, :] = jnp.where(used, 1.0, 0.0)

    for i in range(6):
        mark(64 * i, 64, lens_s[i])
    for i in range(2):
        mark(384 + 256 * i, 256, lens_l[i])
    sums[...] = jnp.zeros_like(sums)
    row = lax.broadcasted_iota(jnp.int32, (16, 128), 0)
    marks = jnp.zeros((16, 128), f32)
    for i in range(4):
        digits = (pos[i] // 16, pos[i] % 16, neg[i] // 16, neg[i] % 16)
        for k in range(4):
            marks = marks + jnp.where((row == i) & (lane == k), digits[k].astype(f32), 0.0)
    gap = jnp.zeros((4, 384), f32)
    asked = queries[...].astype(f32)
    asked = jnp.concatenate([asked[:, 0:384], gap, asked[:, 384:768], gap], axis=0)
    quest[core, z, y, x] = jnp.concatenate([asked, marks], axis=1).astype(bf)
    pl.semaphore_wait(barrier, len(peers))
    moving = hop(quest, 0, 0)
    loads[0].wait()
    loads[1].wait()
    for m in range(3):
        loads[2 + m].wait()
        if m == 2:
            loads.append(load(wo_h, wo, 5))
            loads.append(load(wi_h, wi, 6))
            loads.append(load(wu_h, wu, 7))
            loads.append(load(cots_h, cot.at[0:384], 8))
            loads.append(load(cotl_h, cot.at[384:896], 9))
        if m > 0:
            arrive(moving)
            moving = hop(quest, m, 0)

        @pl.loop(0, 3)
        def _(j):
            cols = pl.ds(pl.multiple_of(j * 256, 256), 256)
            res = dot(qkvx[:, 2304:3072], wqkv[m, :, cols])
            if m != 1:
                res = res + vecs[m:m + 1, cols]
            if m == 0:
                res = res.astype(bf).astype(f32) * HEAD ** (-0.5)
            qkvx[:, pl.ds(pl.multiple_of(m * 768 + j * 256, 256), 256)] = res.astype(bf)

    store(qkvx, qkvx_h)
    low, high = pair_masks()

    ki = lax.broadcasted_iota(jnp.int32, (1, 256), 1)
    kj = lax.broadcasted_iota(jnp.int32, (128, 128), 1)
    qj = lax.broadcasted_iota(jnp.int32, (128, 128), 0)
    groups = [(384 + 256 * n, 256, ki < lens_l[n]) for n in range(2)] + [
        (
            128 * g,
            128,
            ((qj < 64) & (kj < lens_s[2 * g])) | ((qj >= 64) & (kj >= 64) & (kj - 64 < lens_s[2 * g + 1])),
        )
        for g in range(3)
    ]

    def spot(g, p):
        if g < 2:
            return pl.ds(256 * g, 256), pl.multiple_of(p * 512, 512)
        i = (g - 2) * 6 + p
        return pl.ds(pl.multiple_of(512 + 128 * (i // 12), 128), 128), pl.multiple_of((i % 12) * 256, 256)

    def piece(r0, n, p, m):
        return qkvx[pl.ds(r0, n), pl.ds(pl.multiple_of(m * 768 + p * 128, 128), 128)]

    @pl.loop(0, 6)
    def _(p):
        scores = []
        for r0, n, valid in groups:
            q = piece(r0, n, p, 0)
            k = piece(r0, n, p, 1)
            scores.append(dot(q, jnp.concatenate([k * low, k * high], axis=0), NT))
        weights = []
        for g, (r0, n, valid) in enumerate(groups):
            pair = []
            for h in range(2):
                s = jnp.where(valid, scores[g][:, h * n:h * n + n], masked_value)
                e = jnp.exp(s - jnp.max(s, axis=1, keepdims=True))
                pair.append((e * (1.0 / jnp.sum(e, axis=1, keepdims=True))).astype(bf))
            weights.append(jnp.concatenate(pair, axis=1))
        for g, (r0, n, valid) in enumerate(groups):
            rows, lane0 = spot(g, p)
            v = piece(r0, n, p, 2)
            prob[rows, pl.ds(lane0, 2 * n)] = weights[g]
            acc = dot(weights[g], jnp.concatenate([v * low, v * high], axis=0))
            ctx[pl.ds(r0, n), pl.ds(pl.multiple_of(p * 128, 128), 128)] = acc.astype(bf)

    arrive(moving)
    moving = hop(quest, 3, 0)
    store(prob, prob_h)
    store(ctx, ctx_h)
    loads[5].wait()
    loads[6].wait()
    loads[7].wait()
    starts = [64 * k for k in range(6)] + [384 + 256 * k for k in range(2)]

    def heads(ref, c0, c1):
        return jnp.concatenate([ref[r:r + 1, c0:c1].astype(f32) for r in starts] * 2, axis=0)

    mixed = heads(qkvx, 2304, 3072) + dot(heads(ctx, 0, 768).astype(bf), wo[...]) + vec(3)
    value = norm_parts(mixed)[0] * vec(4) + vec(5)
    level = jnp.concatenate([vecs[9 + i:10 + i, :] for i in range(4)], axis=1)
    act = gelu_parts(dot(value.astype(bf), wi[...]) + level)[0]
    mixed = value + dot(act.astype(bf), wu[...]) + vec(6)
    value = norm_parts(mixed)[0] * vec(7) + vec(8)
    table[core, z, y, x] = jnp.concatenate([value[0:8, 0:384], value[0:8, 384:768]], axis=0).astype(bf)
    arrive(moving)
    moving = hop(table, 0, 6)

    @pl.loop(0, 4)
    def _(i):
        rows = pl.ds(pl.multiple_of(i * 224, 32), 224)
        mixed = qkvx[rows, 2304:3072].astype(f32) + dot(ctx[rows, :], wo[...]) + vec(3)
        xhat, rstd = norm_parts(mixed)
        xhat1[rows, :] = xhat.astype(bf)
        rstd_o[rows, :] = jnp.where(lane == 0, rstd, rstd_o[rows, :])
        value = xhat * vec(4) + vec(5)
        first[rows, :] = value
        low1[rows, :] = value.astype(bf)

    store(xhat1, xhat1_h)
    store(low1, low1_h)
    def widen(j):
        cols = pl.ds(pl.multiple_of(j * 256, 256), 256)
        bias = vecs[pl.ds(9 + j // 3, 1), pl.ds(pl.multiple_of((j % 3) * 256, 256), 256)]
        pre = dot(low1[...], wi[:, cols]) + bias
        act, grad = gelu_parts(pre)
        inner[:, cols] = act.astype(bf)
        slope[:, cols] = grad.astype(bf)

    for part in range(3):
        arrive(moving)
        moving = hop(table, part + 1, 6)
        pl.loop(4 * part, 4 * part + 4)(widen)
    store(inner, inner_h)
    store(slope, slope_h)
    loads[8].wait()
    loads[9].wait()
    arrive(moving)
    d_cls = contrast_math(core * 16 + chip, quest, table, core, z, y, x, loss)

    @pl.loop(0, 4)
    def _(i):
        rows = pl.ds(pl.multiple_of(i * 224, 32), 224)
        mixed = first[rows, :] + dot(inner[rows, :], wu[...]) + vec(6)
        xhat, rstd = norm_parts(mixed)
        rstd_o[rows, :] = jnp.where(lane == 1, rstd, rstd_o[rows, :])
        outv[rows, :] = (xhat * vec(7) + vec(8)).astype(bf)
        e = cot[rows, :].astype(f32) * rstd_o[rows, 2:3]
        eg = e * vec(7)
        value = (eg - jnp.mean(eg, axis=1, keepdims=True) - xhat * jnp.mean(eg * xhat, axis=1, keepdims=True)) * rstd
        d[rows, :] = value
        sums[6:7, :] += jnp.sum(e * xhat, axis=0, keepdims=True)
        sums[7:8, :] += jnp.sum(e, axis=0, keepdims=True)
        sums[5:6, :] += jnp.sum(value, axis=0, keepdims=True)
        for k, r in enumerate(starts):

            @pl.when((r >= i * 224) & (r < i * 224 + 224))
            def _():
                keep8[k:k + 1, :] = xhat[r % 224:r % 224 + 1, :]

    store(outv.at[0:384], outs_h)
    store(outv.at[384:896], outl_h)
    xh = keep8[...]
    eg = d_cls * vec(7)
    extra = eg - jnp.mean(eg, axis=1, keepdims=True) - xh * jnp.mean(eg * xh, axis=1, keepdims=True)
    extra = extra * jnp.concatenate([rstd_o[r:r + 1, 1:2] for r in starts], axis=0)
    sums[6:7, :] += jnp.sum(d_cls * xh, axis=0, keepdims=True)
    sums[7:8, :] += jnp.sum(d_cls, axis=0, keepdims=True)
    sums[5:6, :] += jnp.sum(extra, axis=0, keepdims=True)
    for i, r in enumerate(starts):
        d[r:r + 1, :] += extra[i:i + 1, :]
    store(d, d_h)
    for copy in sent:
        copy.wait_send()
    for copy in stores:
        copy.wait()


def forward(
    short_tokens, long_tokens, short_lengths, long_lengths, short_cotangent, long_cotangent, positives, hard_negatives,
    weights, small,
):
    any_ = pl.BlockSpec(memory_space=pl.ANY)
    vmem = pl.BlockSpec(memory_space=pltpu.VMEM)
    smem = pl.BlockSpec(memory_space=pltpu.SMEM)
    sds = jax.ShapeDtypeStruct
    outs = (
        sds((384, 768), bf), sds((512, 768), bf), sds((896, 3072), bf), sds((768, 3072), bf),
        sds((896, 768), bf), sds((896, 768), bf), sds((896, 768), bf),
        sds((896, 3072), bf), sds((896, 3072), bf), sds((896, 768), f32), sds((896, 128), f32),
        sds((16, 768), f32), sds((16, 768), f32), sds((8, 512), f32),
    )
    return pl.pallas_call(
        forward_kernel,
        out_shape=outs,
        in_specs=[smem] * 4 + [any_] * 10 + [vmem] * 10,
        out_specs=tuple([any_] * 10 + [vmem] * 4),
        scratch_shapes=[
            pltpu.VMEM((896, 3072), bf),
            pltpu.VMEM((3, 768, 768), bf),
            pltpu.VMEM((768, 768), bf),
            pltpu.VMEM((768, 3072), bf),
            pltpu.VMEM((3072, 768), bf),
            pltpu.VMEM((768, 3072), bf),
            pltpu.VMEM((896, 768), bf),
            pltpu.VMEM((896, 768), f32),
            pltpu.VMEM((896, 768), bf),
            pltpu.VMEM((896, 768), bf),
            pltpu.VMEM((896, 3072), bf),
            pltpu.VMEM((896, 3072), bf),
            pltpu.VMEM((896, 768), f32),
            pltpu.VMEM((896, 768), bf),
            pltpu.VMEM((896, 768), bf),
            pltpu.VMEM((8, 768), f32),
            pltpu.VMEM((2, 4, 2, 2, 16, 512), bf),
            pltpu.VMEM((2, 4, 2, 2, 16, 384), bf),
            pltpu.SemaphoreType.DMA((10,)),
            pltpu.SemaphoreType.DMA((16,)),
            pltpu.SemaphoreType.DMA((12,)),
            pltpu.SemaphoreType.DMA((12,)),
        ],
        compiler_params=pltpu.CompilerParams(
            collective_id=2, has_side_effects=True, vmem_limit_bytes=62 * 1024 * 1024
        ),
        name="forward",
    )(
        short_lengths, long_lengths, positives, hard_negatives, short_tokens.reshape(384, 768),
        long_tokens.reshape(512, 768), short_cotangent.reshape(384, 768), long_cotangent.reshape(512, 768),
        *weights, *small,
    )


def place():
    core = lax.axis_index("grp")
    chip = lax.axis_index("blk")
    return core, chip, chip // 4, (chip // 2) % 2, chip % 2


PLAN = (
    ("outer", 0), ("outer", 1), ("h1", 0), ("outer", 2), ("h1", 1), ("outer", 3), ("h1", 2), ("pre", 0), ("h1", 3),
    ("pre", 1), ("pre", 2), ("h2", 0), ("pre", 3), ("h2", 1), ("unit", 4), ("unit", 5), ("h1", 4), ("unit", 6),
    ("h1", 5), ("unit", 7), ("h2", 2), ("h2", 3), ("cols", 0), ("h1", 6), ("h1", 7), ("cols", 1), ("h3", 0), ("cols", 2), ("h2", 4),
    ("norm", 0), ("unit", 8), ("h2", 5), ("context", 0), ("h1", 8), ("attend", 0), ("h4", 0), ("h2", 6),
    ("attend", 1), ("h2", 7), ("h3", 4), ("attend", 2), ("h3", 5), ("unit", 9), ("h2", 8), ("unit", 10), ("h1", 9),
    ("unit", 11), ("h1", 10), ("h4", 4), ("h4", 5), ("h3", 6), ("vector", 0), ("drow", 0), ("h1", 11), ("h3", 7),
    ("drow", 1), ("vector", 1), ("h4", 6), ("h2", 9), ("h3", 8), ("drow", 2), ("h4", 7), ("h2", 10), ("vector", 2),
    ("h2", 11), ("h3", 9), ("h4", 8), ("h3", 10), ("h3", 11), ("vector", 3), ("h4", 9), ("h4", 10), ("h4", 11),
)


def backward_kernel(
    vecs, rstd, sums_in, d_h, qkvx_h, prob_h, ctx_h, xhat1_h, low1_h, inner_h, slope_h,
    wq_h, wk_h, wv_h, wo_h, wi_h, wu_h,
    drows_h, fin_h, sums_o,
    bufa, bufb, w1, w2, low1, xhat1, ctx, d, dlow, fin, sums, vr,
    both, came, one, two, three, three_o,
    lsem, osem, cs, cr, s1, q1, s2, q2, s3, q3, s4, q4, vs, vq,
):
    core, chip, z, y, x = place()

    def at(zz, yy, xx):
        return zz * 4 + yy * 2 + xx

    other_core = (1 - core, chip)
    other_x = (core, at(z, y, 1 - x))
    other_y = (core, at(z, 1 - y, x))
    other_z = [(core, at((z + k) % 4, y, x)) for k in (1, 2, 3)]
    peers = [other_core, other_x, other_y] + other_z
    barrier = pltpu.get_barrier_semaphore()
    for peer in peers:
        pl.semaphore_signal(barrier, inc=1, device_id=peer, device_id_type=MESH)

    loads = {}
    sent = []
    got = {}

    def load(name, *pairs):
        copies = []
        for src, dst in pairs:
            copy = pltpu.make_async_copy(src, dst, lsem.at[sum(len(c) for c in loads.values()) + len(copies)])
            copy.start()
            copies.append(copy)
        loads[name] = copies

    def ready(name):
        for copy in loads[name]:
            copy.wait()

    def remote(src, dst, send, recv, peer, late=True):
        copy = pltpu.make_async_remote_copy(
            src_ref=src, dst_ref=dst, send_sem=send, recv_sem=recv, device_id=peer, device_id_type=MESH
        )
        copy.start()
        if late:
            sent.append(copy)
        return copy

    load("d", (d_h, d))
    load("inner", (inner_h, bufa))
    sums[...] = sums_in[...]

    def add_sum(i, value):
        sums[i:i + 1, :] += jnp.sum(value, axis=0, keepdims=True)

    ready("d")
    load("wu", (wu_h, w1))
    load("slope", (slope_h, bufb))
    load("low1", (low1_h, low1))
    load("wi", (wi_h, w2))
    load("xhat1", (xhat1_h, xhat1))
    load("ctx", (ctx_h, ctx))
    dlow[...] = d[...].astype(bf)
    pl.semaphore_wait(barrier, len(peers))

    def plus(a, b):
        return (a.astype(f32) + b.astype(f32)).astype(bf)

    def cross(u):
        got["c", u] = remote(both.at[u, 1 - core], came.at[u % 8], cs.at[u], cr.at[u], other_core)

    def h1(u):
        got["c", u].wait_recv()
        mine = both.at[u, core]
        for a in range(4):
            mine[a] = plus(mine[a], came[u % 8, a])
        if u % 2 == 0:
            got["1", u] = remote(mine.at[:, :, 1 - x], one.at[u], s1.at[u], q1.at[u], other_x)
        else:
            got["1", u] = remote(mine.at[:, 1 - y], one.at[u], s1.at[u], q1.at[u], other_y)

    def h2(u):
        got["1", u].wait_recv()
        mine = both.at[u, core]
        even = u % 2 == 0
        for a in range(4):
            for b in range(2):
                if even:
                    mine[a, b, x] = plus(mine[a, b, x], one[u, a, b])
                else:
                    mine[a, y, b] = plus(mine[a, y, b], one[u, a, b])
        if even:
            got["2", u] = remote(mine.at[:, 1 - y, x], two.at[u], s2.at[u], q2.at[u], other_y)
        else:
            got["2", u] = remote(mine.at[:, y, 1 - x], two.at[u], s2.at[u], q2.at[u], other_x)

    def h3(u):
        for v in range(4) if u < 4 else (u,):
            got["2", v].wait_recv()
            for a in range(4):
                both[v, core, a, y, x] = plus(both[v, core, a, y, x], two[v, a])
        for k in range(3):
            to = (z + k + 1) % 4
            if u < 4:
                got["3", u, k] = remote(both.at[to, core, :, y, x], three_o.at[k], s3.at[0, k], q3.at[0, k], other_z[k])
            else:
                got["3", u, k] = remote(
                    both.at[u, core, to, y, x], three.at[u - 4, k], s3.at[u - 3, k], q3.at[u - 3, k], other_z[k]
                )

    cols = pl.ds(pl.multiple_of(core * 384, 128), 384)

    def h4(u):
        for k in range(3):
            got["3", u, k].wait_recv()
        for v in range(4) if u < 4 else (u,):
            if u < 4:
                total = both[z, core, v, y, x].astype(f32)
                for k in range(3):
                    total = total + three_o[k, v].astype(f32)
            else:
                total = both[u, core, z, y, x].astype(f32)
                for k in range(3):
                    total = total + three[u - 4, k].astype(f32)
            fin[v, :, cols] = total
            got["4", v] = remote(fin.at[v, :, cols], fin.at[v, :, cols], s4.at[v], q4.at[v], other_core)

    def outer(u):
        if u == 0:
            ready("inner")
        for a in range(2):
            res = dot(bufa[:, 768 * u + 384 * a:768 * u + 384 * a + 384], dlow[...], TN).astype(bf)
            for h in range(2):
                for b in range(8):
                    both[u, h, b % 4, a, b // 4] = res[48 * b:48 * b + 48, 384 * h:384 * h + 384]
        cross(u)
        if u == 3:
            load("qkvx", (qkvx_h, bufa))
            ready("wu")
            ready("slope")

    def unit(u):
        if u == 4:
            ready("low1")
        if u == 8:
            ready("ctx")
        if u < 8:
            left, right = low1, bufb.at[:, 768 * (u - 4):768 * (u - 4) + 768]
        elif u == 8:
            left, right = ctx, dlow
        else:
            left, right = bufa.at[:, 2304:3072], bufb.at[:, 768 * (11 - u):768 * (11 - u) + 768]
        for a in range(2):
            res = dot(left[:, 384 * a:384 * a + 384], right[...], TN).astype(bf)
            for h in range(2):
                for b in range(8):
                    both[u, h, 2 * a + b // 4, (b // 2) % 2, b % 2] = res[48 * b:48 * b + 48, 384 * h:384 * h + 384]
        cross(u)

    def pre(g):
        @pl.loop(0, 3)
        def _(j):
            lanes = pl.ds(pl.multiple_of(768 * g + j * 256, 256), 256)
            back = dot(dlow[...], w1[lanes, :], NT) * bufb[:, lanes].astype(f32)
            bufb[:, lanes] = back.astype(bf)
            sums[8 + g:9 + g, pl.ds(pl.multiple_of(j * 256, 256), 256)] = jnp.sum(back, axis=0, keepdims=True)

        if g == 3:
            load(
                "w1", (wq_h, w1.at[0:768]), (wk_h, w1.at[768:1536]), (wv_h, w1.at[1536:2304]),
                (wo_h, w1.at[2304:3072]),
            )

    def first_cols(j):
        if j == 0:
            ready("wi")
        lanes = pl.ds(256 * j, 256)
        d[:, lanes] += dot(bufb[...], w2[lanes, :], NT)
        if j == 2:
            load("prob", (prob_h, w2))
            ready("xhat1")

    def norm_one(_):
        @pl.loop(0, 7)
        def _(i):
            rows = pl.ds(pl.multiple_of(i * 128, 128), 128)
            e = d[rows, :]
            xh = xhat1[rows, :].astype(f32)
            eg = e * vecs[4:5, :]
            add_sum(3, e * xh)
            add_sum(4, e)
            value = (
                eg - jnp.mean(eg, axis=1, keepdims=True) - xh * jnp.mean(eg * xh, axis=1, keepdims=True)
            ) * rstd[rows, 0:1]
            add_sum(2, value)
            d[rows, :] = value
            dlow[rows, :] = value.astype(bf)

    def context(_):
        ready("w1")

        @pl.loop(0, 3)
        def _(j):
            lanes = pl.ds(pl.multiple_of(j * 256, 256), 256)
            low1[:, lanes] = dot(dlow[...], w1[pl.ds(pl.multiple_of(2304 + j * 256, 256), 256), :], NT).astype(bf)

        ready("prob")
        ready("qkvx")

    low, high = pair_masks()
    groups = [(384 + 256 * n, 256) for n in range(2)] + [(128 * g, 128) for g in range(3)]

    def spot(g, p):
        if g < 2:
            return pl.ds(256 * g, 256), pl.ds(pl.multiple_of(p * 512, 512), 512)
        i = (g - 2) * 6 + p
        return pl.ds(pl.multiple_of(512 + 128 * (i // 12), 128), 128), pl.ds(pl.multiple_of((i % 12) * 256, 256), 256)

    def stack(value):
        return jnp.concatenate([value * low, value * high], axis=0)

    def fold(value, n):
        return jnp.concatenate([value[:, :n], value[:, n:]], axis=0)

    def attend(part):
        @pl.loop(2 * part, 2 * part + 2)
        def _(p):
            def lanes(m):
                return pl.ds(pl.multiple_of(m * 768 + p * 128, 128), 128)

            slopes = []
            for r0, n in groups:
                rows = pl.ds(r0, n)
                slopes.append(dot(low1[rows, lanes(0)], stack(bufa[rows, lanes(2)]), NT))
            probs = []
            scores = []
            for g, (r0, n) in enumerate(groups):
                prob = w2[spot(g, p)]
                parts = []
                for h in range(2):
                    pf = prob[:, h * n:h * n + n].astype(f32)
                    dp = slopes[g][:, h * n:h * n + n]
                    parts.append((pf * (dp - jnp.sum(pf * dp, axis=1, keepdims=True))).astype(bf))
                probs.append(prob)
                scores.append(jnp.concatenate(parts, axis=1))
            total_q = total_v = 0.0
            for g, (r0, n) in enumerate(groups):
                rows = pl.ds(r0, n)
                dq = dot(scores[g], stack(bufa[rows, lanes(1)])) * HEAD ** (-0.5)
                dk = dot(fold(scores[g], n), stack(bufa[rows, lanes(0)]), TN)
                dv = dot(fold(probs[g], n), stack(low1[rows, lanes(0)]), TN)
                bufb[rows, lanes(0)] = dq.astype(bf)
                bufb[rows, lanes(1)] = dk.astype(bf)
                bufb[rows, lanes(2)] = dv.astype(bf)
                total_q = total_q + jnp.sum(dq, axis=0, keepdims=True)
                total_v = total_v + jnp.sum(dv, axis=0, keepdims=True)
            sums[0:1, lanes(0)] = total_q
            sums[1:2, lanes(0)] = total_v

    def drow(j):
        total = d[:, 256 * j:256 * j + 256]
        for m in range(3):
            total = total + dot(bufb[:, 768 * m:768 * m + 768], w1[768 * m + 256 * j:768 * m + 256 * j + 256, :], NT)
        d[:, 256 * j:256 * j + 256] = total
        if j == 2:
            got["out"] = pltpu.make_async_copy(d, drows_h, osem.at[0])
            got["out"].start()

    def vector(i):
        if i > 0:
            got["v", i - 1].wait()
            sums[...] += vr[i - 1]
        if i < 3:
            got["v", i] = remote(sums, vr.at[i], vs.at[i], vq.at[i], (other_core, other_x, other_y)[i], False)
        else:
            for k in range(3):
                got["w", k] = remote(sums, vr.at[3 + k], vs.at[3 + k], vq.at[3 + k], other_z[k])

    steps = {
        "outer": outer, "pre": pre, "unit": unit, "cols": first_cols, "norm": norm_one, "context": context,
        "attend": attend, "drow": drow, "h1": h1, "h2": h2, "h3": h3, "h4": h4, "vector": vector,
    }
    for name, i in PLAN:
        steps[name](i)
    for k in range(3):
        got["w", k].wait_recv()
    sums_o[...] = sums[...] + vr[3] + vr[4] + vr[5]
    for u in range(12):
        got["4", u].wait_recv()
    final = pltpu.make_async_copy(fin, fin_h, osem.at[1])
    final.start()
    for copy in sent:
        copy.wait_send()
    got["out"].wait()
    final.wait()


def contrast_math(me, quest, table, core, z, y, x, loss):
    rows = 512
    scale = 768 ** (-0.5)
    asked = quest[...].reshape(rows, 512)
    digits = asked[:, 384:512]
    asked = asked[:, 0:384]
    pick = (
        lax.broadcasted_iota(jnp.int32, (16, 128), 0) == lax.broadcasted_iota(jnp.int32, (16, 128), 1)
    ).astype(bf)
    ids = dot(pick, digits, NT)
    positive = ids[0:1] * 16.0 + ids[1:2]
    negative = ids[2:3] * 16.0 + ids[3:4]

    def join(value):
        pairs = value.reshape(value.shape[0] // 16, 2, 8, rows)
        left = pairs[:, 0].reshape(-1, rows)
        right = pairs[:, 1].reshape(-1, rows)
        return (left + pltpu.roll(right, rows - 8, 1)) * scale

    match = join(dot(table[...].reshape(rows, 384), asked, NT))
    number = lax.broadcasted_iota(jnp.int32, (256, 1), 0).astype(f32)
    top = jnp.max(match, axis=0, keepdims=True)
    lse = jnp.log(jnp.sum(jnp.exp(match - top), axis=0, keepdims=True)) + top
    pos_score = jnp.sum(jnp.where(number == positive, match, 0.0), axis=0, keepdims=True)
    neg_score = jnp.sum(jnp.where(number == negative, match, 0.0), axis=0, keepdims=True)
    gap = neg_score - pos_score
    tail = jnp.exp(-jnp.abs(gap))
    softplus = jnp.maximum(gap, 0.0) + jnp.log1p(tail)
    loss[...] = jnp.broadcast_to(lse - pos_score + softplus, loss.shape)
    sig = jnp.where(gap >= 0, 1.0, tail) / (1.0 + tail)
    own = join(dot(table[core, z, y, x], asked, NT))
    own_number = (me * 8 + lax.broadcasted_iota(jnp.int32, (8, 1), 0)).astype(f32)
    used = lax.broadcasted_iota(jnp.int32, (1, rows), 1) % 16 < 4
    coef = jnp.exp(jnp.where(used, own - lse, -1e30))
    coef = coef - jnp.where(own_number == positive, 1.0 + sig, 0.0) + jnp.where(own_number == negative, sig, 0.0)
    coef = jnp.where(used, contrast_weight * coef, 0.0)
    coef = jnp.concatenate([coef, pltpu.roll(coef, 8, 1)], axis=0)
    total = jnp.zeros((16, 384), f32)
    for _ in range(3):
        part = coef.astype(bf)
        total = total + dot(part, asked)
        coef = coef - part.astype(f32)
    return jnp.concatenate([total[0:8], total[8:16]], axis=1) * scale


def backward(vecs, rstd, sums, *arrays):
    any_ = pl.BlockSpec(memory_space=pl.ANY)
    vmem = pl.BlockSpec(memory_space=pltpu.VMEM)
    sds = jax.ShapeDtypeStruct
    dma = pltpu.SemaphoreType.DMA
    mem = pltpu.VMEM
    return pl.pallas_call(
        backward_kernel,
        out_shape=(sds((896, 768), f32), sds((12, 48, 768), f32), sds((16, 768), f32)),
        in_specs=[vmem] * 3 + [any_] * 14,
        out_specs=(any_, any_, vmem),
        scratch_shapes=[
            mem((896, 3072), bf), mem((896, 3072), bf), mem((3072, 768), bf), mem((768, 3072), bf),
            mem((896, 768), bf), mem((896, 768), bf), mem((896, 768), bf),
            mem((896, 768), f32), mem((896, 768), bf), mem((12, 48, 768), f32), mem((16, 768), f32),
            mem((6, 16, 768), f32),
            mem((12, 2, 4, 2, 2, 48, 384), bf), mem((8, 4, 2, 2, 48, 384), bf), mem((12, 4, 2, 48, 384), bf),
            mem((12, 4, 48, 384), bf), mem((8, 3, 48, 384), bf), mem((3, 4, 48, 384), bf),
            dma((20,)), dma((2,)),
            dma((12,)), dma((12,)), dma((12,)), dma((12,)), dma((12,)), dma((12,)),
            dma((9, 3)), dma((9, 3)), dma((12,)), dma((12,)), dma((6,)), dma((6,)),
        ],
        compiler_params=pltpu.CompilerParams(
            collective_id=1, has_side_effects=True, vmem_limit_bytes=64 * 1024 * 1024 - 65536
        ),
        name="backward",
    )(vecs, rstd, sums, *arrays)


def finish_kernel(
    drows, fin, sums, loss,
    o_short, o_long, o_loss, o_wq, o_bq, o_wk, o_wv, o_bv, o_wo, o_bo, o_g1, o_s1, o_wi, o_bi, o_wu, o_bu, o_g2, o_s2,
    sem,
):
    core, chip, z, y, x = place()
    copies = []

    def move(src, dst):
        copy = pltpu.make_async_copy(src, dst, sem.at[len(copies)])
        copy.start()
        copies.append(copy)

    move(drows.at[0:384], o_short)
    move(drows.at[384:896], o_long)
    for u in range(4):
        move(fin.at[u], o_wu.at[48 * u:48 * u + 48])
        move(fin.at[4 + u], o_wi.at[:, 768 * u:768 * u + 768])
    for u, dst in enumerate((o_wo, o_wv, o_wk, o_wq)):
        move(fin.at[8 + u], dst)
    small = pltpu.roll(sums[0:8, :], (768 - 48 * chip) % 768, 1)
    for i, dst in enumerate((o_bq, o_bv, o_bo, o_g1, o_s1, o_bu, o_g2, o_s2)):
        dst[...] = small[i, 0:48]
    wide = pltpu.roll(sums[pl.ds(8 + z, 1), :], (768 - 192 * (chip % 4)) % 768, 1)
    o_bi[...] = wide[0, 0:192]
    mine = pltpu.roll(loss[...], (512 - 16 * (core * 16 + chip)) % 512, 1)
    o_loss[...] = mine[0, 0:4]
    for copy in copies:
        copy.wait()


def finish(drows, fin, sums, loss):
    any_ = pl.BlockSpec(memory_space=pl.ANY)
    vmem = pl.BlockSpec(memory_space=pltpu.VMEM)
    sds = jax.ShapeDtypeStruct
    square = (sds((48, 768), f32), any_)
    line = (sds((48,), f32), vmem)
    outs = [
        (sds((384, 768), f32), any_), (sds((512, 768), f32), any_), (sds((4,), f32), vmem),
        square, line, square, square, line, square, line, line, line,
        (sds((48, 3072), f32), any_), (sds((192,), f32), vmem), (sds((192, 768), f32), any_), line, line, line,
    ]
    return pl.pallas_call(
        finish_kernel,
        out_shape=tuple(item[0] for item in outs),
        in_specs=[vmem] * 4,
        out_specs=tuple(item[1] for item in outs),
        scratch_shapes=[pltpu.SemaphoreType.DMA((14,))],
        compiler_params=pltpu.CompilerParams(vmem_limit_bytes=16 * 1024 * 1024),
        name="finish",
    )(drows, fin, sums, loss)


def fast_body(
    short_tokens, long_tokens, short_lengths, long_lengths, short_cotangent, long_cotangent, queries, positives,
    hard_negatives, w_query, b_query, w_key, w_value, b_value, w_out, b_out, gain_one, shift_one, w_inner, b_inner,
    w_outer, b_outer, gain_two, shift_two,
):
    weights = (w_query, w_key, w_value, w_out, w_inner, w_outer)
    small = (queries, b_query, b_value, b_out, gain_one, shift_one, b_outer, gain_two, shift_two, b_inner)
    (
        out_short, out_long, qkvx, prob, ctx, xhat1, low1, inner, slope, d, rstd, vecs, sums, loss,
    ) = forward(
        short_tokens, long_tokens, short_lengths, long_lengths, short_cotangent, long_cotangent, positives,
        hard_negatives, weights, small,
    )
    drows, fin, sums = backward(
        vecs, rstd, sums, d, qkvx, prob, ctx, xhat1, low1, inner, slope, *weights,
    )
    (
        d_short, d_long, losses, g_wq, g_bq, g_wk, g_wv, g_bv, g_wo, g_bo, g_g1, g_s1, g_wi, g_bi, g_wu, g_bu, g_g2,
        g_s2,
    ) = finish(drows, fin, sums, loss)
    return (
        out_short.reshape(short_tokens.shape), out_long.reshape(long_tokens.shape),
        d_short.reshape(short_tokens.shape), d_long.reshape(long_tokens.shape),
        losses, g_wq, g_bq, g_wk, g_wv, g_bv, g_wo, g_bo, g_g1, g_s1, g_wi, g_bi, g_wu, g_bu, g_g2, g_s2,
    )


def solution(mesh):
    fast = mesh.shape["grp"] == 2 and mesh.shape["blk"] == 16
    in_specs = (
        P(("grp", "blk"), None, None),
        P(("grp", "blk"), None, None),
        P(("grp", "blk")),
        P(("grp", "blk")),
        P(("grp", "blk"), None, None),
        P(("grp", "blk"), None, None),
        P(("grp", "blk"), None),
        P(("grp", "blk")),
        P(("grp", "blk")),
        P(),
        P(),
        P(),
        P(),
        P(),
        P(),
        P(),
        P(),
        P(),
        P(),
        P(),
        P(),
        P(),
        P(),
        P(),
    )
    out_specs = (
        P(("grp", "blk"), None, None),
        P(("grp", "blk"), None, None),
        P(("grp", "blk"), None, None),
        P(("grp", "blk"), None, None),
        P(("grp", "blk")),
        P("blk", None),
        P("blk"),
        P("blk", None),
        P("blk", None),
        P("blk"),
        P("blk", None),
        P("blk"),
        P("blk"),
        P("blk"),
        P("blk", None),
        P("blk"),
        P("blk", None),
        P("blk"),
        P("blk"),
        P("blk"),
    )
    return jax.shard_map(fast_body if fast else body, mesh=mesh, in_specs=in_specs, out_specs=out_specs, check_vma=False)
```

```python
import jax
import jax.numpy as jnp
from jax import lax
from jax.experimental import pallas as pl
from jax.experimental.pallas import tpu as pltpu
from jax.sharding import PartitionSpec as P

HEADS = 12
HEAD = 64


norm_epsilon = 1e-05
contrast_weight = 8.0
masked_value = -1000000000.0
bf = jnp.bfloat16
f32 = jnp.float32
NT = (((1,), (1,)), ((), ()))
TN = (((0,), (0,)), ((), ()))
NN = (((1,), (0,)), ((), ()))
MESH = pl.DeviceIdType.MESH


def layer_norm(value, gain, shift):
    center = value - jnp.mean(value, axis=-1, keepdims=True)
    spread = jnp.mean(center * center, axis=-1, keepdims=True)
    return center * lax.rsqrt(spread + norm_epsilon) * gain + shift


def exact_gelu(value):
    return jax.nn.gelu(value, approximate=False)


def split_heads(value, count, seq):
    return value.reshape(count, seq, HEADS, HEAD)


def attention_scores(query, keys, valid):
    scores = jnp.einsum(
        "nqhd,nkhd->nhqk", query, keys, preferred_element_type=jnp.float32
    ) * HEAD ** (-0.5)
    return jnp.where(valid[:, None, None, :], scores, masked_value)


def forward_bucket(tokens, lengths, params):
    (
        w_query,
        b_query,
        w_key,
        w_value,
        b_value,
        w_out,
        b_out,
        gain_one,
        shift_one,
        w_inner,
        b_inner,
        w_outer,
        b_outer,
        gain_two,
        shift_two,
    ) = params
    count, seq, width = tokens.shape
    rows = tokens.reshape(count * seq, width)
    query = (jnp.dot(rows, w_query, preferred_element_type=jnp.float32) + b_query).astype(
        jnp.bfloat16
    )
    keys = jnp.dot(rows, w_key, preferred_element_type=jnp.float32).astype(jnp.bfloat16)
    values = (jnp.dot(rows, w_value, preferred_element_type=jnp.float32) + b_value).astype(
        jnp.bfloat16
    )
    valid = lax.broadcasted_iota(jnp.int32, (count, seq), 1) < lengths[:, None]
    scores = attention_scores(split_heads(query, count, seq), split_heads(keys, count, seq), valid)
    top = jnp.max(scores, axis=-1, keepdims=True)
    expo = jnp.exp(scores - top)
    total = jnp.sum(expo, axis=-1, keepdims=True)
    logsum = top + jnp.log(total)
    probs = (expo / total).astype(jnp.bfloat16)
    context = (
        jnp.einsum(
            "nhqk,nkhd->nqhd",
            probs,
            split_heads(values, count, seq),
            preferred_element_type=jnp.float32,
        )
        .astype(jnp.bfloat16)
        .reshape(count * seq, width)
    )
    mixed_one = rows + jnp.dot(context, w_out, preferred_element_type=jnp.float32) + b_out
    first = layer_norm(mixed_one, gain_one, shift_one)
    first_low = first.astype(jnp.bfloat16)
    pre = jnp.dot(first_low, w_inner, preferred_element_type=jnp.float32) + b_inner
    inner = exact_gelu(pre).astype(jnp.bfloat16)
    mixed_two = first + jnp.dot(inner, w_outer, preferred_element_type=jnp.float32) + b_outer
    output = layer_norm(mixed_two, gain_two, shift_two)
    kept = (
        rows,
        query,
        keys,
        values,
        valid,
        logsum,
        context,
        mixed_one,
        first_low,
        pre,
        inner,
        mixed_two,
    )
    return (output.reshape(count, seq, width), kept)


def backward_bucket(d_output, kept, params):
    (
        w_query,
        b_query,
        w_key,
        w_value,
        b_value,
        w_out,
        b_out,
        gain_one,
        shift_one,
        w_inner,
        b_inner,
        w_outer,
        b_outer,
        gain_two,
        shift_two,
    ) = params
    (
        rows,
        query,
        keys,
        values,
        valid,
        logsum,
        context,
        mixed_one,
        first_low,
        pre,
        inner,
        mixed_two,
    ) = kept
    count, seq = valid.shape
    width = rows.shape[1]
    f32 = jnp.float32
    unused, pull_two = jax.vjp(layer_norm, mixed_two, gain_two, shift_two)
    d_mixed_two, grad_gain_two, grad_shift_two = pull_two(d_output)
    d_second = d_mixed_two.astype(jnp.bfloat16)
    grad_w_outer = jnp.einsum("rf,rd->fd", inner, d_second, preferred_element_type=f32)
    grad_b_outer = jnp.sum(d_mixed_two, axis=0)
    d_inner = jnp.einsum("rd,fd->rf", d_second, w_outer, preferred_element_type=f32)
    unused, pull_gelu = jax.vjp(exact_gelu, pre)
    (d_pre,) = pull_gelu(d_inner)
    d_pre_low = d_pre.astype(jnp.bfloat16)
    grad_w_inner = jnp.einsum("rd,rf->df", first_low, d_pre_low, preferred_element_type=f32)
    grad_b_inner = jnp.sum(d_pre, axis=0)
    d_first = d_mixed_two + jnp.einsum("rf,df->rd", d_pre_low, w_inner, preferred_element_type=f32)
    unused, pull_one = jax.vjp(layer_norm, mixed_one, gain_one, shift_one)
    d_mixed_one, grad_gain_one, grad_shift_one = pull_one(d_first)
    d_attended = d_mixed_one.astype(jnp.bfloat16)
    grad_w_out = jnp.einsum("rd,re->de", context, d_attended, preferred_element_type=f32)
    grad_b_out = jnp.sum(d_mixed_one, axis=0)
    d_context = jnp.einsum("re,de->rd", d_attended, w_out, preferred_element_type=f32).astype(
        jnp.bfloat16
    )
    query_heads = split_heads(query, count, seq)
    key_heads = split_heads(keys, count, seq)
    value_heads = split_heads(values, count, seq)
    context_heads = split_heads(d_context, count, seq)
    probs = jnp.exp(attention_scores(query_heads, key_heads, valid) - logsum)
    d_probs = jnp.einsum("nqhd,nkhd->nhqk", context_heads, value_heads, preferred_element_type=f32)
    d_values = jnp.einsum(
        "nhqk,nqhd->nkhd", probs.astype(jnp.bfloat16), context_heads, preferred_element_type=f32
    ).reshape(count * seq, width)
    d_scores = (probs * (d_probs - jnp.sum(probs * d_probs, axis=-1, keepdims=True))).astype(
        jnp.bfloat16
    )
    d_query = jnp.einsum(
        "nhqk,nkhd->nqhd", d_scores, key_heads, preferred_element_type=f32
    ).reshape(count * seq, width) * HEAD ** (-0.5)
    d_keys = jnp.einsum(
        "nhqk,nqhd->nkhd", d_scores, query_heads, preferred_element_type=f32
    ).reshape(count * seq, width) * HEAD ** (-0.5)
    grad_b_query = jnp.sum(d_query, axis=0)
    grad_b_value = jnp.sum(d_values, axis=0)
    query_low = d_query.astype(jnp.bfloat16)
    keys_low = d_keys.astype(jnp.bfloat16)
    values_low = d_values.astype(jnp.bfloat16)
    grad_w_query = jnp.einsum("rd,re->de", rows, query_low, preferred_element_type=f32)
    grad_w_key = jnp.einsum("rd,re->de", rows, keys_low, preferred_element_type=f32)
    grad_w_value = jnp.einsum("rd,re->de", rows, values_low, preferred_element_type=f32)
    d_rows = d_mixed_one + jnp.einsum("re,de->rd", query_low, w_query, preferred_element_type=f32)
    d_rows = d_rows + jnp.einsum("re,de->rd", keys_low, w_key, preferred_element_type=f32)
    d_rows = d_rows + jnp.einsum("re,de->rd", values_low, w_value, preferred_element_type=f32)
    grads = (
        grad_w_query,
        grad_b_query,
        grad_w_key,
        grad_w_value,
        grad_b_value,
        grad_w_out,
        grad_b_out,
        grad_gain_one,
        grad_shift_one,
        grad_w_inner,
        grad_b_inner,
        grad_w_outer,
        grad_b_outer,
        grad_gain_two,
        grad_shift_two,
    )
    return (d_rows.reshape(count, seq, width), grads)


def contrast_whole(cls_low, queries, positives, hard_negatives, scale):
    f32 = jnp.float32
    passage_count = cls_low.shape[0]
    query_count = queries.shape[0]
    me = lax.axis_index(("grp", "blk"))
    own_ids = me * passage_count + lax.broadcasted_iota(jnp.int32, (passage_count,), 0)
    start_top = jnp.full((query_count,), -1e30, f32)
    piece = lax.all_gather(cls_low, ("grp", "blk"), axis=0, tiled=True)
    top = start_top
    scores = jnp.einsum("qd,pd->qp", queries, piece, preferred_element_type=f32) * scale
    ids = lax.broadcasted_iota(jnp.int32, (1, piece.shape[0]), 1)
    new_top = jnp.maximum(top, jnp.max(scores, axis=1))
    total = jnp.sum(jnp.exp(scores - new_top[:, None]), axis=1)
    pos_score = jnp.sum(jnp.where(ids == positives[:, None], scores, 0.0), axis=1)
    neg_score = jnp.sum(jnp.where(ids == hard_negatives[:, None], scores, 0.0), axis=1)
    top, total, pos_score, neg_score = (new_top, total, pos_score, neg_score)
    logsum = top + jnp.log(total)
    losses = logsum - pos_score + jax.nn.softplus(neg_score - pos_score)
    sigma = jax.nn.sigmoid(neg_score - pos_score)
    coef_pos = contrast_weight * (1.0 + sigma)
    coef_neg = contrast_weight * sigma
    query_piece = lax.all_gather(queries.astype(f32), ("grp", "blk"), axis=0, tiled=True)
    lse_piece = lax.all_gather(logsum, ("grp", "blk"), axis=0, tiled=True)
    pos_coef = lax.all_gather(coef_pos, ("grp", "blk"), axis=0, tiled=True)
    neg_coef = lax.all_gather(coef_neg, ("grp", "blk"), axis=0, tiled=True)
    pos_piece = lax.all_gather(positives, ("grp", "blk"), axis=0, tiled=True)
    neg_piece = lax.all_gather(hard_negatives, ("grp", "blk"), axis=0, tiled=True)
    scores = (
        jnp.einsum(
            "pd,qd->pq", cls_low, query_piece.astype(jnp.bfloat16), preferred_element_type=f32
        )
        * scale
    )
    weight = contrast_weight * jnp.exp(scores - lse_piece[None, :])
    weight = weight - jnp.where(own_ids[:, None] == pos_piece[None, :], pos_coef[None, :], 0.0)
    weight = weight + jnp.where(own_ids[:, None] == neg_piece[None, :], neg_coef[None, :], 0.0)
    d_cls = (
        jnp.dot(weight, query_piece, precision=lax.Precision.HIGHEST, preferred_element_type=f32)
        * scale
    )
    return losses, d_cls


def reduce_whole(totals):
    reduced = (
        lax.psum_scatter(totals[0], "blk", scatter_dimension=0, tiled=True),
        lax.psum_scatter(totals[1], "blk", scatter_dimension=0, tiled=True),
        lax.psum_scatter(totals[2], "blk", scatter_dimension=0, tiled=True),
        lax.psum_scatter(totals[3], "blk", scatter_dimension=0, tiled=True),
        lax.psum_scatter(totals[4], "blk", scatter_dimension=0, tiled=True),
        lax.psum_scatter(totals[5], "blk", scatter_dimension=0, tiled=True),
        lax.psum_scatter(totals[6], "blk", scatter_dimension=0, tiled=True),
        lax.psum_scatter(totals[7], "blk", scatter_dimension=0, tiled=True),
        lax.psum_scatter(totals[8], "blk", scatter_dimension=0, tiled=True),
        lax.psum_scatter(totals[9], "blk", scatter_dimension=0, tiled=True),
        lax.psum_scatter(totals[10], "blk", scatter_dimension=0, tiled=True),
        lax.psum_scatter(totals[11], "blk", scatter_dimension=0, tiled=True),
        lax.psum_scatter(totals[12], "blk", scatter_dimension=0, tiled=True),
        lax.psum_scatter(totals[13], "blk", scatter_dimension=0, tiled=True),
        lax.psum_scatter(totals[14], "blk", scatter_dimension=0, tiled=True),
    )
    reduced = (
        lax.psum(reduced[0].astype(jnp.bfloat16), "grp").astype(jnp.float32),
        lax.psum(reduced[1].astype(jnp.bfloat16), "grp").astype(jnp.float32),
        lax.psum(reduced[2].astype(jnp.bfloat16), "grp").astype(jnp.float32),
        lax.psum(reduced[3].astype(jnp.bfloat16), "grp").astype(jnp.float32),
        lax.psum(reduced[4].astype(jnp.bfloat16), "grp").astype(jnp.float32),
        lax.psum(reduced[5].astype(jnp.bfloat16), "grp").astype(jnp.float32),
        lax.psum(reduced[6].astype(jnp.bfloat16), "grp").astype(jnp.float32),
        lax.psum(reduced[7].astype(jnp.bfloat16), "grp").astype(jnp.float32),
        lax.psum(reduced[8].astype(jnp.bfloat16), "grp").astype(jnp.float32),
        lax.psum(reduced[9].astype(jnp.bfloat16), "grp").astype(jnp.float32),
        lax.psum(reduced[10].astype(jnp.bfloat16), "grp").astype(jnp.float32),
        lax.psum(reduced[11].astype(jnp.bfloat16), "grp").astype(jnp.float32),
        lax.psum(reduced[12].astype(jnp.bfloat16), "grp").astype(jnp.float32),
        lax.psum(reduced[13].astype(jnp.bfloat16), "grp").astype(jnp.float32),
        lax.psum(reduced[14].astype(jnp.bfloat16), "grp").astype(jnp.float32),
    )
    return reduced


def body(
    short_tokens,
    long_tokens,
    short_lengths,
    long_lengths,
    short_cotangent,
    long_cotangent,
    queries,
    positives,
    hard_negatives,
    w_query,
    b_query,
    w_key,
    w_value,
    b_value,
    w_out,
    b_out,
    gain_one,
    shift_one,
    w_inner,
    b_inner,
    w_outer,
    b_outer,
    gain_two,
    shift_two,
):
    f32 = jnp.float32
    params = (
        w_query,
        b_query.astype(f32),
        w_key,
        w_value,
        b_value.astype(f32),
        w_out,
        b_out.astype(f32),
        gain_one.astype(f32),
        shift_one.astype(f32),
        w_inner,
        b_inner.astype(f32),
        w_outer,
        b_outer.astype(f32),
        gain_two.astype(f32),
        shift_two.astype(f32),
    )
    short_out, short_kept = forward_bucket(short_tokens, short_lengths, params)
    long_out, long_kept = forward_bucket(long_tokens, long_lengths, params)
    short_count = short_tokens.shape[0]
    width = short_tokens.shape[2]
    scale = width ** (-0.5)
    cls_low = jnp.concatenate([short_out[:, 0, :], long_out[:, 0, :]], axis=0).astype(jnp.bfloat16)
    passage_count = cls_low.shape[0]
    query_count = queries.shape[0]
    me = lax.axis_index(("grp", "blk"))
    losses, d_cls = contrast_whole(cls_low, queries, positives, hard_negatives, scale)
    short_d = short_cotangent.astype(f32) * short_kept[4][:, :, None]
    short_d = short_d.at[:, 0, :].add(d_cls[:short_count])
    long_d = long_cotangent.astype(f32) * long_kept[4][:, :, None]
    long_d = long_d.at[:, 0, :].add(d_cls[short_count:])
    short_grad, short_terms = backward_bucket(short_d.reshape(-1, width), short_kept, params)
    long_grad, long_terms = backward_bucket(long_d.reshape(-1, width), long_kept, params)
    totals = tuple((first + second for first, second in zip(short_terms, long_terms)))
    reduced = reduce_whole(totals)
    return (
        short_out.astype(jnp.bfloat16),
        long_out.astype(jnp.bfloat16),
        short_grad,
        long_grad,
        losses,
        reduced[0],
        reduced[1],
        reduced[2],
        reduced[3],
        reduced[4],
        reduced[5],
        reduced[6],
        reduced[7],
        reduced[8],
        reduced[9],
        reduced[10],
        reduced[11],
        reduced[12],
        reduced[13],
        reduced[14],
    )


def dot(a, b, dims=NN):
    return lax.dot_general(a, b, dims, preferred_element_type=f32)


def pair_masks():
    lane = lax.broadcasted_iota(jnp.int32, (1, 128), 1)
    low = (lane < HEAD).astype(bf)
    return low, 1 - low


def gelu_parts(pre):
    bell = jnp.exp(pre * pre * -0.5)
    phi = 0.5 * (1.0 + lax.erf(pre * 0.7071067811865476))
    return pre * phi, phi + pre * (bell * 0.3989422804014327)


def norm_parts(value):
    center = value - jnp.mean(value, axis=-1, keepdims=True)
    spread = jnp.mean(center * center, axis=-1, keepdims=True)
    rstd = lax.rsqrt(spread + norm_epsilon)
    return center * rstd, rstd


def forward_kernel(
    lens_s, lens_l, pos, neg, xs_h, xl_h, cots_h, cotl_h, wq_h, wk_h, wv_h, wo_h, wi_h, wu_h,
    queries, b_query, b_value, b_out, gain_one, shift_one, b_outer, gain_two, shift_two, b_inner,
    outs_h, outl_h, qkvx_h, prob_h, ctx_h, xhat1_h, low1_h, inner_h, slope_h, d_h, rstd_o, vecs, sums, loss,
    qkvx, wqkv, wo, wi, wu, prob, ctx, first, xhat1, low1, inner, slope, d, outv, cot, keep8, quest, table, lsem, osem, gs, gr,
):
    core, chip, z, y, x = place()

    def at(zz, yy, xx):
        return zz * 4 + yy * 2 + xx

    other_core = (1 - core, chip)
    other_x = (core, at(z, y, 1 - x))
    other_y = (core, at(z, 1 - y, x))
    other_z = [(core, at((z + k) % 4, y, x)) for k in (1, 2, 3)]
    peers = [other_core, other_x, other_y] + other_z
    barrier = pltpu.get_barrier_semaphore()
    for peer in peers:
        pl.semaphore_signal(barrier, inc=1, device_id=peer, device_id_type=MESH)
    sent = []

    def hop(array, stage, first):
        if stage == 0:
            pieces = [(array.at[core, z, y, x], peer) for peer in other_z]
        elif stage == 1:
            pieces = [(array.at[core, :, y, x], other_x)]
        elif stage == 2:
            pieces = [(array.at[core, :, y], other_y)]
        else:
            pieces = [(array.at[core], other_core)]
        copies = []
        for k, (piece, peer) in enumerate(pieces):
            slot = first + (k if stage == 0 else stage + 2)
            copy = pltpu.make_async_remote_copy(
                src_ref=piece, dst_ref=piece, send_sem=gs.at[slot], recv_sem=gr.at[slot], device_id=peer,
                device_id_type=MESH,
            )
            copy.start()
            copies.append(copy)
        sent.extend(copies)
        return copies

    def arrive(copies):
        for copy in copies:
            copy.wait_recv()

    def load(src, dst, k):
        copy = pltpu.make_async_copy(src, dst, lsem.at[k])
        copy.start()
        return copy

    loads = [
        load(xs_h, qkvx.at[0:384, 2304:3072], 0),
        load(xl_h, qkvx.at[384:896, 2304:3072], 1),
        load(wq_h, wqkv.at[0], 2),
        load(wk_h, wqkv.at[1], 3),
        load(wv_h, wqkv.at[2], 4),
    ]
    stores = []

    def store(src, dst):
        copy = pltpu.make_async_copy(src, dst, osem.at[len(stores)])
        copy.start()
        stores.append(copy)

    def vec(i):
        return vecs[i:i + 1, :]

    vecs[...] = jnp.zeros_like(vecs)
    for i, item in enumerate((b_query, None, b_value, b_out, gain_one, shift_one, b_outer, gain_two, shift_two)):
        if item is not None:
            vecs[i:i + 1, :] = item[...].astype(f32).reshape(1, 768)
    for i in range(4):
        vecs[9 + i:10 + i, :] = b_inner[768 * i:768 * i + 768].astype(f32).reshape(1, 768)

    lane = lax.broadcasted_iota(jnp.int32, (1, 128), 1)

    def mark(r0, n, count):
        used = lax.broadcasted_iota(jnp.int32, (n, 128), 0) < count
        rstd_o[r0:r0 + n, :] = jnp.where(used, 1.0, 0.0)

    for i in range(6):
        mark(64 * i, 64, lens_s[i])
    for i in range(2):
        mark(384 + 256 * i, 256, lens_l[i])
    sums[...] = jnp.zeros_like(sums)
    row = lax.broadcasted_iota(jnp.int32, (16, 128), 0)
    marks = jnp.zeros((16, 128), f32)
    for i in range(4):
        digits = (pos[i] // 16, pos[i] % 16, neg[i] // 16, neg[i] % 16)
        for k in range(4):
            marks = marks + jnp.where((row == i) & (lane == k), digits[k].astype(f32), 0.0)
    gap = jnp.zeros((4, 384), f32)
    asked = queries[...].astype(f32)
    asked = jnp.concatenate([asked[:, 0:384], gap, asked[:, 384:768], gap], axis=0)
    quest[core, z, y, x] = jnp.concatenate([asked, marks], axis=1).astype(bf)
    loads[0].wait()
    loads[1].wait()
    for m in range(3):
        loads[2 + m].wait()
        if m == 2:
            loads.append(load(wo_h, wo, 5))
            loads.append(load(wi_h, wi, 6))
            loads.append(load(wu_h, wu, 7))
            loads.append(load(cots_h, cot.at[0:384], 8))
            loads.append(load(cotl_h, cot.at[384:896], 9))
        @pl.loop(0, 3)
        def _(j):
            cols = pl.ds(pl.multiple_of(j * 256, 256), 256)
            res = dot(qkvx[:, 2304:3072], wqkv[m, :, cols])
            if m != 1:
                res = res + vecs[m:m + 1, cols]
            if m == 0:
                res = res.astype(bf).astype(f32) * HEAD ** (-0.5)
            qkvx[:, pl.ds(pl.multiple_of(m * 768 + j * 256, 256), 256)] = res.astype(bf)

    store(qkvx, qkvx_h)
    low, high = pair_masks()

    ki = lax.broadcasted_iota(jnp.int32, (1, 256), 1)
    kj = lax.broadcasted_iota(jnp.int32, (128, 128), 1)
    qj = lax.broadcasted_iota(jnp.int32, (128, 128), 0)
    groups = [(384 + 256 * n, 256, ki < lens_l[n]) for n in range(2)] + [
        (
            128 * g,
            128,
            ((qj < 64) & (kj < lens_s[2 * g])) | ((qj >= 64) & (kj >= 64) & (kj - 64 < lens_s[2 * g + 1])),
        )
        for g in range(3)
    ]

    def spot(g, p):
        if g < 2:
            return pl.ds(256 * g, 256), pl.multiple_of(p * 512, 512)
        i = (g - 2) * 6 + p
        return pl.ds(pl.multiple_of(512 + 128 * (i // 12), 128), 128), pl.multiple_of((i % 12) * 256, 256)

    def piece(r0, n, p, m):
        return qkvx[pl.ds(r0, n), pl.ds(pl.multiple_of(m * 768 + p * 128, 128), 128)]

    def attend(p):
        scores = []
        for r0, n, valid in groups:
            q = piece(r0, n, p, 0)
            k = piece(r0, n, p, 1)
            scores.append(dot(q, jnp.concatenate([k * low, k * high], axis=0), NT))
        weights = []
        for g, (r0, n, valid) in enumerate(groups):
            pair = []
            for h in range(2):
                s = jnp.where(valid, scores[g][:, h * n:h * n + n], masked_value)
                e = jnp.exp(s - jnp.max(s, axis=1, keepdims=True))
                pair.append((e * (1.0 / jnp.sum(e, axis=1, keepdims=True))).astype(bf))
            weights.append(jnp.concatenate(pair, axis=1))
        for g, (r0, n, valid) in enumerate(groups):
            rows, lane0 = spot(g, p)
            v = piece(r0, n, p, 2)
            prob[rows, pl.ds(lane0, 2 * n)] = weights[g]
            acc = dot(weights[g], jnp.concatenate([v * low, v * high], axis=0))
            ctx[pl.ds(r0, n), pl.ds(pl.multiple_of(p * 128, 128), 128)] = acc.astype(bf)

    pl.semaphore_wait(barrier, len(peers))
    asking = hop(quest, 0, 0)
    pl.loop(0, 6)(attend)
    arrive(asking)
    asking = hop(quest, 1, 0)
    store(prob, prob_h)
    store(ctx, ctx_h)
    loads[5].wait()
    loads[6].wait()
    loads[7].wait()
    starts = [64 * k for k in range(6)] + [384 + 256 * k for k in range(2)]

    def heads(ref, c0, c1):
        return jnp.concatenate([ref[r:r + 1, c0:c1].astype(f32) for r in starts] * 2, axis=0)

    mixed = heads(qkvx, 2304, 3072) + dot(heads(ctx, 0, 768).astype(bf), wo[...]) + vec(3)
    value = norm_parts(mixed)[0] * vec(4) + vec(5)
    level = jnp.concatenate([vecs[9 + i:10 + i, :] for i in range(4)], axis=1)
    act = gelu_parts(dot(value.astype(bf), wi[...]) + level)[0]
    mixed = value + dot(act.astype(bf), wu[...]) + vec(6)
    value = norm_parts(mixed)[0] * vec(7) + vec(8)
    table[core, z, y, x] = jnp.concatenate([value[0:8, 0:384], value[0:8, 384:768]], axis=0).astype(bf)
    moving = hop(table, 0, 6)

    @pl.loop(0, 4)
    def _(i):
        rows = pl.ds(pl.multiple_of(i * 224, 32), 224)
        mixed = qkvx[rows, 2304:3072].astype(f32) + dot(ctx[rows, :], wo[...]) + vec(3)
        xhat, rstd = norm_parts(mixed)
        xhat1[rows, :] = xhat.astype(bf)
        rstd_o[rows, :] = jnp.where(lane == 0, rstd, rstd_o[rows, :])
        value = xhat * vec(4) + vec(5)
        first[rows, :] = value
        low1[rows, :] = value.astype(bf)

    store(xhat1, xhat1_h)
    store(low1, low1_h)
    def widen(j):
        cols = pl.ds(pl.multiple_of(j * 256, 256), 256)
        bias = vecs[pl.ds(9 + j // 3, 1), pl.ds(pl.multiple_of((j % 3) * 256, 256), 256)]
        pre = dot(low1[...], wi[:, cols]) + bias
        act, grad = gelu_parts(pre)
        inner[:, cols] = act.astype(bf)
        slope[:, cols] = grad.astype(bf)

    arrive(asking)
    asking = hop(quest, 2, 0)
    pl.loop(0, 2)(widen)
    arrive(moving)
    moving = hop(table, 1, 6)
    pl.loop(2, 5)(widen)
    arrive(asking)
    asking = hop(quest, 3, 0)
    pl.loop(5, 8)(widen)
    arrive(moving)
    moving = hop(table, 2, 6)
    pl.loop(8, 12)(widen)
    store(inner, inner_h)
    store(slope, slope_h)
    loads[8].wait()
    loads[9].wait()

    def narrow(i):
        rows = pl.ds(pl.multiple_of(i * 224, 32), 224)
        mixed = first[rows, :] + dot(inner[rows, :], wu[...]) + vec(6)
        xhat, rstd = norm_parts(mixed)
        rstd_o[rows, :] = jnp.where(lane == 1, rstd, rstd_o[rows, :])
        outv[rows, :] = (xhat * vec(7) + vec(8)).astype(bf)
        e = cot[rows, :].astype(f32) * rstd_o[rows, 2:3]
        eg = e * vec(7)
        value = (eg - jnp.mean(eg, axis=1, keepdims=True) - xhat * jnp.mean(eg * xhat, axis=1, keepdims=True)) * rstd
        d[rows, :] = value
        sums[6:7, :] += jnp.sum(e * xhat, axis=0, keepdims=True)
        sums[7:8, :] += jnp.sum(e, axis=0, keepdims=True)
        sums[5:6, :] += jnp.sum(value, axis=0, keepdims=True)
        for k, r in enumerate(starts):

            @pl.when((r >= i * 224) & (r < i * 224 + 224))
            def _():
                keep8[k:k + 1, :] = xhat[r % 224:r % 224 + 1, :]

    pl.loop(0, 2)(narrow)
    arrive(moving)
    arrive(asking)
    moving = hop(table, 3, 6)
    pl.loop(2, 4)(narrow)
    arrive(moving)
    d_cls = contrast_math(core * 16 + chip, quest, table, core, z, y, x, loss)
    store(outv.at[0:384], outs_h)
    store(outv.at[384:896], outl_h)
    xh = keep8[...]
    eg = d_cls * vec(7)
    extra = eg - jnp.mean(eg, axis=1, keepdims=True) - xh * jnp.mean(eg * xh, axis=1, keepdims=True)
    extra = extra * jnp.concatenate([rstd_o[r:r + 1, 1:2] for r in starts], axis=0)
    sums[6:7, :] += jnp.sum(d_cls * xh, axis=0, keepdims=True)
    sums[7:8, :] += jnp.sum(d_cls, axis=0, keepdims=True)
    sums[5:6, :] += jnp.sum(extra, axis=0, keepdims=True)
    for i, r in enumerate(starts):
        d[r:r + 1, :] += extra[i:i + 1, :]
    store(d, d_h)
    for copy in sent:
        copy.wait_send()
    for copy in stores:
        copy.wait()


def forward(
    short_tokens, long_tokens, short_lengths, long_lengths, short_cotangent, long_cotangent, positives, hard_negatives,
    weights, small,
):
    any_ = pl.BlockSpec(memory_space=pl.ANY)
    vmem = pl.BlockSpec(memory_space=pltpu.VMEM)
    smem = pl.BlockSpec(memory_space=pltpu.SMEM)
    sds = jax.ShapeDtypeStruct
    outs = (
        sds((384, 768), bf), sds((512, 768), bf), sds((896, 3072), bf), sds((768, 3072), bf),
        sds((896, 768), bf), sds((896, 768), bf), sds((896, 768), bf),
        sds((896, 3072), bf), sds((896, 3072), bf), sds((896, 768), f32), sds((896, 128), f32),
        sds((16, 768), f32), sds((16, 768), f32), sds((8, 512), f32),
    )
    return pl.pallas_call(
        forward_kernel,
        out_shape=outs,
        in_specs=[smem] * 4 + [any_] * 10 + [vmem] * 10,
        out_specs=tuple([any_] * 10 + [vmem] * 4),
        scratch_shapes=[
            pltpu.VMEM((896, 3072), bf),
            pltpu.VMEM((3, 768, 768), bf),
            pltpu.VMEM((768, 768), bf),
            pltpu.VMEM((768, 3072), bf),
            pltpu.VMEM((3072, 768), bf),
            pltpu.VMEM((768, 3072), bf),
            pltpu.VMEM((896, 768), bf),
            pltpu.VMEM((896, 768), f32),
            pltpu.VMEM((896, 768), bf),
            pltpu.VMEM((896, 768), bf),
            pltpu.VMEM((896, 3072), bf),
            pltpu.VMEM((896, 3072), bf),
            pltpu.VMEM((896, 768), f32),
            pltpu.VMEM((896, 768), bf),
            pltpu.VMEM((896, 768), bf),
            pltpu.VMEM((8, 768), f32),
            pltpu.VMEM((2, 4, 2, 2, 16, 512), bf),
            pltpu.VMEM((2, 4, 2, 2, 16, 384), bf),
            pltpu.SemaphoreType.DMA((10,)),
            pltpu.SemaphoreType.DMA((16,)),
            pltpu.SemaphoreType.DMA((12,)),
            pltpu.SemaphoreType.DMA((12,)),
        ],
        compiler_params=pltpu.CompilerParams(
            collective_id=2, has_side_effects=True, vmem_limit_bytes=62 * 1024 * 1024
        ),
        name="forward",
    )(
        short_lengths, long_lengths, positives, hard_negatives, short_tokens.reshape(384, 768),
        long_tokens.reshape(512, 768), short_cotangent.reshape(384, 768), long_cotangent.reshape(512, 768),
        *weights, *small,
    )


def place():
    core = lax.axis_index("grp")
    chip = lax.axis_index("blk")
    return core, chip, chip // 4, (chip // 2) % 2, chip % 2


PLAN = (
    ("outer", 0), ("outer", 1), ("h1", 0), ("outer", 2), ("h1", 1), ("outer", 3), ("fetch", 0), ("pre", 0), ("h1", 2),
    ("pre", 1), ("h1", 3), ("fetch", 1), ("pre", 2), ("pre", 3), ("rows", 0), ("unit", 4), ("h2", 0), ("h2", 1),
    ("rows", 1), ("h1", 4), ("fetch", 2), ("unit", 7), ("h2", 2), ("h2", 3), ("unit", 6), ("unit", 5), ("h1", 7),
    ("norm", 0), ("unit", 8), ("context", 0), ("h1", 6), ("h1", 5), ("h3", 0), ("attend", 0), ("attend", 1),
    ("h2", 7), ("h2", 4), ("attend", 2), ("vector", 0), ("vector", 1), ("h2", 6), ("h1", 8), ("unit", 9), ("h3", 7),
    ("vector", 2), ("h1", 9), ("unit", 10), ("h3", 4), ("unit", 11), ("h2", 5), ("h3", 6), ("h2", 8), ("h4", 7),
    ("vector", 3), ("h1", 11), ("h1", 10), ("h3", 5), ("h4", 0), ("drow", 0), ("h2", 9), ("h4", 6), ("drow", 1),
    ("h3", 8), ("h2", 10), ("h3", 9), ("h2", 11), ("h4", 5), ("h4", 4), ("h3", 10), ("h4", 8), ("drow", 2),
    ("h3", 11), ("h4", 10), ("h4", 9), ("h4", 11),
)


def backward_kernel(
    vecs, rstd, sums_in, d_h, qkvx_h, prob_h, ctx_h, xhat1_h, low1_h, inner_h, slope_h,
    wq_h, wk_h, wv_h, wo_h, wi_h, wu_h,
    drows_h, fin_h, sums_o,
    bufa, bufb, w1, w2, low1, xhat1, ctx, d, dlow, fin, sums, vr,
    both, came, one, two, three, three_o,
    lsem, osem, cs, cr, s1, q1, s2, q2, s3, q3, s4, q4, vs, vq,
):
    core, chip, z, y, x = place()

    def at(zz, yy, xx):
        return zz * 4 + yy * 2 + xx

    other_core = (1 - core, chip)
    other_x = (core, at(z, y, 1 - x))
    other_y = (core, at(z, 1 - y, x))
    other_z = [(core, at((z + k) % 4, y, x)) for k in (1, 2, 3)]
    peers = [other_core, other_x, other_y] + other_z
    barrier = pltpu.get_barrier_semaphore()
    for peer in peers:
        pl.semaphore_signal(barrier, inc=1, device_id=peer, device_id_type=MESH)

    loads = {}
    waited = set()
    sent = []
    got = {}

    def load(name, *pairs):
        copies = []
        for src, dst in pairs:
            copy = pltpu.make_async_copy(src, dst, lsem.at[sum(len(c) for c in loads.values()) + len(copies)])
            copy.start()
            copies.append(copy)
        loads[name] = copies

    def ready(name):
        if name not in waited:
            waited.add(name)
            for copy in loads[name]:
                copy.wait()

    def remote(src, dst, send, recv, peer, late=True):
        copy = pltpu.make_async_remote_copy(
            src_ref=src, dst_ref=dst, send_sem=send, recv_sem=recv, device_id=peer, device_id_type=MESH
        )
        copy.start()
        if late:
            sent.append(copy)
        return copy

    load("d", (d_h, d))
    load("inner", (inner_h, bufa))
    sums[...] = sums_in[...]

    def add_sum(i, value):
        sums[i:i + 1, :] += jnp.sum(value, axis=0, keepdims=True)

    ready("d")
    load("wu", (wu_h, w1))
    load("slope", (slope_h, bufb))
    dlow[...] = d[...].astype(bf)
    pl.semaphore_wait(barrier, len(peers))

    def plus(a, b):
        return (a.astype(f32) + b.astype(f32)).astype(bf)

    def cross(u):
        got["c", u] = remote(both.at[u, 1 - core], came.at[u % 8], cs.at[u], cr.at[u], other_core)

    def h1(u):
        got["c", u].wait_recv()
        mine = both.at[u, core]
        for a in range(4):
            mine[a] = plus(mine[a], came[u % 8, a])
        if u % 2 == 0:
            got["1", u] = remote(mine.at[:, :, 1 - x], one.at[u], s1.at[u], q1.at[u], other_x)
        else:
            got["1", u] = remote(mine.at[:, 1 - y], one.at[u], s1.at[u], q1.at[u], other_y)

    def h2(u):
        got["1", u].wait_recv()
        mine = both.at[u, core]
        even = u % 2 == 0
        for a in range(4):
            for b in range(2):
                if even:
                    mine[a, b, x] = plus(mine[a, b, x], one[u, a, b])
                else:
                    mine[a, y, b] = plus(mine[a, y, b], one[u, a, b])
        if even:
            got["2", u] = remote(mine.at[:, 1 - y, x], two.at[u], s2.at[u], q2.at[u], other_y)
        else:
            got["2", u] = remote(mine.at[:, y, 1 - x], two.at[u], s2.at[u], q2.at[u], other_x)

    def h3(u):
        for v in range(4) if u < 4 else (u,):
            got["2", v].wait_recv()
            for a in range(4):
                both[v, core, a, y, x] = plus(both[v, core, a, y, x], two[v, a])
        for k in range(3):
            to = (z + k + 1) % 4
            if u < 4:
                got["3", u, k] = remote(both.at[to, core, :, y, x], three_o.at[k], s3.at[0, k], q3.at[0, k], other_z[k])
            else:
                got["3", u, k] = remote(
                    both.at[u, core, to, y, x], three.at[u - 4, k], s3.at[u - 3, k], q3.at[u - 3, k], other_z[k]
                )

    cols = pl.ds(pl.multiple_of(core * 384, 128), 384)

    def h4(u):
        for k in range(3):
            got["3", u, k].wait_recv()
        for v in range(4) if u < 4 else (u,):
            if u < 4:
                total = both[z, core, v, y, x].astype(f32)
                for k in range(3):
                    total = total + three_o[k, v].astype(f32)
            else:
                total = both[u, core, z, y, x].astype(f32)
                for k in range(3):
                    total = total + three[u - 4, k].astype(f32)
            fin[v, :, cols] = total
            got["4", v] = remote(fin.at[v, :, cols], fin.at[v, :, cols], s4.at[v], q4.at[v], other_core)

    def outer(u):
        ready("inner")
        for a in range(2):
            res = dot(bufa[:, 768 * u + 384 * a:768 * u + 384 * a + 384], dlow[...], TN).astype(bf)
            for h in range(2):
                for b in range(8):
                    both[u, h, b % 4, a, b // 4] = res[48 * b:48 * b + 48, 384 * h:384 * h + 384]
        cross(u)
        if u == 3:
            load("qkvx", (qkvx_h, bufa))

    def unit(u):
        ready("low1" if u < 8 else "ctx")
        if u < 8:
            left, right = low1, bufb.at[:, 768 * (u - 4):768 * (u - 4) + 768]
        elif u == 8:
            left, right = ctx, dlow
        else:
            left, right = bufa.at[:, 2304:3072], bufb.at[:, 768 * (11 - u):768 * (11 - u) + 768]
        for a in range(2):
            res = dot(left[:, 384 * a:384 * a + 384], right[...], TN).astype(bf)
            for h in range(2):
                for b in range(8):
                    both[u, h, 2 * a + b // 4, (b // 2) % 2, b % 2] = res[48 * b:48 * b + 48, 384 * h:384 * h + 384]
        cross(u)

    def pre(g):
        ready("wu")
        ready("slope")
        lanes = pl.ds(768 * g, 768)
        back = dot(dlow[...], w1[lanes, :], NT) * bufb[:, lanes].astype(f32)
        bufb[:, lanes] = back.astype(bf)
        sums[8 + g:9 + g, :] = jnp.sum(back, axis=0, keepdims=True)

        if g == 3:
            load(
                "w1", (wq_h, w1.at[0:768]), (wk_h, w1.at[768:1536]), (wv_h, w1.at[1536:2304]),
                (wo_h, w1.at[2304:3072]),
            )

    def first_rows(j):
        if j == 0:
            ready("wi")
        rows = pl.ds(448 * j, 448)
        d[rows, :] += dot(bufb[rows, :], w2[...], NT)
        if j == 1:
            load("prob", (prob_h, w2))

    def norm_one(_):
        ready("xhat1")

        @pl.loop(0, 7)
        def _(i):
            rows = pl.ds(pl.multiple_of(i * 128, 128), 128)
            e = d[rows, :]
            xh = xhat1[rows, :].astype(f32)
            eg = e * vecs[4:5, :]
            add_sum(3, e * xh)
            add_sum(4, e)
            value = (
                eg - jnp.mean(eg, axis=1, keepdims=True) - xh * jnp.mean(eg * xh, axis=1, keepdims=True)
            ) * rstd[rows, 0:1]
            add_sum(2, value)
            d[rows, :] = value
            dlow[rows, :] = value.astype(bf)

    def context(_):
        ready("w1")

        @pl.loop(0, 3)
        def _(j):
            lanes = pl.ds(pl.multiple_of(j * 256, 256), 256)
            low1[:, lanes] = dot(dlow[...], w1[pl.ds(pl.multiple_of(2304 + j * 256, 256), 256), :], NT).astype(bf)

        ready("prob")
        ready("qkvx")

    low, high = pair_masks()
    groups = [(384 + 256 * n, 256) for n in range(2)] + [(128 * g, 128) for g in range(3)]

    def spot(g, p):
        if g < 2:
            return pl.ds(256 * g, 256), pl.ds(pl.multiple_of(p * 512, 512), 512)
        i = (g - 2) * 6 + p
        return pl.ds(pl.multiple_of(512 + 128 * (i // 12), 128), 128), pl.ds(pl.multiple_of((i % 12) * 256, 256), 256)

    def stack(value):
        return jnp.concatenate([value * low, value * high], axis=0)

    def fold(value, n):
        return jnp.concatenate([value[:, :n], value[:, n:]], axis=0)

    def attend(part):
        @pl.loop(2 * part, 2 * part + 2)
        def _(p):
            def lanes(m):
                return pl.ds(pl.multiple_of(m * 768 + p * 128, 128), 128)

            slopes = []
            for r0, n in groups:
                rows = pl.ds(r0, n)
                slopes.append(dot(low1[rows, lanes(0)], stack(bufa[rows, lanes(2)]), NT))
            probs = []
            scores = []
            for g, (r0, n) in enumerate(groups):
                prob = w2[spot(g, p)]
                parts = []
                for h in range(2):
                    pf = prob[:, h * n:h * n + n].astype(f32)
                    dp = slopes[g][:, h * n:h * n + n]
                    parts.append((pf * (dp - jnp.sum(pf * dp, axis=1, keepdims=True))).astype(bf))
                probs.append(prob)
                scores.append(jnp.concatenate(parts, axis=1))
            total_q = total_v = 0.0
            for g, (r0, n) in enumerate(groups):
                rows = pl.ds(r0, n)
                dq = dot(scores[g], stack(bufa[rows, lanes(1)])) * HEAD ** (-0.5)
                dk = dot(fold(scores[g], n), stack(bufa[rows, lanes(0)]), TN)
                dv = dot(fold(probs[g], n), stack(low1[rows, lanes(0)]), TN)
                bufb[rows, lanes(0)] = dq.astype(bf)
                bufb[rows, lanes(1)] = dk.astype(bf)
                bufb[rows, lanes(2)] = dv.astype(bf)
                total_q = total_q + jnp.sum(dq, axis=0, keepdims=True)
                total_v = total_v + jnp.sum(dv, axis=0, keepdims=True)
            sums[0:1, lanes(0)] = total_q
            sums[1:2, lanes(0)] = total_v

    def drow(j):
        total = d[:, 256 * j:256 * j + 256]
        for m in range(3):
            total = total + dot(bufb[:, 768 * m:768 * m + 768], w1[768 * m + 256 * j:768 * m + 256 * j + 256, :], NT)
        d[:, 256 * j:256 * j + 256] = total
        if j == 2:
            got["out"] = pltpu.make_async_copy(d, drows_h, osem.at[0])
            got["out"].start()

    def vector(i):
        if i > 0:
            got["v", i - 1].wait()
            sums[...] += vr[i - 1]
        if i < 3:
            got["v", i] = remote(sums, vr.at[i], vs.at[i], vq.at[i], (other_core, other_x, other_y)[i], False)
        else:
            for k in range(3):
                got["w", k] = remote(sums, vr.at[3 + k], vs.at[3 + k], vq.at[3 + k], other_z[k])

    def fetch(i):
        if i == 0:
            load("low1", (low1_h, low1))
        elif i == 1:
            load("wi", (wi_h, w2))
        else:
            load("xhat1", (xhat1_h, xhat1))
            load("ctx", (ctx_h, ctx))

    steps = {
        "fetch": fetch,
        "outer": outer, "pre": pre, "unit": unit, "rows": first_rows, "norm": norm_one, "context": context,
        "attend": attend, "drow": drow, "h1": h1, "h2": h2, "h3": h3, "h4": h4, "vector": vector,
    }
    for name, i in PLAN:
        steps[name](i)
    for k in range(3):
        got["w", k].wait_recv()
    sums_o[...] = sums[...] + vr[3] + vr[4] + vr[5]
    for u in range(12):
        got["4", u].wait_recv()
    final = pltpu.make_async_copy(fin, fin_h, osem.at[1])
    final.start()
    for copy in sent:
        copy.wait_send()
    got["out"].wait()
    final.wait()


def contrast_math(me, quest, table, core, z, y, x, loss):
    rows = 512
    scale = 768 ** (-0.5)
    asked = quest[...].reshape(rows, 512)
    digits = asked[:, 384:512]
    asked = asked[:, 0:384]
    pick = (
        lax.broadcasted_iota(jnp.int32, (16, 128), 0) == lax.broadcasted_iota(jnp.int32, (16, 128), 1)
    ).astype(bf)
    ids = dot(pick, digits, NT)
    positive = ids[0:1] * 16.0 + ids[1:2]
    negative = ids[2:3] * 16.0 + ids[3:4]

    def join(value):
        pairs = value.reshape(value.shape[0] // 16, 2, 8, rows)
        left = pairs[:, 0].reshape(-1, rows)
        right = pairs[:, 1].reshape(-1, rows)
        return (left + pltpu.roll(right, rows - 8, 1)) * scale

    match = join(dot(table[...].reshape(rows, 384), asked, NT))
    number = lax.broadcasted_iota(jnp.int32, (256, 1), 0).astype(f32)
    top = jnp.max(match, axis=0, keepdims=True)
    lse = jnp.log(jnp.sum(jnp.exp(match - top), axis=0, keepdims=True)) + top
    pos_score = jnp.sum(jnp.where(number == positive, match, 0.0), axis=0, keepdims=True)
    neg_score = jnp.sum(jnp.where(number == negative, match, 0.0), axis=0, keepdims=True)
    gap = neg_score - pos_score
    tail = jnp.exp(-jnp.abs(gap))
    softplus = jnp.maximum(gap, 0.0) + jnp.log1p(tail)
    loss[...] = jnp.broadcast_to(lse - pos_score + softplus, loss.shape)
    sig = jnp.where(gap >= 0, 1.0, tail) / (1.0 + tail)
    own = join(dot(table[core, z, y, x], asked, NT))
    own_number = (me * 8 + lax.broadcasted_iota(jnp.int32, (8, 1), 0)).astype(f32)
    used = lax.broadcasted_iota(jnp.int32, (1, rows), 1) % 16 < 4
    coef = jnp.exp(jnp.where(used, own - lse, -1e30))
    coef = coef - jnp.where(own_number == positive, 1.0 + sig, 0.0) + jnp.where(own_number == negative, sig, 0.0)
    coef = jnp.where(used, contrast_weight * coef, 0.0)
    coef = jnp.concatenate([coef, pltpu.roll(coef, 8, 1)], axis=0)
    total = jnp.zeros((16, 384), f32)
    for _ in range(3):
        part = coef.astype(bf)
        total = total + dot(part, asked)
        coef = coef - part.astype(f32)
    return jnp.concatenate([total[0:8], total[8:16]], axis=1) * scale


def backward(vecs, rstd, sums, *arrays):
    any_ = pl.BlockSpec(memory_space=pl.ANY)
    vmem = pl.BlockSpec(memory_space=pltpu.VMEM)
    sds = jax.ShapeDtypeStruct
    dma = pltpu.SemaphoreType.DMA
    mem = pltpu.VMEM
    return pl.pallas_call(
        backward_kernel,
        out_shape=(sds((896, 768), f32), sds((12, 48, 768), f32), sds((16, 768), f32)),
        in_specs=[vmem] * 3 + [any_] * 14,
        out_specs=(any_, any_, vmem),
        scratch_shapes=[
            mem((896, 3072), bf), mem((896, 3072), bf), mem((3072, 768), bf), mem((768, 3072), bf),
            mem((896, 768), bf), mem((896, 768), bf), mem((896, 768), bf),
            mem((896, 768), f32), mem((896, 768), bf), mem((12, 48, 768), f32), mem((16, 768), f32),
            mem((6, 16, 768), f32),
            mem((12, 2, 4, 2, 2, 48, 384), bf), mem((8, 4, 2, 2, 48, 384), bf), mem((12, 4, 2, 48, 384), bf),
            mem((12, 4, 48, 384), bf), mem((8, 3, 48, 384), bf), mem((3, 4, 48, 384), bf),
            dma((20,)), dma((2,)),
            dma((12,)), dma((12,)), dma((12,)), dma((12,)), dma((12,)), dma((12,)),
            dma((9, 3)), dma((9, 3)), dma((12,)), dma((12,)), dma((6,)), dma((6,)),
        ],
        compiler_params=pltpu.CompilerParams(
            collective_id=1, has_side_effects=True, vmem_limit_bytes=64 * 1024 * 1024 - 65536
        ),
        name="backward",
    )(vecs, rstd, sums, *arrays)


def finish_kernel(
    drows_h, fin_h, sums_h, loss_h, outs_h, outl_h,
    o_outs, o_outl, o_short, o_long, o_loss, o_wq, o_bq, o_wk, o_wv, o_bv, o_wo, o_bo, o_g1, o_s1, o_wi, o_bi, o_wu,
    o_bu, o_g2, o_s2,
    drows, fin, sums, loss, outs, outl, isem, osem,
):
    core, chip, z, y, x = place()
    copies = []

    def fetch(src, dst, k):
        copy = pltpu.make_async_copy(src, dst, isem.at[k])
        copy.start()
        return copy

    def move(src, dst):
        copy = pltpu.make_async_copy(src, dst, osem.at[len(copies)])
        copy.start()
        copies.append(copy)

    pairs = ((sums_h, sums), (loss_h, loss), (fin_h, fin), (outs_h, outs), (outl_h, outl))
    came = [fetch(src, dst, k) for k, (src, dst) in enumerate(pairs)]
    parts = [fetch(drows_h.at[pl.ds(128 * i, 128)], drows.at[pl.ds(128 * i, 128)], 5 + i) for i in range(7)]
    came[2].wait()
    for u in range(4):
        move(fin.at[u], o_wu.at[48 * u:48 * u + 48])
        move(fin.at[4 + u], o_wi.at[:, 768 * u:768 * u + 768])
    for u, dst in enumerate((o_wo, o_wv, o_wk, o_wq)):
        move(fin.at[8 + u], dst)
    came[3].wait()
    move(outs, o_outs)
    came[4].wait()
    move(outl, o_outl)
    for i in range(7):
        parts[i].wait()
        if i < 3:
            move(drows.at[pl.ds(128 * i, 128)], o_short.at[pl.ds(128 * i, 128)])
        else:
            move(drows.at[pl.ds(128 * i, 128)], o_long.at[pl.ds(128 * i - 384, 128)])
    came[0].wait()
    came[1].wait()
    small = pltpu.roll(sums[0:8, :], (768 - 48 * chip) % 768, 1)
    for i, dst in enumerate((o_bq, o_bv, o_bo, o_g1, o_s1, o_bu, o_g2, o_s2)):
        dst[...] = small[i, 0:48]
    wide = pltpu.roll(sums[pl.ds(8 + z, 1), :], (768 - 192 * (chip % 4)) % 768, 1)
    o_bi[...] = wide[0, 0:192]
    mine = pltpu.roll(loss[...], (512 - 16 * (core * 16 + chip)) % 512, 1)
    o_loss[...] = mine[0, 0:4]
    for copy in copies:
        copy.wait()


def finish(drows, fin, sums, loss, outs, outl):
    any_ = pl.BlockSpec(memory_space=pl.ANY)
    vmem = pl.BlockSpec(memory_space=pltpu.VMEM)
    sds = jax.ShapeDtypeStruct
    mem = pltpu.VMEM
    square = (sds((48, 768), f32), any_)
    line = (sds((48,), f32), vmem)
    results = [
        (sds((384, 768), bf), any_), (sds((512, 768), bf), any_),
        (sds((384, 768), f32), any_), (sds((512, 768), f32), any_), (sds((4,), f32), vmem),
        square, line, square, square, line, square, line, line, line,
        (sds((48, 3072), f32), any_), (sds((192,), f32), vmem), (sds((192, 768), f32), any_), line, line, line,
    ]
    return pl.pallas_call(
        finish_kernel,
        out_shape=tuple(item[0] for item in results),
        in_specs=[any_] * 6,
        out_specs=tuple(item[1] for item in results),
        scratch_shapes=[
            mem((896, 768), f32), mem((12, 48, 768), f32), mem((16, 768), f32), mem((8, 512), f32),
            mem((384, 768), bf), mem((512, 768), bf),
            pltpu.SemaphoreType.DMA((12,)), pltpu.SemaphoreType.DMA((21,)),
        ],
        compiler_params=pltpu.CompilerParams(vmem_limit_bytes=62 * 1024 * 1024),
        name="finish",
    )(drows, fin, sums, loss, outs, outl)


def fast_body(
    short_tokens, long_tokens, short_lengths, long_lengths, short_cotangent, long_cotangent, queries, positives,
    hard_negatives, w_query, b_query, w_key, w_value, b_value, w_out, b_out, gain_one, shift_one, w_inner, b_inner,
    w_outer, b_outer, gain_two, shift_two,
):
    weights = (w_query, w_key, w_value, w_out, w_inner, w_outer)
    small = (queries, b_query, b_value, b_out, gain_one, shift_one, b_outer, gain_two, shift_two, b_inner)
    (
        out_short, out_long, qkvx, prob, ctx, xhat1, low1, inner, slope, d, rstd, vecs, sums, loss,
    ) = forward(
        short_tokens, long_tokens, short_lengths, long_lengths, short_cotangent, long_cotangent, positives,
        hard_negatives, weights, small,
    )
    drows, fin, sums = backward(
        vecs, rstd, sums, d, qkvx, prob, ctx, xhat1, low1, inner, slope, *weights,
    )
    (
        out_short, out_long, d_short, d_long, losses, g_wq, g_bq, g_wk, g_wv, g_bv, g_wo, g_bo, g_g1, g_s1, g_wi, g_bi, g_wu, g_bu, g_g2,
        g_s2,
    ) = finish(drows, fin, sums, loss, out_short, out_long)
    return (
        out_short.reshape(short_tokens.shape), out_long.reshape(long_tokens.shape),
        d_short.reshape(short_tokens.shape), d_long.reshape(long_tokens.shape),
        losses, g_wq, g_bq, g_wk, g_wv, g_bv, g_wo, g_bo, g_g1, g_s1, g_wi, g_bi, g_wu, g_bu, g_g2, g_s2,
    )


def solution(mesh):
    fast = mesh.shape["grp"] == 2 and mesh.shape["blk"] == 16
    in_specs = (
        P(("grp", "blk"), None, None),
        P(("grp", "blk"), None, None),
        P(("grp", "blk")),
        P(("grp", "blk")),
        P(("grp", "blk"), None, None),
        P(("grp", "blk"), None, None),
        P(("grp", "blk"), None),
        P(("grp", "blk")),
        P(("grp", "blk")),
        P(),
        P(),
        P(),
        P(),
        P(),
        P(),
        P(),
        P(),
        P(),
        P(),
        P(),
        P(),
        P(),
        P(),
        P(),
    )
    out_specs = (
        P(("grp", "blk"), None, None),
        P(("grp", "blk"), None, None),
        P(("grp", "blk"), None, None),
        P(("grp", "blk"), None, None),
        P(("grp", "blk")),
        P("blk", None),
        P("blk"),
        P("blk", None),
        P("blk", None),
        P("blk"),
        P("blk", None),
        P("blk"),
        P("blk"),
        P("blk"),
        P("blk", None),
        P("blk"),
        P("blk", None),
        P("blk"),
        P("blk"),
        P("blk"),
    )
    return jax.shard_map(fast_body if fast else body, mesh=mesh, in_specs=in_specs, out_specs=out_specs, check_vma=False)
```
